32 devices in a mesh: wide: 8 (over z, x), tp: 4 (over y, core).
Axes of the slice: x: 2, y: 2, z: 4, core: 2. Of those that a mesh axis runs over, the one named last changes fastest.
Arguments:
- maps: bfloat16 [64, 4, 32, 32, 256], P(('wide', 'tp')), may hold values from -6 to 6
- roi_image: int32 [8192], P(('wide', 'tp')), may hold values from 0 to 1
- roi_level: int32 [8192], P(('wide', 'tp')), may hold values from 0 to 3
- roi_corner: int32 [8192, 2], P(('wide', 'tp')), may hold values from 0 to 16
- roi_weights: bfloat16 [8192, 2, 7, 16], P(('wide', 'tp')), may hold values from 0.049804688 to 0.5
- crowd: int32 [8192], P(('wide', 'tp')), may hold values from 0 to 1
- labels: int32 [8192], P(('wide', 'tp')), may hold values from 0 to 80
- box_targets: bfloat16 [8192, 4], P(('wide', 'tp')), may hold values from -5 to 5
- w_first: float32 [12544, 1024], P('wide', 'tp'), may hold values from -0.0546875 to 0.0546875
- m_first: float32 [12544, 1024], P('wide', 'tp'), may hold values from -0.0009765625 to 0.0009765625
- v_first: float32 [12544, 1024], P('wide', 'tp'), may hold values from 1.5869141e-10 to 2.4414062e-09
- w_second: float32 [1024, 1024], P('tp', 'wide'), may hold values from -0.1875 to 0.1875
- m_second: float32 [1024, 1024], P('tp', 'wide'), may hold values from -0.0009765625 to 0.0009765625
- v_second: float32 [1024, 1024], P('tp', 'wide'), may hold values from 1.5869141e-10 to 2.4414062e-09
- w_heads: float32 [1024, 401], P(('wide', 'tp')), may hold values from -0.375 to 0.375
- m_heads: float32 [1024, 401], P(('wide', 'tp')), may hold values from -0.0009765625 to 0.0009765625
- v_heads: float32 [1024, 401], P(('wide', 'tp')), may hold values from 1.5869141e-10 to 2.4414062e-09
- biases: float32 [2449], replicated, may hold values from -3 to 3
- bias_m: float32 [2449], replicated, may hold values from -0.0009765625 to 0.0009765625
- bias_v: float32 [2449], replicated, may hold values from 1.5869141e-10 to 2.4414062e-09
Outputs:
- loss_total: float32 [], replicated
- roi_count: float32 [], replicated
- first_new: float32 [12544, 1024], P('wide', 'tp')
- first_moment: float32 [12544, 1024], P('wide', 'tp')
- first_second: float32 [12544, 1024], P('wide', 'tp')
- second_new: float32 [1024, 1024], P('tp', 'wide')
- second_moment: float32 [1024, 1024], P('tp', 'wide')
- second_second: float32 [1024, 1024], P('tp', 'wide')
- heads_new: float32 [1024, 401], P(('wide', 'tp'))
- heads_moment: float32 [1024, 401], P(('wide', 'tp'))
- heads_second: float32 [1024, 401], P(('wide', 'tp'))
- biases_new: float32 [2449], replicated
- biases_moment: float32 [2449], replicated
- biases_second: float32 [2449], replicated
The draws below stay inside these ranges and needn't reach their ends.
All inputs are finite; a program needn't handle non-finite values.
Results may differ from the reference program's by a relative error of at most 0.019.
Values may be sent and summed in bfloat16 or wider, within the bound.
No kernel may reach another device: no remote copies, remote signals or barrier semaphores. Data moves between devices by JAX's collectives and lax.ppermute only.
A program may use at most 192 MiB of HBM per device.

```python
import math
import jax
import jax.numpy as jnp
from jax import lax

C = 256
HID = 1024
CLS = 81
POOL = 7
LEVELS = 4
WIN = 16
MAP = 32
IMG_DEV = 2
ROI_IMG = 128
STEP = 10
FEAT = 12544
HEAD = 401
NBIAS = 2449
IMAGES = 64
ROIS = 8192
N_WIDE = 8
N_TP = 4


def draw_crowd(key, part):
    key = jax.random.fold_in(key, 11)
    rows = jnp.arange(ROIS, dtype=jnp.int32)
    device = rows // (IMG_DEV * ROI_IMG)
    wide_pos = device // N_TP
    tp_pos = device % N_TP
    keep_level = 150 + 350 * wide_pos // max(N_WIDE - 1, 1) + 350 * tp_pos // max(N_TP - 1, 1)
    roll = jax.random.randint(key, (ROIS,), 0, 1000)
    return (roll >= keep_level).astype(jnp.int32)


def draw_labels(key, part):
    key = jax.random.fold_in(key, 23)
    key_fore, key_class = jax.random.split(key)
    fore_roll = jax.random.randint(key_fore, (ROIS,), 0, 4)
    classes = jax.random.randint(key_class, (ROIS,), 1, CLS)
    return jnp.where(fore_roll == 0, classes, 0).astype(jnp.int32)


def place_ends(drawn, stream_key, least, largest):
    extent = drawn.shape
    place = [jax.random.randint(jax.random.fold_in(stream_key, axis), (), 0, extent[axis]) for axis in range(len(extent))]
    drawn = drawn.at[tuple(place)].set(least)
    longest = extent.index(max(extent))
    place[longest] = (place[longest] + 1) % extent[longest]
    return drawn.at[tuple(place)].set(largest)


def levels(stream_key, dims, cuts, smallest, high):
    loudness = 1.0
    for dim, blocks in cuts:
        heights = jax.random.uniform(jax.random.fold_in(jax.random.fold_in(stream_key, 6), dim), (blocks,), jnp.float32, smallest / len(cuts), high / len(cuts))
        loudness = loudness * jnp.repeat(jnp.exp(heights), dims[dim] // blocks).reshape((-1,) + (1,) * (len(dims) - 1 - dim))
    return loudness


def normal_values(key, dims, spread, limit, cuts=(), held_as=jnp.bfloat16):
    array = spread * jax.random.normal(key, dims, jnp.float32)
    if cuts:
        array = array * levels(key, dims, cuts, -0.22, 0.18)
    return jnp.clip(array, -limit, limit).astype(held_as)


def setup_inputs(seed: int = 0) -> dict:
    splits = jax.random.split(jax.random.key(seed), 21)
    maps = normal_values(splits[0], (IMAGES, LEVELS, MAP, MAP, C), 1.0, 6.0, ((0, 32),))
    roi_image = place_ends(jax.random.randint(splits[1], (ROIS,), 0, IMG_DEV), jax.random.fold_in(splits[1], 1), 0, IMG_DEV - 1).astype(jnp.int32)
    roi_level = place_ends(jax.random.randint(splits[2], (ROIS,), 0, LEVELS), jax.random.fold_in(splits[2], 1), 0, LEVELS - 1).astype(jnp.int32)
    roi_corner = place_ends(jax.random.randint(splits[3], (ROIS, 2), 0, MAP - WIN + 1), jax.random.fold_in(splits[3], 1), 0, MAP - WIN).astype(jnp.int32)
    roi_weights = jnp.clip(0.049804688 + 0.4501953 * jax.random.uniform(splits[4], (ROIS, 2, POOL, WIN), jnp.float32) ** levels(splits[4], (ROIS, 2, POOL, WIN), ((0, 32),), -0.2, 0.2), 0.049804688, 0.5).astype(jnp.bfloat16)
    crowd = draw_crowd(jax.random.fold_in(splits[20], 71), 0)
    labels = draw_labels(jax.random.fold_in(splits[20], 71), 0)
    box_targets = normal_values(splits[7], (ROIS, 4), 1.0, 5.0, ((0, 32),))
    w_first = normal_values(splits[8], (FEAT, HID), FEAT ** -0.5, 0.0546875, ((0, 8), (1, 4)), jnp.float32)
    m_first = normal_values(splits[9], (FEAT, HID), (0.006 * ROIS ** -0.5), 0.0009765625, ((0, 8), (1, 4)), jnp.float32)
    v_first = jnp.clip(jnp.exp(math.log(2.4414061883248905e-09) - 2.733368 * jax.random.uniform(splits[10], (FEAT, HID), jnp.float32) ** levels(splits[10], (FEAT, HID), ((0, 8), (1, 4)), -0.2, 0.2)), 1.586914072371215e-10, 2.4414061883248905e-09)
    w_second = normal_values(splits[11], (HID, HID), HID ** -0.5, 0.1875, ((0, 4), (1, 8)), jnp.float32)
    m_second = normal_values(splits[12], (HID, HID), (0.006 * ROIS ** -0.5), 0.0009765625, ((0, 4), (1, 8)), jnp.float32)
    v_second = jnp.clip(jnp.exp(math.log(2.4414061883248905e-09) - 2.733368 * jax.random.uniform(splits[13], (HID, HID), jnp.float32) ** levels(splits[13], (HID, HID), ((0, 4), (1, 8)), -0.2, 0.2)), 1.586914072371215e-10, 2.4414061883248905e-09)
    w_heads = normal_values(splits[14], (HID, HEAD), (HID // 4) ** -0.5, 0.375, ((0, 32),), jnp.float32)
    m_heads = normal_values(splits[15], (HID, HEAD), (0.006 * ROIS ** -0.5), 0.0009765625, ((0, 32),), jnp.float32)
    v_heads = jnp.clip(jnp.exp(math.log(2.4414061883248905e-09) - 2.733368 * jax.random.uniform(splits[16], (HID, HEAD), jnp.float32) ** levels(splits[16], (HID, HEAD), ((0, 32),), -0.2, 0.2)), 1.586914072371215e-10, 2.4414061883248905e-09)
    biases = normal_values(splits[17], (NBIAS,), 0.5, 3.0, (), jnp.float32)
    bias_m = normal_values(splits[18], (NBIAS,), (0.006 * ROIS ** -0.5), 0.0009765625, (), jnp.float32)
    bias_v = jnp.clip(jnp.exp(jax.random.uniform(splits[19], (NBIAS,), jnp.float32, math.log(1.586914072371215e-10), math.log(2.4414061883248905e-09))), 1.586914072371215e-10, 2.4414061883248905e-09)
    return dict(maps=maps, roi_image=roi_image, roi_level=roi_level, roi_corner=roi_corner, roi_weights=roi_weights, crowd=crowd, labels=labels, box_targets=box_targets, w_first=w_first, m_first=m_first, v_first=v_first, w_second=w_second, m_second=m_second, v_second=v_second, w_heads=w_heads, m_heads=m_heads, v_heads=v_heads, biases=biases, bias_m=bias_m, bias_v=bias_v)


@jax.custom_vjp
def low(v):
    return lax.optimization_barrier(v.astype(jnp.bfloat16)).astype(jnp.float32)

@jax.custom_vjp
def low_back(v):
    return v

def low_keep(v):
    return (low(v), None)

def low_pass(kept, grad):
    return (grad,)

def back_keep(v):
    return (v, None)

def back_low(kept, grad):
    return (low(grad),)
low.defvjp(low_keep, low_pass)
low_back.defvjp(back_keep, back_low)
highest = lax.Precision.HIGHEST
rate_first = 0.02
rate_second = 0.06
rate_heads = 0.06
rate_biases = 0.3
decay_one = 0.9
decay_two = 0.999
epsilon = 1e-08
weight_decay = 0.1

def crop_rows(device, maps, roi_image, roi_level, roi_corner, roi_weights):
    rows_dev = IMG_DEV * ROI_IMG
    local = lax.dynamic_slice_in_dim(maps, device * IMG_DEV, IMG_DEV, 0)
    image = lax.dynamic_slice_in_dim(roi_image, device * rows_dev, rows_dev, 0)
    level = lax.dynamic_slice_in_dim(roi_level, device * rows_dev, rows_dev, 0)
    corner = lax.dynamic_slice_in_dim(roi_corner, device * rows_dev, rows_dev, 0)
    weights = lax.dynamic_slice_in_dim(roi_weights, device * rows_dev, rows_dev, 0).astype(jnp.float32)

    def single_window(img, lev, row_at, col_at):
        zero = jnp.zeros((), jnp.int32)
        return lax.dynamic_slice(local, (img, lev, row_at, col_at, zero), (1, 1, WIN, WIN, C))[0, 0]
    windows = jax.vmap(single_window)(image, level, corner[:, 0], corner[:, 1]).astype(jnp.float32)
    partial_rows = jnp.einsum('rau,ruvc->ravc', weights[:, 0], windows, precision=highest)
    pooled = jnp.einsum('rbv,ravc->rabc', weights[:, 1], partial_rows, precision=highest)
    return pooled.reshape(rows_dev, FEAT).astype(jnp.bfloat16)

def head_loss(outputs, labels, crowd, targets):
    logits = outputs[:, :CLS]
    boxes = outputs[:, CLS:].reshape(-1, CLS - 1, 4)
    valid_rows = 1.0 - crowd.astype(jnp.float32)
    classes = jnp.arange(CLS, dtype=jnp.int32)
    onehot = (labels[:, None] == classes[None, :]).astype(jnp.float32)
    row_max = lax.optimization_barrier(jnp.max(logits, axis=1, keepdims=True))
    log_total = jnp.log(lax.optimization_barrier(jnp.sum(jnp.exp(logits - row_max), axis=1))) + row_max[:, 0]
    cross_entropy = log_total - lax.optimization_barrier(jnp.sum(onehot * logits, axis=1))
    foreground = valid_rows * (labels > 0).astype(jnp.float32)
    box_error = lax.optimization_barrier(jnp.sum(onehot[:, 1:, None] * boxes, axis=1)) - targets
    magnitude = jnp.abs(box_error)
    smooth_loss = lax.optimization_barrier(jnp.sum(jnp.where(magnitude < 1.0, 0.5 * box_error * box_error, magnitude - 0.5), axis=1))
    return valid_rows * cross_entropy + foreground * smooth_loss

def block_loss(lowered, crops_block, labels_block, crowd_block, targets_block):
    first_w, second_w, heads_w, bias_all = lowered
    inputs = crops_block.astype(jnp.float32)
    pre_first = low_back(jnp.dot(inputs, first_w, precision=highest) + bias_all[:HID])
    hidden_first = low(jax.nn.gelu(pre_first))
    share = HID // N_TP
    parts = jnp.einsum('rgk,gkh->rgh', hidden_first.reshape(-1, N_TP, share), second_w.reshape(N_TP, share, HID), precision=highest)
    pre_second = low_back(lax.optimization_barrier(jnp.sum(low(parts), axis=1)) + bias_all[HID:2 * HID])
    hidden_second = low(jax.nn.gelu(pre_second))
    outputs = low_back(jnp.dot(hidden_second, heads_w, precision=highest) + bias_all[2 * HID:])
    return jnp.sum(head_loss(outputs, labels_block, crowd_block, targets_block.astype(jnp.float32)))

def adam_update(weight, grad, first, second, rate):
    first_new = decay_one * first + (1.0 - decay_one) * grad
    second_new = decay_two * second + (1.0 - decay_two) * grad * grad
    first_hat = first_new / (1.0 - decay_one ** STEP)
    second_hat = second_new / (1.0 - decay_two ** STEP)
    weight_new = weight - rate * (first_hat / (jnp.sqrt(second_hat) + epsilon) + weight_decay * weight)
    return (weight_new, first_new, second_new)

def reference(maps, roi_image, roi_level, roi_corner, roi_weights, crowd, labels, box_targets, w_first, m_first, v_first, w_second, m_second, v_second, w_heads, m_heads, v_heads, biases, bias_m, bias_v):
    devices = N_WIDE * N_TP
    rows_dev = IMG_DEV * ROI_IMG

    def crop_device(device):
        return crop_rows(device, maps, roi_image, roi_level, roi_corner, roi_weights)
    crops = lax.map(crop_device, jnp.arange(devices, dtype=jnp.int32))
    labels_blocks = labels.reshape(devices, rows_dev)
    crowd_blocks = crowd.reshape(devices, rows_dev)
    target_blocks = box_targets.reshape(devices, rows_dev, 4)
    roi_count = jnp.sum(1.0 - crowd.astype(jnp.float32))

    def total_loss(params):
        first_w, second_w, heads_w, bias_all = params
        lowered = (low(first_w), low(second_w), low(heads_w), bias_all)
        checked = jax.checkpoint(block_loss)

        def add_block(carry, block):
            return (carry + checked(lowered, *block), None)
        total, _ = lax.scan(add_block, jnp.zeros((), jnp.float32), (crops, labels_blocks, crowd_blocks, target_blocks))
        return (total / roi_count, total)
    params = (w_first, w_second, w_heads, biases)
    _, pull_back, loss_total = jax.vjp(total_loss, params, has_aux=True)
    grads = pull_back(jnp.ones((), jnp.float32))[0]
    first_out = adam_update(w_first, grads[0], m_first, v_first, rate_first)
    second_out = adam_update(w_second, grads[1], m_second, v_second, rate_second)
    heads_out = adam_update(w_heads, grads[2], m_heads, v_heads, rate_heads)
    bias_out = adam_update(biases, grads[3], bias_m, bias_v, rate_biases)
    return (loss_total, roi_count, first_out[0], first_out[1], first_out[2], second_out[0], second_out[1], second_out[2], heads_out[0], heads_out[1], heads_out[2], bias_out[0], bias_out[1], bias_out[2])
```

```python
import functools

import jax
import jax.numpy as jnp
import numpy as np
from jax import lax
from jax.experimental import pallas as pl
from jax.experimental.pallas import tpu as pltpu
from jax.sharding import PartitionSpec as P

HID = 1024
CLS = 81
POOL = 7
CELLS = POOL * POOL
WIN = 16
STEP = 10
HEAD = 401
HEADP = 512
CORES = 2
CHUNKS = 4
GROUP = 32
KSTEP = 7
MIB = 2**20

AXES = ("wide", "tp")
rate_first = 0.02
rate_second = 0.06
rate_heads = 0.06
rate_biases = 0.3
decay_one = 0.9
decay_two = 0.999
epsilon = 1e-08
weight_decay = 0.1
GELU_A = 0.7978845608028654
GELU_B = 0.044715

f32 = jnp.float32
bf16 = jnp.bfloat16


def dot(a, b, contract=((1,), (0,))):
    return lax.dot_general(a, b, (contract, ((), ())), preferred_element_type=f32)


def crop_kernel(base_ref, col_ref, maps_ref, wr_ref, wc_ref, rep_ref, tile_ref, out_ref, rows_s, cols_s, left, right):
    step = pl.program_id(0)
    lanes = rows_s.shape[1]
    halves = (left, right)
    rows_s[...] = dot(wr_ref[...], rep_ref[...])
    cols_s[...] = dot(wc_ref[...], tile_ref[...])

    def one(i, carry):
        r = step * GROUP + i
        at = pl.multiple_of(i * 8, 8)
        rows = rows_s[pl.ds(at, 8), :]
        x0 = col_ref[r]
        cols = jnp.concatenate(
            [pltpu.roll(cols_s[pl.ds(at, 8), k : k + 128], x0, 1) for k in range(0, lanes, 128)], axis=1
        )
        both = jnp.concatenate([rows[a : a + 1, :] * cols for a in range(POOL)], axis=0)
        high = both.astype(bf16)
        low = (both - high.astype(f32)).astype(bf16)
        window = maps_ref[pl.ds(base_ref[r], WIN), :, :].reshape(lanes, maps_ref.shape[2])
        got = dot(jnp.concatenate([high, low], axis=0), window)
        got = got[: POOL * 8] + got[POOL * 8 :]
        for h, half in enumerate(halves):
            half[pl.ds(pl.multiple_of(i * POOL * 8, 8), POOL * 8), :] = got[:, h * 128 : (h + 1) * 128]
        return carry

    lax.fori_loop(0, GROUP, one, 0, unroll=4)
    for a in range(POOL):
        for b in range(POOL):
            for h, half in enumerate(halves):
                out_ref[a * POOL + b, :, h * 128 : (h + 1) * 128] = half[
                    pl.ds(a * 8 + b, GROUP, stride=POOL * 8), :
                ].astype(bf16)


def window_crops(maps, base, col, wr, wc):
    count = base.shape[0]
    rows, width, channels = maps.shape
    lanes = WIN * width
    lane = np.arange(lanes)[None]
    unit = np.arange(WIN)[:, None]
    rep = jnp.asarray(lane // width == unit, bf16)
    til = jnp.asarray(lane % width == unit, bf16)
    return pl.pallas_call(
        crop_kernel,
        grid_spec=pltpu.PrefetchScalarGridSpec(
            num_scalar_prefetch=2,
            grid=(count // GROUP,),
            in_specs=[
                pl.BlockSpec(maps.shape, lambda i, *_: (0, 0, 0)),
                pl.BlockSpec((GROUP * 8, WIN), lambda i, *_: (i, 0)),
                pl.BlockSpec((GROUP * 8, WIN), lambda i, *_: (i, 0)),
                pl.BlockSpec(rep.shape, lambda i, *_: (0, 0)),
                pl.BlockSpec(til.shape, lambda i, *_: (0, 0)),
            ],
            out_specs=pl.BlockSpec((CELLS, GROUP, channels), lambda i, *_: (0, i, 0)),
            scratch_shapes=[
                pltpu.VMEM((GROUP * 8, lanes), f32),
                pltpu.VMEM((GROUP * 8, lanes), f32),
                pltpu.VMEM((GROUP * POOL * 8, 128), f32),
                pltpu.VMEM((GROUP * POOL * 8, 128), f32),
            ],
        ),
        out_shape=jax.ShapeDtypeStruct((CELLS, count, channels), bf16),
        compiler_params=pltpu.CompilerParams(vmem_limit_bytes=40 * MIB),
        cost_estimate=pl.CostEstimate(
            flops=2 * count * 112 * lanes * channels * 4, bytes_accessed=12 * MIB, transcendentals=0
        ),
        name="crops",
    )(base, col, maps, wr, wc, rep, til)


def first_kernel(parts, *refs):
    crops, weight, own, send = refs[:parts], refs[parts], refs[parts + 1], refs[parts + 2]
    step = pl.program_id(0)
    blocks, depth, cols = weight.shape
    channels = crops[0].shape[2]

    @pl.when(step == 0)
    def _():
        own[...] = jnp.zeros_like(own)
        send[...] = jnp.zeros_like(send)

    for out, refs_half in ((own, crops[: parts // 2]), (send, crops[parts // 2 :])):
        lhs = jnp.concatenate(
            [jnp.concatenate([ref[j] for ref in refs_half], axis=0) for j in range(depth // channels)], axis=1
        )
        for y in range(blocks):
            out[:, y * cols : (y + 1) * cols] += dot(lhs, weight[y])


def first_layer(crops, weight):
    parts = len(crops)
    blocks, feats, cols = weight.shape
    channels = crops[0].shape[2]
    rows = sum(c.shape[1] for c in crops) // 2
    return pl.pallas_call(
        functools.partial(first_kernel, parts),
        grid=(CELLS // KSTEP,),
        in_specs=[pl.BlockSpec((KSTEP,) + c.shape[1:], lambda i: (i, 0, 0)) for c in crops]
        + [pl.BlockSpec((blocks, KSTEP * channels, cols), lambda i: (0, i, 0))],
        out_specs=[pl.BlockSpec((rows, blocks * cols), lambda i: (0, 0))] * 2,
        out_shape=[jax.ShapeDtypeStruct((rows, blocks * cols), f32)] * 2,
        compiler_params=pltpu.CompilerParams(vmem_limit_bytes=40 * MIB),
        cost_estimate=pl.CostEstimate(
            flops=4 * rows * feats * blocks * cols, bytes_accessed=26 * MIB, transcendentals=0
        ),
        name="first_layer",
    )(*crops, weight)


def first_grad_kernel(parts, cols, *refs):
    crops, own, got, out = refs[:parts], refs[parts], refs[parts + 1], refs[parts + 2]
    channels = crops[0].shape[2]
    grads = jnp.concatenate([own[...], got[...]], axis=0)
    for j in range(crops[0].shape[0]):
        lhs = jnp.concatenate([ref[j] for ref in crops], axis=0)
        res = dot(lhs, grads, ((0,), (0,))).astype(bf16)
        for y in range(out.shape[0]):
            out[y, j * channels : (j + 1) * channels, :] = res[:, y * cols : (y + 1) * cols]


def first_grad(crops, own, got, blocks):
    parts = len(crops)
    rows, units = own.shape
    cols = units // blocks
    channels = crops[0].shape[2]
    return pl.pallas_call(
        functools.partial(first_grad_kernel, parts, cols),
        grid=(CELLS // KSTEP,),
        in_specs=[pl.BlockSpec((KSTEP,) + c.shape[1:], lambda i: (i, 0, 0)) for c in crops]
        + [pl.BlockSpec((rows, units), lambda i: (0, 0))] * 2,
        out_specs=pl.BlockSpec((blocks, KSTEP * channels, cols), lambda i: (0, i, 0)),
        out_shape=jax.ShapeDtypeStruct((blocks, CELLS * channels, cols), bf16),
        compiler_params=pltpu.CompilerParams(vmem_limit_bytes=40 * MIB),
        cost_estimate=pl.CostEstimate(
            flops=4 * rows * CELLS * channels * units, bytes_accessed=26 * MIB, transcendentals=0
        ),
        name="first_grad",
    )(*crops, own, got)


def gelu(x):
    return 0.5 * x * (1.0 + jnp.tanh(GELU_A * (x + GELU_B * x * x * x)))


def gelu_slope(x):
    t = jnp.tanh(GELU_A * (x + GELU_B * x * x * x))
    return 0.5 * (1.0 + t) + 0.5 * x * (1.0 - t * t) * (GELU_A * (1.0 + 3.0 * GELU_B * x * x))


def head_kernel(
    share,
    count_ref,
    pre_own,
    pre_sib,
    w2_own,
    w2_sib,
    wh,
    b1,
    b2,
    bh,
    labels,
    crowd,
    targets,
    g_own,
    g_sib,
    gw2_own,
    gw2_sib,
    gwh,
    gb1,
    gb2,
    gbh,
    loss,
    h1,
    pre2,
    gpre2,
):
    rows, units = pre_own.shape
    sides = ((pre_own, w2_own, g_own, gw2_own, 0), (pre_sib, w2_sib, g_sib, gw2_sib, units))
    pre2[...] = jnp.zeros_like(pre2) + b2[...]
    for pre, w2, _, _, at in sides:
        h1[:, at : at + units] = gelu(pre[...] + b1[:, at : at + units]).astype(bf16)
        for k in range(0, units, share):
            part = dot(h1[:, at + k : at + k + share], w2[k : k + share, :])
            pre2[...] += part.astype(bf16).astype(f32)
    h2 = gelu(pre2[...]).astype(bf16)
    out = dot(h2, wh[...]) + bh[...]
    col = lax.broadcasted_iota(jnp.int32, out.shape, 1)
    label = labels[...]
    valid = 1.0 - crowd[...].astype(f32)
    fore = jnp.where(label > 0, valid, 0.0)
    is_logit = col < CLS
    onehot = jnp.where(col == label, 1.0, 0.0)
    masked = jnp.where(is_logit, out, -jnp.inf)
    top = jnp.max(masked, axis=1, keepdims=True)
    shifted = jnp.exp(masked - top)
    total = jnp.sum(shifted, axis=1, keepdims=True)
    row_loss = valid * (jnp.log(total) + top - jnp.sum(onehot * out, axis=1, keepdims=True))
    scale = 1.0 / count_ref[0, 0]
    grad = (shifted / total - onehot) * (valid * scale)
    base = CLS + 4 * (label - 1)
    for j in range(4):
        mark = (col == base + j) & (col >= CLS)
        err = jnp.sum(jnp.where(mark, out, 0.0), axis=1, keepdims=True) - targets[:, j : j + 1]
        size = jnp.abs(err)
        row_loss += fore * jnp.where(size < 1.0, 0.5 * err * err, size - 0.5)
        grad += jnp.where(mark, jnp.clip(err, -1.0, 1.0) * (fore * scale), 0.0)
    loss[...] = jnp.sum(row_loss, axis=0, keepdims=True)
    g_out = grad.astype(bf16)
    gbh[...] = jnp.sum(g_out.astype(f32), axis=0, keepdims=True)
    gwh[...] = dot(h2, g_out, ((0,), (0,)))
    g_h2 = dot(g_out, wh[...], ((1,), (1,)))
    g2 = (g_h2 * gelu_slope(pre2[...])).astype(bf16)
    gb2[...] = jnp.sum(g2.astype(f32), axis=0, keepdims=True)
    gpre2[...] = g2
    for pre, w2, g1, gw2, at in sides:
        gw2[...] = dot(h1[:, at : at + units], gpre2[...], ((0,), (0,)))
        g_h1 = dot(gpre2[...], w2[...], ((1,), (1,)))
        g = (g_h1 * gelu_slope(pre[...] + b1[:, at : at + units])).astype(bf16)
        gb1[:, at : at + units] = jnp.sum(g.astype(f32), axis=0, keepdims=True)
        g1[...] = g


def heads_step(share, count, pre_own, pre_sib, w2_own, w2_sib, wh, b1, b2, bh, labels, crowd, targets):
    rows, units = pre_own.shape
    vmem = pl.BlockSpec(memory_space=pltpu.VMEM)
    shape = jax.ShapeDtypeStruct
    return pl.pallas_call(
        functools.partial(head_kernel, share),
        in_specs=[pl.BlockSpec(memory_space=pltpu.SMEM)] + [vmem] * 11,
        out_specs=[vmem] * 9,
        out_shape=[
            shape((rows, units), bf16),
            shape((rows, units), bf16),
            shape((units, HID), f32),
            shape((units, HID), f32),
            shape((HID, HEADP), f32),
            shape((1, HID), f32),
            shape((1, HID), f32),
            shape((1, HEADP), f32),
            shape((1, 1), f32),
        ],
        scratch_shapes=[pltpu.VMEM((rows, HID), bf16), pltpu.VMEM((rows, HID), f32), pltpu.VMEM((rows, HID), bf16)],
        compiler_params=pltpu.CompilerParams(vmem_limit_bytes=48 * MIB),
        cost_estimate=pl.CostEstimate(
            flops=6 * rows * HID * (HID + HEADP), bytes_accessed=12 * MIB, transcendentals=8 * rows * HID
        ),
        name="heads",
    )(count, pre_own, pre_sib, w2_own, w2_sib, wh, b1, b2, bh, labels, crowd, targets)


class Grid:
    def __init__(self):
        self.wide = lax.axis_size("wide")
        self.tp = lax.axis_size("tp")
        self.y = self.tp // CORES
        self.x = self.y if self.wide % self.y == 0 else 1
        self.z = self.wide // self.x
        self.size = {"z": self.z, "x": self.x, "y": self.y, "c": CORES}
        wide, tp = lax.axis_index("wide"), lax.axis_index("tp")
        self.at = {"z": wide // self.x, "x": wide % self.x, "y": tp // CORES, "c": tp % CORES}

    def move(self, value, axis, by):
        pairs = []
        for z in range(self.z):
            for x in range(self.x):
                for y in range(self.y):
                    for c in range(CORES):
                        to = {"z": z, "x": x, "y": y, "c": c}
                        to[axis] = (to[axis] + by) % self.size[axis]
                        pairs.append((self.index(z, x, y, c), self.index(to["z"], to["x"], to["y"], to["c"])))
        return lax.ppermute(value, AXES, pairs)

    def index(self, z, x, y, c):
        return ((z * self.x + x) * self.y + y) * CORES + c

    def swap(self, value):
        return self.move(value, "c", 1)


def spread(grid, value, order):
    blocks = {(0, 0, 0): value}
    for axis in order:
        place = "zxy".index(axis)
        for key in list(blocks):
            for by in range(1, grid.size[axis]):
                new = list(key)
                new[place] = by
                blocks[tuple(new)] = grid.move(blocks[key], axis, by)
    return blocks


def spread_stacked(grid, value, order):
    stack = value[None, None, None]
    for axis in order:
        place = "zxy".index(axis)
        stack = jnp.concatenate([stack] + [grid.move(stack, axis, by) for by in range(1, grid.size[axis])], axis=place)
    for place, axis in enumerate("zxy"):
        if grid.size[axis] > 1:
            back = (grid.at[axis] - jnp.arange(grid.size[axis])) % grid.size[axis]
            stack = jnp.take(stack, back, axis=place, mode="clip")
    return stack


def collect_stacked(grid, stack, order):
    left = "zxy"
    total = stack
    for axis in order:
        place = left.index(axis)
        total = total.astype(bf16)

        def block(by):
            at = (grid.at[axis] + by) % grid.size[axis]
            return lax.dynamic_index_in_dim(total, at, place, keepdims=False)

        mine = block(0).astype(f32)
        for by in range(1, grid.size[axis]):
            mine = mine + grid.move(block(by), axis, by).astype(f32)
        total = mine
        left = left.replace(axis, "")
    return total


def collect(grid, get, order):
    keys = [(z, x, y) for z in range(grid.z) for x in range(grid.x) for y in range(grid.y)]
    blocks = {key: get(*key) for key in keys}
    for axis in order:
        place = "zxy".index(axis)
        far_first = sorted((k for k in blocks if k[place]), key=lambda k: (-sum(v > 0 for v in k), k))
        got = {}
        for key in far_first:
            home = list(key)
            home[place] = 0
            got.setdefault(tuple(home), []).append(grid.move(blocks[key], axis, key[place]))
        new = {}
        for home, extra in got.items():
            total = blocks[home].astype(f32)
            for value in extra:
                total = total + value.astype(f32)
            new[home] = total
        blocks = new if got else blocks
        if axis != order[-1]:
            blocks = {k: v.astype(bf16) for k, v in blocks.items()}
    return blocks[(0, 0, 0)].astype(f32)


def all_sum(value):
    count = lax.axis_size("wide") * lax.axis_size("tp")
    if count & (count - 1):
        return lax.psum(value, AXES)
    bit = 1
    while bit < count:
        value = value + lax.ppermute(value, AXES, [(i, i ^ bit) for i in range(count)])
        bit *= 2
    return value


def adam_update(weight, grad, first, second, rate):
    first_new = decay_one * first + (1.0 - decay_one) * grad
    second_new = decay_two * second + (1.0 - decay_two) * grad * grad
    first_hat = first_new / (1.0 - decay_one**STEP)
    second_hat = second_new / (1.0 - decay_two**STEP)
    weight_new = weight - rate * (first_hat / (jnp.sqrt(second_hat) + epsilon) + weight_decay * weight)
    return (weight_new, first_new, second_new)


def shards(
    maps,
    roi_image,
    roi_level,
    roi_corner,
    roi_weights,
    crowd,
    labels,
    box_targets,
    w_first,
    m_first,
    v_first,
    w_second,
    m_second,
    v_second,
    w_heads,
    m_heads,
    v_heads,
    biases,
    bias_m,
    bias_v,
):
    grid = Grid()
    rows = crowd.shape[0]
    feats, cols = w_first.shape
    share, second_cols = w_second.shape
    head_rows = w_heads.shape[0]
    units = HID // CORES
    core = grid.at["c"]
    few = grid.z * grid.x * grid.y <= 16
    orders = ("zxy", "zyx")

    kept = jnp.sum(1 - crowd)
    head_block = jnp.pad(w_heads, ((0, 0), (0, HEADP - HEAD)))
    spot = (lax.broadcasted_iota(jnp.int32, head_block.shape, 0) == 0) * 1
    lane = lax.broadcasted_iota(jnp.int32, head_block.shape, 1)
    head_block = head_block + (
        spot * (jnp.where(lane == HEADP - 1, kept % 128, 0) + jnp.where(lane == HEADP - 2, kept // 128, 0))
    ).astype(f32)
    small = jnp.concatenate(
        [w_second.astype(bf16).reshape(-1, cols), head_block.astype(bf16).reshape(-1, cols)], axis=0
    )
    second_rows = share * second_cols // cols
    small_all = spread_stacked(grid, small, "zxy")

    first_low = w_first.astype(bf16)
    half = feats // 2
    weight = jnp.zeros((grid.y, grid.wide * feats, cols), bf16)
    for p, order in enumerate(orders):
        piece = first_low[p * half : (p + 1) * half]
        if few:
            blocks = spread(grid, piece, order)
            for (bz, bx, by), block in blocks.items():
                z = (grid.at["z"] - bz) % grid.z
                x = (grid.at["x"] - bx) % grid.x
                y = (grid.at["y"] - by) % grid.y
                weight = lax.dynamic_update_slice(weight, block[None], (y, (z * grid.x + x) * feats + p * half, 0))
        else:
            stack = spread_stacked(grid, piece, order).transpose(2, 0, 1, 3, 4)
            weight = weight.reshape(grid.y, grid.z, grid.x, feats, cols)
            weight = weight.at[:, :, :, p * half : (p + 1) * half].set(stack).reshape(grid.y, -1, cols)

    images, levels, height, width, channels = maps.shape
    base = ((roi_image * levels + roi_level) * height + roi_corner[:, 0]).astype(jnp.int32)
    col = roi_corner[:, 1].astype(jnp.int32)
    flat_maps = maps.reshape(images * levels * height, width, channels)
    padded = jnp.pad(roi_weights, ((0, 0), (0, 0), (0, 1), (0, 0)))
    row_w = padded[:, 0].reshape(rows * 8, WIN)
    col_w = padded[:, 1].reshape(rows * 8, WIN)
    step = rows // CHUNKS
    own_crops = []
    for at in range(0, rows, step):
        own_crops.append(
            window_crops(
                flat_maps,
                base[at : at + step],
                col[at : at + step],
                row_w[at * 8 : (at + step) * 8],
                col_w[at * 8 : (at + step) * 8],
            )
        )
    crops = own_crops + [grid.swap(c) for c in own_crops]

    small_all = small_all.reshape(grid.wide, grid.y, *small.shape)
    second_own = (
        small_all[:, :, :second_rows]
        .reshape(grid.wide, grid.y, share, second_cols)
        .transpose(1, 2, 0, 3)
        .reshape(units, HID)
    )
    heads_own = small_all[:, :, second_rows:].reshape(grid.wide, grid.y, head_rows, HEADP)
    second_sib = grid.swap(second_own)
    heads_sib = grid.swap(heads_own)
    head_matrix = jnp.where(
        core == 0, jnp.stack([heads_own, heads_sib], axis=2), jnp.stack([heads_sib, heads_own], axis=2)
    ).reshape(HID, HEADP)
    counts = jnp.sum(head_matrix[:, HEADP - 2 :].astype(f32), axis=0)
    roi_count = counts[0] * 128.0 + counts[1]
    first_bias = biases[:HID].reshape(grid.y, CORES, share)
    bias_rel = jnp.concatenate(
        [
            lax.dynamic_index_in_dim(first_bias, core, 1, keepdims=False).reshape(1, -1),
            lax.dynamic_index_in_dim(first_bias, 1 - core, 1, keepdims=False).reshape(1, -1),
        ],
        axis=1,
    )
    second_bias = biases[HID : 2 * HID].reshape(1, -1)
    head_bias = jnp.pad(biases[2 * HID :], (0, HEADP - HEAD)).reshape(1, -1)

    pre_own, pre_send = first_layer(crops, weight)
    pre_sib = grid.swap(pre_send)
    g_own, g_send, gw2_own, gw2_send, gwh, gb1, gb2, gbh, loss = heads_step(
        share,
        roi_count.reshape(1, 1),
        pre_own,
        pre_sib,
        second_own,
        second_sib,
        head_matrix,
        bias_rel,
        second_bias,
        head_bias,
        labels[:, None],
        crowd[:, None],
        box_targets.astype(f32),
    )
    grad = first_grad(crops, g_own, grid.swap(g_send), grid.y)

    grad = grad.reshape(grid.y, grid.wide, 2, half, cols)
    first_parts = []
    for p, order in enumerate(orders):
        back = order[::-1]
        if few:

            def get(dz, dx, dy):
                z = (grid.at["z"] + dz) % grid.z
                x = (grid.at["x"] + dx) % grid.x
                y = (grid.at["y"] + dy) % grid.y
                return lax.dynamic_slice(grad, (y, z * grid.x + x, p, 0, 0), (1, 1, 1, half, cols))[0, 0, 0]

            first_parts.append(collect(grid, get, back))
        else:
            stack = grad[:, :, p].transpose(1, 0, 2, 3).reshape(grid.z, grid.x, grid.y, half, cols)
            first_parts.append(collect_stacked(grid, stack, back))
    first_total = jnp.concatenate(first_parts, axis=0)

    gw2 = gw2_own + grid.swap(gw2_send)
    gwh = gwh.reshape(grid.wide, grid.y, CORES, head_rows, HEADP)
    gwh = lax.dynamic_index_in_dim(gwh, core, 2, keepdims=False) + grid.swap(
        lax.dynamic_index_in_dim(gwh, 1 - core, 2, keepdims=False)
    )
    gw2 = gw2.astype(bf16).reshape(grid.y, share, grid.wide, second_cols).transpose(2, 0, 1, 3)
    small_grad = jnp.concatenate(
        [
            gw2.reshape(grid.wide, grid.y, second_rows, cols),
            gwh.astype(bf16).reshape(grid.wide, grid.y, -1, cols),
        ],
        axis=2,
    ).reshape(grid.z, grid.x, grid.y, -1, cols)
    small_total = collect_stacked(grid, small_grad, "yxz")
    second_total = small_total[:second_rows].reshape(share, second_cols)
    heads_total = small_total[second_rows:].reshape(head_rows, HEADP)[:, :HEAD]

    gb1 = gb1.reshape(CORES, grid.y, share)
    gb1 = jnp.where(core == 0, gb1, gb1[::-1]).transpose(1, 0, 2).reshape(-1)
    sums = all_sum(jnp.concatenate([gb1, gb2[0], gbh[0, :HEAD], loss[0]]))
    loss_total = sums[-1]
    bias_grad = sums[:-1]

    first_out = adam_update(w_first, first_total, m_first, v_first, rate_first)
    second_out = adam_update(w_second, second_total, m_second, v_second, rate_second)
    heads_out = adam_update(w_heads, heads_total, m_heads, v_heads, rate_heads)
    bias_out = adam_update(biases, bias_grad, bias_m, bias_v, rate_biases)
    return (loss_total, roi_count, *first_out, *second_out, *heads_out, *bias_out)


def solution(mesh):
    rows = P(("wide", "tp"))
    both = P("wide", "tp")
    turned = P("tp", "wide")
    return jax.shard_map(
        shards,
        mesh=mesh,
        in_specs=(rows,) * 8 + (both,) * 3 + (turned,) * 3 + (rows,) * 3 + (P(),) * 3,
        out_specs=(P(), P()) + (both,) * 3 + (turned,) * 3 + (rows,) * 3 + (P(),) * 3,
        check_vma=False,
    )
```

```python
import functools

import jax
import jax.numpy as jnp
import numpy as np
from jax import lax
from jax.experimental import pallas as pl
from jax.experimental.pallas import tpu as pltpu
from jax.sharding import PartitionSpec as P

HID = 1024
CLS = 81
POOL = 7
CELLS = POOL * POOL
WIN = 16
STEP = 10
HEAD = 401
HEADP = 512
CORES = 2
CHUNKS = 4
GROUP = 32
KSTEP = 7
LATE_OUT = 192
LATE_BACK = 160
TERMS = 3
EXTRA = 16
MIB = 2**20
LIGHT = pl.CostEstimate(flops=0, bytes_accessed=1024, transcendentals=0)

AXES = ("wide", "tp")
rate_first = 0.02
rate_second = 0.06
rate_heads = 0.06
rate_biases = 0.3
decay_one = 0.9
decay_two = 0.999
epsilon = 1e-08
weight_decay = 0.1
GELU_A = 0.7978845608028654
GELU_B = 0.044715

f32 = jnp.float32
bf16 = jnp.bfloat16


def dot(a, b, contract=((1,), (0,))):
    return lax.dot_general(a, b, (contract, ((), ())), preferred_element_type=f32)


def crop_kernel(first, base_ref, col_ref, maps_ref, wr_ref, wc_ref, rep_ref, tile_ref, *refs):
    out_ref, rows_s, cols_s, left, right = refs
    step = pl.program_id(0)
    lanes = rows_s.shape[1]
    halves = (left, right)
    rows_s[...] = dot(wr_ref[...], rep_ref[...])
    cols_s[...] = dot(wc_ref[...], tile_ref[...])

    def one(i, carry):
        r = first + step * GROUP + i
        at = pl.multiple_of(i * 8, 8)
        rows = rows_s[pl.ds(at, 8), :]
        x0 = col_ref[r]
        cols = jnp.concatenate(
            [pltpu.roll(cols_s[pl.ds(at, 8), k : k + 128], x0, 1) for k in range(0, lanes, 128)], axis=1
        )
        both = jnp.concatenate([rows[a : a + 1, :] * cols for a in range(POOL)], axis=0)
        high = both.astype(bf16)
        low = (both - high.astype(f32)).astype(bf16)
        window = maps_ref[pl.ds(base_ref[r], WIN), :, :].reshape(lanes, maps_ref.shape[2])
        got = dot(jnp.concatenate([high, low], axis=0), window)
        got = got[: POOL * 8] + got[POOL * 8 :]
        for h, half in enumerate(halves):
            half[pl.ds(pl.multiple_of(i * POOL * 8, 8), POOL * 8), :] = got[:, h * 128 : (h + 1) * 128]
        return carry

    lax.fori_loop(0, GROUP, one, 0, unroll=4)
    for a in range(POOL):
        for b in range(POOL):
            for h, half in enumerate(halves):
                out_ref[a * POOL + b, :, h * 128 : (h + 1) * 128] = half[
                    pl.ds(a * 8 + b, GROUP, stride=POOL * 8), :
                ].astype(bf16)


def window_crops(maps, base, col, wr, wc, first, count):
    rows, width, channels = maps.shape
    lanes = WIN * width
    lane = np.arange(lanes)[None]
    unit = np.arange(WIN)[:, None]
    rep = jnp.asarray(lane // width == unit, bf16)
    til = jnp.asarray(lane % width == unit, bf16)
    return pl.pallas_call(
        functools.partial(crop_kernel, first),
        grid_spec=pltpu.PrefetchScalarGridSpec(
            num_scalar_prefetch=2,
            grid=(count // GROUP,),
            in_specs=[
                pl.BlockSpec(maps.shape, lambda i, *_: (0, 0, 0)),
                pl.BlockSpec((GROUP * 8, WIN), lambda i, *_: (first // GROUP + i, 0)),
                pl.BlockSpec((GROUP * 8, WIN), lambda i, *_: (first // GROUP + i, 0)),
                pl.BlockSpec(rep.shape, lambda i, *_: (0, 0)),
                pl.BlockSpec(til.shape, lambda i, *_: (0, 0)),
            ],
            out_specs=pl.BlockSpec((CELLS, GROUP, channels), lambda i, *_: (0, i, 0)),
            scratch_shapes=[
                pltpu.VMEM((GROUP * 8, lanes), f32),
                pltpu.VMEM((GROUP * 8, lanes), f32),
                pltpu.VMEM((GROUP * POOL * 8, 128), f32),
                pltpu.VMEM((GROUP * POOL * 8, 128), f32),
            ],
        ),
        out_shape=jax.ShapeDtypeStruct((CELLS, count, channels), bf16),
        compiler_params=pltpu.CompilerParams(vmem_limit_bytes=18 * MIB),
        cost_estimate=LIGHT,
        name="crops",
    )(base, col, maps, wr, wc, rep, til)


def first_kernel(parts, *refs):
    crops, weight, own, send = refs[:parts], refs[parts], refs[parts + 1], refs[parts + 2]
    step = pl.program_id(0)
    blocks, depth, cols = weight.shape
    channels = crops[0].shape[2]

    @pl.when(step == 0)
    def _():
        own[...] = jnp.zeros_like(own)
        send[...] = jnp.zeros_like(send)

    for out, refs_half in ((own, crops[: parts // 2]), (send, crops[parts // 2 :])):
        lhs = jnp.concatenate(
            [jnp.concatenate([ref[j] for ref in refs_half], axis=0) for j in range(depth // channels)], axis=1
        )
        for y in range(blocks):
            out[:, y * cols : (y + 1) * cols] += dot(lhs, weight[y])


def first_layer(crops, weight):
    parts = len(crops)
    blocks, feats, cols = weight.shape
    channels = crops[0].shape[2]
    rows = sum(c.shape[1] for c in crops) // 2
    return pl.pallas_call(
        functools.partial(first_kernel, parts),
        grid=(CELLS // KSTEP,),
        in_specs=[pl.BlockSpec((KSTEP,) + c.shape[1:], lambda i: (i, 0, 0)) for c in crops]
        + [pl.BlockSpec((blocks, KSTEP * channels, cols), lambda i: (0, i, 0))],
        out_specs=[pl.BlockSpec((rows, blocks * cols), lambda i: (0, 0))] * 2,
        out_shape=[jax.ShapeDtypeStruct((rows, blocks * cols), f32)] * 2,
        compiler_params=pltpu.CompilerParams(vmem_limit_bytes=60 * MIB),
        cost_estimate=LIGHT,
        name="first_layer",
    )(*crops, weight)


def first_grad_kernel(parts, cols, *refs):
    crops, own, got, out = refs[:parts], refs[parts], refs[parts + 1], refs[parts + 2]
    channels = crops[0].shape[2]
    grads = jnp.concatenate([own[...], got[...]], axis=0)
    for j in range(crops[0].shape[0]):
        lhs = jnp.concatenate([ref[j] for ref in crops], axis=0)
        res = dot(lhs, grads, ((0,), (0,))).astype(bf16)
        for y in range(out.shape[0]):
            out[y, j * channels : (j + 1) * channels, :] = res[:, y * cols : (y + 1) * cols]


def first_grad(crops, own, got, blocks):
    parts = len(crops)
    rows, units = own.shape
    cols = units // blocks
    channels = crops[0].shape[2]
    return pl.pallas_call(
        functools.partial(first_grad_kernel, parts, cols),
        grid=(CELLS // KSTEP,),
        in_specs=[pl.BlockSpec((KSTEP,) + c.shape[1:], lambda i: (i, 0, 0)) for c in crops]
        + [pl.BlockSpec((rows, units), lambda i: (0, 0))] * 2,
        out_specs=pl.BlockSpec((blocks, KSTEP * channels, cols), lambda i: (0, i, 0)),
        out_shape=jax.ShapeDtypeStruct((blocks, CELLS * channels, cols), bf16),
        compiler_params=pltpu.CompilerParams(vmem_limit_bytes=60 * MIB),
        cost_estimate=LIGHT,
        name="first_grad",
    )(*crops, own, got)


def block_span(feats, wide, channels):
    span = max(-(-((w * feats) % channels + feats) // channels) for w in range(wide))
    return span if all(w * feats // channels + span <= CELLS for w in range(wide)) else 0


def cell_copies(crops, start, span, cells, sems):
    found = []
    at = 0
    for n, ref in enumerate(crops):
        rows = ref.shape[1]
        found.append(pltpu.make_async_copy(ref.at[pl.ds(start, span)], cells.at[:, pl.ds(at, rows)], sems.at[n]))
        at += rows
    return found


def block_kernel(span, items, feats, most, parts, fresh, place, *refs):
    count = len(items)
    crops, rest = refs[:parts], refs[parts:]
    own, send, pad, cells, sems = rest[-5:]
    before, inputs = (None, rest[:-5]) if fresh else (rest[:2], rest[2:-5])
    step = pl.program_id(0)
    rows = own.shape[0]
    channels = cells.shape[3]
    cols = inputs[0].shape[1]
    firsts = [sum(len(ys) + 1 for _, ys in items[:i]) for i in range(count)]

    def copies(i):
        slot = i % 2
        start = place[i] * feats
        at = pl.multiple_of(start % channels, 16)
        side, ys = items[i]
        found = cell_copies(crops, start // channels, span, cells.at[slot], sems.at[slot])
        group = inputs[firsts[i] : firsts[i] + len(ys) + 1]
        for k, y in enumerate(ys):
            lanes = pl.ds(y * cols, cols)
            found.append(
                pltpu.make_async_copy(
                    group[k].at[pl.ds(0, most)], pad.at[slot, pl.ds(at, most), lanes], sems.at[slot, parts + 2 * k]
                )
            )
            found.append(
                pltpu.make_async_copy(
                    group[-1].at[y, side, pl.ds(0, feats - most)],
                    pad.at[slot, pl.ds(pl.multiple_of(at + most, 16), feats - most), lanes],
                    sems.at[slot, parts + 1 + 2 * k],
                )
            )
        return found

    def edges(i):
        pad[i % 2, :channels, :] = jnp.zeros((channels, pad.shape[2]), bf16)
        pad[i % 2, pad.shape[1] - channels :, :] = jnp.zeros((channels, pad.shape[2]), bf16)

    @pl.when(step == 0)
    def _():
        edges(0)
        for copy in copies(0):
            copy.start()
        if fresh:
            own[...] = jnp.zeros_like(own)
            send[...] = jnp.zeros_like(send)
        else:
            own[...] = before[0][...]
            send[...] = before[1][...]

    def multiply(lanes):
        slot = lax.rem(step, 2)
        weight = pad[slot, :, lanes]
        for at, out in ((0, own), (rows, send)):
            lhs = jnp.concatenate([cells[slot, j, at : at + rows, :] for j in range(span)], axis=1)
            out[:, lanes] += dot(lhs, weight)

    for i in range(count):

        @pl.when(step == i)
        def _(i=i):
            if i + 1 < count:
                edges(i + 1)
                for copy in copies(i + 1):
                    copy.start()
            for copy in copies(i):
                copy.wait()

    every = tuple(range(pad.shape[2] // cols))
    for ys in sorted({ys for _, ys in items}):
        here = [i for i, item in enumerate(items) if item[1] == ys]
        lanes = slice(0, pad.shape[2]) if ys == every else slice(ys[0] * cols, (ys[0] + 1) * cols)

        @pl.when(functools.reduce(jnp.logical_or, [step == i for i in here]))
        def _(lanes=lanes):
            multiply(lanes)


def whole(shape):
    return pl.BlockSpec(shape, lambda i, place: (0,) * len(shape))


def first_blocks(place, crops, inputs, items, feats, most, span, blocks, before):
    rows = sum(c.shape[1] for c in crops) // 2
    channels = crops[0].shape[2]
    units = blocks * inputs[0].shape[1]
    lead = [] if before is None else list(before)
    away = pl.BlockSpec(memory_space=pl.ANY)
    parts = len(crops)
    return pl.pallas_call(
        functools.partial(block_kernel, span, items, feats, most, parts, before is None),
        grid_spec=pltpu.PrefetchScalarGridSpec(
            num_scalar_prefetch=1,
            grid=(len(items),),
            in_specs=[away] * parts + [whole((rows, units))] * len(lead) + [away] * len(inputs),
            out_specs=[whole((rows, units))] * 2,
            scratch_shapes=[
                pltpu.VMEM((2, span * channels, units), bf16),
                pltpu.VMEM((2, span, 2 * rows, channels), bf16),
                pltpu.SemaphoreType.DMA((2, parts + 2 * blocks)),
            ],
        ),
        out_shape=[jax.ShapeDtypeStruct((rows, units), f32)] * 2,
        input_output_aliases={} if before is None else {1 + parts: 0, 2 + parts: 1},
        compiler_params=pltpu.CompilerParams(vmem_limit_bytes=60 * MIB),
        cost_estimate=LIGHT,
        name="first_blocks",
    )(place, *crops, *lead, *inputs)


def block_grad_kernel(span, feats, blocks, parts, place, *refs):
    crops, (own, got), rest = refs[:parts], refs[parts : parts + 2], refs[parts + 2 :]
    outs, (full, cells, in_sems, out_sems) = rest[:-4], rest[-4:]
    step = pl.program_id(0)
    count = len(outs) // (2 * blocks)
    channels = cells.shape[3]
    cols = full.shape[2] // blocks

    def loads(i):
        return cell_copies(crops, (place[i] * feats) // channels, span, cells.at[i % 2], in_sems.at[i % 2])

    def stores(i):
        at = pl.multiple_of((place[i] * feats) % channels, 16)
        found = []
        for y in range(blocks):
            main, late = outs[(i * blocks + y) * 2], outs[(i * blocks + y) * 2 + 1]
            most = main.shape[0]
            lanes = pl.ds(y * cols, cols)
            found.append(pltpu.make_async_copy(full.at[i % 2, pl.ds(at, most), lanes], main, out_sems.at[i % 2, 2 * y]))
            found.append(
                pltpu.make_async_copy(
                    full.at[i % 2, pl.ds(pl.multiple_of(at + most, 16), feats - most), lanes],
                    late,
                    out_sems.at[i % 2, 2 * y + 1],
                )
            )
        return found

    @pl.when(step == 0)
    def _():
        for copy in loads(0):
            copy.start()

    for i in range(count):

        @pl.when(step == i)
        def _(i=i):
            if i + 1 < count:
                for copy in loads(i + 1):
                    copy.start()
            for copy in loads(i):
                copy.wait()
            if i >= 2:
                for copy in stores(i - 2):
                    copy.wait()

    slot = lax.rem(step, 2)
    grads = jnp.concatenate([own[...], got[...]], axis=0)
    for j in range(span):
        full[slot, j * channels : (j + 1) * channels, :] = dot(cells[slot, j], grads, ((0,), (0,))).astype(bf16)

    for i in range(count):

        @pl.when(step == i)
        def _(i=i):
            for copy in stores(i):
                copy.start()
            if i == count - 1:
                for k in range(max(0, count - 2), count):
                    for copy in stores(k):
                        copy.wait()


def first_grad_blocks(place, crops, own, got, feats, late, blocks, span):
    rows, units = own.shape
    channels = crops[0].shape[2]
    cols = units // blocks
    count = place.shape[0]
    parts = len(crops)
    outs = [(feats - late, cols), (late, cols)] * (count * blocks)
    away = pl.BlockSpec(memory_space=pl.ANY)
    return pl.pallas_call(
        functools.partial(block_grad_kernel, span, feats, blocks, parts),
        grid_spec=pltpu.PrefetchScalarGridSpec(
            num_scalar_prefetch=1,
            grid=(count,),
            in_specs=[away] * parts + [whole((rows, units))] * 2,
            out_specs=[away] * len(outs),
            scratch_shapes=[
                pltpu.VMEM((2, span * channels, units), bf16),
                pltpu.VMEM((2, span, 2 * rows, channels), bf16),
                pltpu.SemaphoreType.DMA((2, parts)),
                pltpu.SemaphoreType.DMA((2, 2 * blocks)),
            ],
        ),
        out_shape=[jax.ShapeDtypeStruct(v, bf16) for v in outs],
        compiler_params=pltpu.CompilerParams(vmem_limit_bytes=60 * MIB),
        cost_estimate=LIGHT,
        name="first_grad",
    )(place, *crops, own, got)


def small_place(half, begin, end):
    lane = 0 if end <= half else 128
    back = half if lane else 0
    return slice(begin - back, end - back), slice(lane, lane + 128)


def prepare_kernel(first, second, heads, crowd, mine, low, wide_heads):
    feats = first.shape[0]
    share = second.shape[0]
    rows = heads.shape[0]
    half = mine.shape[0] - feats
    value = first[...].astype(bf16)
    mine[:feats, :] = value
    low[...] = value[: low.shape[0], :]
    kept = jnp.sum(1 - crowd[...], axis=1, keepdims=True)
    wide_heads[...] = jnp.zeros_like(wide_heads)
    wide_heads[:, :HEAD] = heads[...]
    lane = lax.broadcasted_iota(jnp.int32, (rows, 128), 1)
    row = lax.broadcasted_iota(jnp.int32, (rows, 128), 0)
    marks = jnp.where(lane == 127, kept % 128, jnp.where(lane == 126, kept // 128, 0))
    wide_heads[:, HEADP - 128 :] += jnp.where(row == 0, marks, 0).astype(f32)
    for begin, end in ((0, min(share, half)), (half, share)):
        if begin < end:
            at, lanes = small_place(half, begin, end)
            mine[feats + at.start : feats + at.stop, lanes] = second[begin:end, :].astype(bf16)
    for k in range(HEADP // 128):
        at, lanes = small_place(half, share + k * rows, share + (k + 1) * rows)
        mine[feats + at.start : feats + at.stop, lanes] = wide_heads[:, k * 128 : (k + 1) * 128].astype(bf16)


def prepare(first, second, heads, crowd, most):
    feats, cols = first.shape
    half = (second.shape[0] + heads.shape[0] * HEADP // 128) // 2
    vmem = pl.BlockSpec(memory_space=pltpu.VMEM)
    return pl.pallas_call(
        prepare_kernel,
        in_specs=[vmem] * 4,
        out_specs=[vmem] * 2,
        out_shape=[jax.ShapeDtypeStruct((feats + half, cols), bf16), jax.ShapeDtypeStruct((most, cols), bf16)],
        scratch_shapes=[pltpu.VMEM((heads.shape[0], HEADP), f32)],
        cost_estimate=LIGHT,
        compiler_params=pltpu.CompilerParams(vmem_limit_bytes=16 * MIB),
        name="prepare",
    )(first, second, heads, crowd[None, :])


def unpack_kernel(depth, core_ref, wide_ref, *refs):
    stacks_own, stacks_sib = refs[:depth], refs[depth : 2 * depth]
    w2_own, w2_sib, wh = refs[2 * depth :]
    blocks, xs, half, _ = stacks_sib[0].shape
    share = w2_own.shape[0] // blocks
    count = depth * xs
    rows = wh.shape[0] // (count * blocks * CORES)
    for n in range(count):
        at = wide_ref[n]
        for y in range(blocks):
            turned = lax.rem(wide_ref[count] + blocks - y, blocks)
            for stacks, w2, side in ((stacks_own, w2_own, core_ref[0]), (stacks_sib, w2_sib, 1 - core_ref[0])):
                stack = stacks[n // xs]
                skip = stack.shape[2] - half

                def small(begin, end):
                    rows_at, lanes_at = small_place(half, begin, end)
                    return stack[y, n % xs, skip + rows_at.start : skip + rows_at.stop, lanes_at]

                lanes = pl.ds(pl.multiple_of(at * 128, 128), 128)
                for begin, end in ((0, min(share, half)), (half, share)):
                    if begin < end:
                        w2[y * share + begin : y * share + end, lanes] = small(begin, end)
                to = pl.multiple_of(((at * blocks + turned) * CORES + side) * rows, rows)
                for k in range(HEADP // 128):
                    wh[pl.ds(to, rows), k * 128 : (k + 1) * 128] = small(share + k * rows, share + (k + 1) * rows)


def unpack(core, wide, own, sib, units):
    smem = pl.BlockSpec(memory_space=pltpu.SMEM)
    vmem = pl.BlockSpec(memory_space=pltpu.VMEM)
    return pl.pallas_call(
        functools.partial(unpack_kernel, len(own)),
        in_specs=[smem, smem] + [vmem] * (2 * len(own)),
        out_specs=[vmem] * 3,
        out_shape=[jax.ShapeDtypeStruct((units, HID), bf16)] * 2 + [jax.ShapeDtypeStruct((HID, HEADP), bf16)],
        cost_estimate=LIGHT,
        compiler_params=pltpu.CompilerParams(vmem_limit_bytes=16 * MIB),
        name="unpack",
    )(core, wide, *own, *sib)


def pack_kernel(core_ref, wide_ref, gw2, gw2_got, gwh, gwh_got, sums, out):
    depth, blocks, xs, half, _ = out.shape
    half -= EXTRA
    share = gw2.shape[0] // blocks
    count = depth * xs
    rows = gwh.shape[0] // (count * blocks * CORES)
    for n in range(count):
        at = wide_ref[n]
        lanes = pl.ds(pl.multiple_of(at * 128, 128), 128)
        for y in range(blocks):

            def small(begin, end, value):
                rows_at, lanes_at = small_place(half, begin, end)
                out[n // xs, y, n % xs, rows_at, lanes_at] = value.astype(bf16)

            ahead = lax.rem(wide_ref[count] + y, blocks)
            turned = (blocks - y) % blocks
            for begin, end in ((0, min(share, half)), (half, share)):
                if begin < end:
                    part = slice(turned * share + begin, turned * share + end)
                    small(begin, end, gw2[part, lanes] + gw2_got[part, lanes].astype(f32))
            here = pl.ds(pl.multiple_of(((at * blocks + ahead) * CORES + core_ref[0]) * rows, rows), rows)
            for k in range(HEADP // 128):
                group = slice(k * 128, (k + 1) * 128)
                small(share + k * rows, share + (k + 1) * rows, gwh[here, group] + gwh_got[here, group].astype(f32))
    rest = sums[...]
    rows_left = []
    for _ in range(TERMS):
        term = rest.astype(bf16).astype(f32)
        rest = rest - term
        rows_left += [term[:, k : k + 256] for k in range(0, term.shape[1], 256)]
    rows_left += [jnp.zeros_like(rows_left[0])] * (-len(rows_left) % 8)
    each = len(rows_left) // (blocks * xs)
    for y in range(blocks):
        for x in range(xs):
            n = y * xs + x
            some = rows_left[n * each : (n + 1) * each] + [jnp.zeros_like(rows_left[0])] * (EXTRA - each)
            some = jnp.concatenate(some, axis=0).astype(bf16)
            for dz in range(depth):
                out[dz, y, x, half:, :] = some if dz >= 2 else jnp.zeros_like(some)


def pack(core, wide, gw2, gw2_got, gwh, gwh_got, sums, shape):
    smem = pl.BlockSpec(memory_space=pltpu.SMEM)
    vmem = pl.BlockSpec(memory_space=pltpu.VMEM)
    return pl.pallas_call(
        pack_kernel,
        in_specs=[smem, smem] + [vmem] * 5,
        out_specs=vmem,
        out_shape=jax.ShapeDtypeStruct(shape, bf16),
        cost_estimate=LIGHT,
        compiler_params=pltpu.CompilerParams(vmem_limit_bytes=18 * MIB),
        name="pack",
    )(core, wide, gw2, gw2_got, gwh, gwh_got, sums)


def gelu(x):
    return 0.5 * x * (1.0 + jnp.tanh(GELU_A * (x + GELU_B * x * x * x)))


def gelu_slope(x):
    t = jnp.tanh(GELU_A * (x + GELU_B * x * x * x))
    return 0.5 * (1.0 + t) + 0.5 * x * (1.0 - t * t) * (GELU_A * (1.0 + 3.0 * GELU_B * x * x))


def head_kernel(
    share,
    at_ref,
    pre_own,
    pre_sib,
    w2_own,
    w2_sib,
    wh,
    b1,
    b2,
    bh,
    tags,
    g_own,
    g_sib,
    gw2_own,
    gw2_sib,
    gwh,
    gwh_low,
    sums,
    count,
    h1,
    pre2,
    gpre2,
):
    rows, units = pre_own.shape
    sides = ((pre_own, w2_own, g_own, gw2_own, 0), (pre_sib, w2_sib, g_sib, gw2_sib, units))
    pre2[...] = jnp.zeros_like(pre2) + b2[...]
    for pre, w2, _, _, at in sides:
        h1[:, at : at + units] = gelu(pre[...] + b1[:, at : at + units]).astype(bf16)
        for k in range(0, units, share):
            part = dot(h1[:, at + k : at + k + share], w2[k : k + share, :])
            pre2[...] += part.astype(bf16).astype(f32)
    h2 = gelu(pre2[...]).astype(bf16)
    out = dot(h2, wh[...]) + bh[...]
    col = lax.broadcasted_iota(jnp.int32, out.shape, 1)
    label = tags[:, 4:5].astype(jnp.int32)
    valid = 1.0 - tags[:, 5:6]
    fore = jnp.where(label > 0, valid, 0.0)
    is_logit = col < CLS
    onehot = jnp.where(col == label, 1.0, 0.0)
    masked = jnp.where(is_logit, out, -jnp.inf)
    top = jnp.max(masked, axis=1, keepdims=True)
    shifted = jnp.exp(masked - top)
    total = jnp.sum(shifted, axis=1, keepdims=True)
    row_loss = valid * (jnp.log(total) + top - jnp.sum(onehot * out, axis=1, keepdims=True))
    ends = jnp.sum(wh[:, HEADP - 128 :].astype(f32), axis=0, keepdims=True)
    kept = 128.0 * ends[:, 126:127] + ends[:, 127:128]
    count[...] = kept
    scale = 1.0 / kept
    grad = (shifted / total - onehot) * (valid * scale)
    base = CLS + 4 * (label - 1)
    for j in range(4):
        mark = (col == base + j) & (col >= CLS)
        err = jnp.sum(jnp.where(mark, out, 0.0), axis=1, keepdims=True) - tags[:, j : j + 1]
        size = jnp.abs(err)
        row_loss += fore * jnp.where(size < 1.0, 0.5 * err * err, size - 0.5)
        grad += jnp.where(mark, jnp.clip(err, -1.0, 1.0) * (fore * scale), 0.0)
    g_out = grad.astype(bf16)
    head_sums = jnp.sum(g_out.astype(f32), axis=0, keepdims=True)
    lane = lax.broadcasted_iota(jnp.int32, head_sums.shape, 1)
    loss = jnp.sum(row_loss, axis=0, keepdims=True)
    sums[:, 2 * HID : 2 * HID + HEADP] = jnp.where(lane == HEAD, loss, head_sums)
    gwh[...] = dot(h2, g_out, ((0,), (0,)))
    gwh_low[...] = gwh[...].astype(bf16)
    g_h2 = dot(g_out, wh[...], ((1,), (1,)))
    g2 = (g_h2 * gelu_slope(pre2[...])).astype(bf16)
    sums[:, HID : 2 * HID] = jnp.sum(g2.astype(f32), axis=0, keepdims=True)
    gpre2[...] = g2
    for n, (pre, w2, g1, gw2, at) in enumerate(sides):
        g_h1 = dot(gpre2[...], w2[...], ((1,), (1,)))
        g = (g_h1 * gelu_slope(pre[...] + b1[:, at : at + units])).astype(bf16)
        g1[...] = g
        columns = jnp.sum(g.astype(f32), axis=0, keepdims=True)
        for k in range(units // share):
            to = pl.multiple_of(at_ref[n * (units // share) + k] * share, share)
            sums[:, pl.ds(to, share)] = columns[:, k * share : (k + 1) * share]
        gw2[...] = dot(h1[:, at : at + units], gpre2[...], ((0,), (0,))).astype(gw2.dtype)


def heads_step(share, at, pre_own, pre_sib, w2_own, w2_sib, wh, b1, b2, bh, tags):
    rows, units = pre_own.shape
    vmem = pl.BlockSpec(memory_space=pltpu.VMEM)
    shape = jax.ShapeDtypeStruct
    return pl.pallas_call(
        functools.partial(head_kernel, share),
        in_specs=[pl.BlockSpec(memory_space=pltpu.SMEM)] + [vmem] * 9,
        out_specs=[vmem] * 8,
        out_shape=[
            shape((rows, units), bf16),
            shape((rows, units), bf16),
            shape((units, HID), f32),
            shape((units, HID), bf16),
            shape((HID, HEADP), f32),
            shape((HID, HEADP), bf16),
            shape((1, 2 * HID + HEADP), f32),
            shape((1, 1), f32),
        ],
        scratch_shapes=[pltpu.VMEM((rows, HID), bf16), pltpu.VMEM((rows, HID), f32), pltpu.VMEM((rows, HID), bf16)],
        compiler_params=pltpu.CompilerParams(vmem_limit_bytes=26 * MIB),
        cost_estimate=LIGHT,
        name="heads",
    )(at, pre_own, pre_sib, w2_own, w2_sib, wh, b1, b2, bh, tags)


class Grid:
    def __init__(self):
        self.wide = lax.axis_size("wide")
        self.tp = lax.axis_size("tp")
        self.y = self.tp // CORES
        self.x = self.y if self.wide % self.y == 0 else 1
        self.z = self.wide // self.x
        self.size = {"z": self.z, "x": self.x, "y": self.y, "c": CORES}
        wide, tp = lax.axis_index("wide"), lax.axis_index("tp")
        self.at = {"z": wide // self.x, "x": wide % self.x, "y": tp // CORES, "c": tp % CORES}

    def move(self, value, axis, by):
        pairs = []
        for z in range(self.z):
            for x in range(self.x):
                for y in range(self.y):
                    for c in range(CORES):
                        to = {"z": z, "x": x, "y": y, "c": c}
                        for a in axis:
                            to[a] = (to[a] + by) % self.size[a]
                        pairs.append((self.index(z, x, y, c), self.index(to["z"], to["x"], to["y"], to["c"])))
        return lax.ppermute(value, AXES, pairs)

    def flip(self, value, axis, bit):
        unit = {"c": 1, "y": CORES, "x": CORES * self.y, "z": CORES * self.y * self.x}
        step = bit * sum(unit[a] for a in axis)
        return lax.ppermute(value, AXES, [(i, i ^ step) for i in range(self.wide * self.tp)])

    def index(self, z, x, y, c):
        return ((z * self.x + x) * self.y + y) * CORES + c

    def swap(self, value):
        return self.move(value, "c", 1)


def spread_stacked(grid, value, order):
    stack = value[None, None, None]
    for axis in order:
        place = "zxy".index(axis)
        stack = jnp.concatenate([stack] + [grid.move(stack, axis, by) for by in range(1, grid.size[axis])], axis=place)
    for place, axis in enumerate("zxy"):
        if grid.size[axis] > 1:
            back = (grid.at[axis] - jnp.arange(grid.size[axis])) % grid.size[axis]
            stack = jnp.take(stack, back, axis=place, mode="clip")
    return stack


def collect_stacked(grid, stack, order):
    left = "zxy"
    total = stack
    for axis in order:
        place = left.index(axis)
        total = total.astype(bf16)

        def block(by):
            at = (grid.at[axis] + by) % grid.size[axis]
            return lax.dynamic_index_in_dim(total, at, place, keepdims=False)

        mine = block(0).astype(f32)
        for by in range(1, grid.size[axis]):
            mine = mine + grid.move(block(by), axis, by).astype(f32)
        total = mine
        left = left.replace(axis, "")
    return total


def all_sum(value):
    count = lax.axis_size("wide") * lax.axis_size("tp")
    if count & (count - 1):
        return lax.psum(value, AXES)
    bit = 1
    while bit < count:
        value = value + lax.ppermute(value, AXES, [(i, i ^ bit) for i in range(count)])
        bit *= 2
    return value


def after(value, *others):
    return lax.optimization_barrier((value, *others))[0]


class Links:
    def __init__(self, grid):
        self.grid = grid
        self.last = {}
        self.slots = [{}, {}, {}]

    def next(self):
        self.slots.append({})

    def send(self, value, axis, by=1):
        step = self.slots[-2 if axis == "z" else -3]
        before = [step[a] for a in "zxy" if a in step and a != axis]
        if axis in self.last:
            before.append(self.last[axis])
        sent = self.grid.move(after(value, *before) if before else value, axis, by)
        self.last[axis] = self.slots[-1][axis] = sent
        return sent


def adam_update(weight, grad, first, second, rate):
    first_new = decay_one * first + (1.0 - decay_one) * grad
    second_new = decay_two * second + (1.0 - decay_two) * grad * grad
    first_hat = first_new / (1.0 - decay_one**STEP)
    second_hat = second_new / (1.0 - decay_two**STEP)
    weight_new = weight - rate * (first_hat / (jnp.sqrt(second_hat) + epsilon) + weight_decay * weight)
    return (weight_new, first_new, second_new)


def by_blocks(grid, feats, cols, share, second_cols, head_rows, channels, rows):
    return (
        (grid.z, grid.x, grid.y) == (4, 2, 2)
        and feats % 16 == 0
        and feats > max(LATE_OUT, LATE_BACK)
        and cols == channels == 256
        and second_cols == 128
        and (share, head_rows) == (256, 32)
        and rows % (CHUNKS * GROUP) == 0
        and block_span(feats, grid.wide, channels) > 0
    )


def wide_places(grid, sign):
    places = [
        ((grid.at["z"] + sign * dz) % grid.z) * grid.x + (grid.at["x"] + sign * dx) % grid.x
        for dz in range(grid.z)
        for dx in range(grid.x)
    ]
    return jnp.stack(places + [grid.at["y"]]).astype(jnp.int32)


def low_sum(first, *others):
    total = first.astype(f32)
    for value in others:
        total = total + value.astype(f32)
    return total.astype(bf16)


def terms(value):
    found = []
    for _ in range(TERMS):
        found.append(lax.optimization_barrier(value.astype(bf16)))
        value = value - found[-1].astype(f32)
    return jnp.concatenate(found, axis=0)


def from_terms(rows):
    count = rows.shape[0] // TERMS
    total = rows[:count].astype(f32)
    for k in range(1, TERMS):
        total = total + rows[k * count : (k + 1) * count].astype(f32)
    return total


def blocks_step(grid, make_crops, w_first, w_second, w_heads, biases, crowd, tags):
    feats, cols = w_first.shape
    share, _ = w_second.shape
    head_rows = w_heads.shape[0]
    core = grid.at["c"]
    core_ref = core.reshape(1).astype(jnp.int32)

    links = Links(grid)
    most = feats - LATE_OUT
    mine, first_low = prepare(w_first, w_second, w_heads, crowd, most)
    half = mine.shape[0] - feats
    m = {(0, 0, 0): mine}
    stacks = {}

    m[0, 1, 0] = grid.move(mine, "x", 1)
    m[0, 0, 1] = grid.move(mine, "y", 1)
    m[0, 1, 1] = grid.move(mine, "xy", 1)
    m[1, 0, 0] = grid.move(first_low, "z", 1)
    m[3, 0, 0] = grid.move(first_low, "z", 3)
    own_crops = [make_crops(i) for i in range(CHUNKS)]
    made = own_crops + [m[key] for key in ((0, 1, 0), (0, 0, 1), (0, 1, 1), (1, 0, 0), (3, 0, 0))]
    stacks[0] = jnp.stack([jnp.stack([m[0, x, y][most:] for x in range(grid.x)]) for y in range(grid.y)])
    m[2, 0, 0] = links.send(after(m[1, 0, 0], *made), "z", 1)
    m[1, 1, 0] = links.send(after(m[1, 0, 0], *made), "x")
    m[1, 0, 1] = links.send(after(m[1, 0, 0], *made), "y")
    links.next()
    stacks[1] = links.send(stacks[0], "z", 1)
    m[3, 1, 0] = links.send(m[3, 0, 0], "x")
    m[3, 0, 1] = links.send(m[3, 0, 0], "y")
    links.next()
    stacks[3] = links.send(stacks[0], "z", 3)
    m[2, 1, 0] = links.send(m[2, 0, 0], "x")
    m[2, 0, 1] = links.send(m[2, 0, 0], "y")
    links.next()
    stacks[2] = links.send(stacks[1], "z", 1)
    m[1, 1, 1] = links.send(m[1, 0, 1], "x")
    m[2, 1, 1] = links.send(m[2, 1, 0], "y")
    links.next()
    m[3, 1, 1] = links.send(m[3, 0, 1], "x")
    sib_crops = []
    for chunk in own_crops:
        sib_crops.append(grid.swap(after(chunk, *made)))
    crops = own_crops + sib_crops

    def place(dz, dx, sign):
        z = (grid.at["z"] + sign * dz) % grid.z
        x = (grid.at["x"] + sign * dx) % grid.x
        return z * grid.x + x

    def places(keys, sign):
        return jnp.stack([place(*key, sign) for key in keys]).astype(jnp.int32)

    span = block_span(feats, grid.wide, cols)
    pre = None
    both = (0, 1)
    for work in (
        ((0, 0, both), (0, 1, both), (1, 0, both)),
        ((3, 0, both), (1, 1, both), (2, 0, both), (2, 1, both), (3, 1, (0,))),
        ((3, 1, (1,)),),
    ):
        inputs = [v for dz, dx, ys in work for v in [m[dz, dx, y] for y in ys] + [stacks[dz]]]
        keys = [(dz, dx) for dz, dx, _ in work]
        items = tuple((dx, ys) for _, dx, ys in work)
        pre = first_blocks(places(keys, -1), crops, inputs, items, feats, most, span, grid.y, pre)

    second_own, second_sib, head_matrix = unpack(
        core_ref,
        wide_places(grid, -1),
        [stacks[z] for z in range(4)],
        [grid.swap(stacks[z][:, :, LATE_OUT:]) for z in range(4)],
        HID // CORES,
    )
    bias = biases[:HID].reshape(grid.y, CORES, share)
    bias = jnp.where(grid.at["y"] == 0, bias, bias[::-1])
    bias = jnp.where(core == 0, bias, bias[:, ::-1]).transpose(1, 0, 2).reshape(1, -1)
    unit_at = [2 * ((grid.at["y"] + y) % grid.y) + c for c in (core, 1 - core) for y in range(grid.y)]
    g_own, g_send, gw2, gw2_send, gwh, gwh_low, sums, roi_count = heads_step(
        share,
        jnp.stack(unit_at).astype(jnp.int32),
        pre[0],
        grid.swap(pre[1]),
        second_own,
        second_sib,
        head_matrix,
        bias,
        biases[HID : 2 * HID].reshape(1, -1),
        jnp.pad(biases[2 * HID :], (0, HEADP - HEAD)).reshape(1, -1),
        tags,
    )

    g_got = grid.swap(g_send)
    m = {}
    parts = {}

    def gradients(keys, wait=()):
        where = places(keys, 1)
        outs = first_grad_blocks(after(where, *wait), crops, g_own, g_got, feats, LATE_BACK, grid.y, span)
        for i, (dz, dx) in enumerate(keys):
            for y in range(grid.y):
                m[dz, dx, y], parts[dz, dx, y] = outs[(i * grid.y + y) * 2 : (i * grid.y + y) * 2 + 2]

    gradients([(2, 1), (3, 1)])
    gradients([(2, 0)])
    shape = (grid.z, grid.y, grid.x, half + EXTRA, cols)
    packed = pack(core_ref, wide_places(grid, 1), gw2, grid.swap(gw2_send), gwh, grid.swap(gwh_low), sums, shape)

    def stack_of(dz):
        first = jnp.stack([jnp.stack([parts[dz, dx, y] for dx in range(grid.x)]) for y in range(grid.y)])
        return jnp.concatenate([first, packed[dz]], axis=2)

    links = Links(grid)
    far = stack_of(2)
    gradients([(3, 0), (1, 1)], [far])
    gradients([(1, 0), (0, 1)], [far])
    gradients([(0, 0)], [far])
    x0 = links.send(m[3, 1, 1], "x")
    y0 = links.send(m[2, 1, 1], "y")
    z0 = links.send(far, "z", 1)
    links.next()
    z1 = links.send(stack_of(3), "z", 3)
    x1 = links.send(m[3, 1, 0], "x")
    y1 = links.send(m[2, 0, 1], "y")
    links.next()
    z2 = links.send(low_sum(stack_of(1), z0), "z", 1)
    x2 = links.send(low_sum(m[2, 1, 0], y0), "x")
    y2 = links.send(low_sum(m[3, 0, 1], x0), "y")
    links.next()
    z3 = links.send(low_sum(m[2, 0, 0], x2, y1), "z", 1)
    x3 = links.send(m[1, 1, 1], "x")
    y3 = links.send(m[0, 1, 1], "y")
    links.next()
    z4 = links.send(low_sum(m[3, 0, 0], x1, y2), "z", 3)
    x4 = links.send(m[1, 1, 0], "x")
    y4 = links.send(low_sum(m[1, 0, 1], x3), "y")

    def extra_rows(stack):
        rows = stack[:, :, -EXTRA : 8 - EXTRA].reshape(-1, cols)
        return from_terms(rows[: TERMS * (sums.shape[1] // cols)])

    odd = grid.at["z"] % 2 == 1
    below, above, opposite = extra_rows(z0), extra_rows(z1), extra_rows(z2)
    total = sums.reshape(-1, cols)
    total = (total + jnp.where(odd, below, above)) + (opposite + jnp.where(odd, above, below))
    count = TERMS * total.shape[0]
    late = low_sum(stack_of(0), z1, z2)
    links.next()
    y5 = links.send(jnp.concatenate([late[1].reshape(-1, cols), terms(total)], axis=0), "y")
    x5 = links.send(low_sum(m[0, 1, 0], y3), "x")
    z5 = links.send(low_sum(m[1, 0, 0], x4, y4, z3), "z", 1)
    links.next()
    y6 = links.send(m[0, 0, 1], "y")
    total = total + from_terms(y5[-count:])
    late = low_sum(late[0], y5[:-count].reshape(late[0].shape))
    x6 = links.send(jnp.concatenate([late[1], terms(total)], axis=0), "x")
    total = total + from_terms(x6[-count:])
    total = total + grid.swap(total)
    sums = total.reshape(1, -1)
    main = m[0, 0, 0].astype(f32)
    for value in (x5, y6, z4, z5):
        main = main + value.astype(f32)
    late = late[0].astype(f32) + x6[:-count].astype(f32)

    first_total = jnp.concatenate([main, late[:LATE_BACK]], axis=0)
    late = late[LATE_BACK : LATE_BACK + half]
    total = jnp.concatenate([late[:, :128], late[:, 128:]], axis=0)
    heads_total = jnp.concatenate(
        [total[share + k * head_rows : share + (k + 1) * head_rows] for k in range(HEADP // 128)], axis=1
    )[:, :HEAD]
    return roi_count.reshape(()), sums, first_total, total[:share], heads_total


def stacked_step(grid, make_crops, w_first, w_second, w_heads, biases, crowd, tags):
    feats, cols = w_first.shape
    share, second_cols = w_second.shape
    head_rows = w_heads.shape[0]
    units = HID // CORES
    core = grid.at["c"]
    kept = jnp.sum(1 - crowd)
    head_block = jnp.pad(w_heads, ((0, 0), (0, HEADP - HEAD)))
    spot = (lax.broadcasted_iota(jnp.int32, head_block.shape, 0) == 0) * 1
    lane = lax.broadcasted_iota(jnp.int32, head_block.shape, 1)
    head_block = head_block + (
        spot * (jnp.where(lane == HEADP - 1, kept % 128, 0) + jnp.where(lane == HEADP - 2, kept // 128, 0))
    ).astype(f32)
    small = jnp.concatenate(
        [w_second.astype(bf16).reshape(-1, cols), head_block.astype(bf16).reshape(-1, cols)], axis=0
    )
    second_rows = share * second_cols // cols
    small_all = spread_stacked(grid, small, "zxy").reshape(grid.wide, grid.y, *small.shape)
    weight = spread_stacked(grid, w_first.astype(bf16), "zxy")
    weight = weight.transpose(2, 0, 1, 3, 4).reshape(grid.y, grid.wide * feats, cols)
    crops = [make_crops(i) for i in range(CHUNKS)]
    crops = crops + [grid.swap(c) for c in crops]
    second_own = (
        small_all[:, :, :second_rows]
        .reshape(grid.wide, grid.y, share, second_cols)
        .transpose(1, 2, 0, 3)
        .reshape(units, HID)
    )
    heads_own = small_all[:, :, second_rows:].reshape(grid.wide, grid.y, head_rows, HEADP)
    heads_sib = grid.swap(heads_own)
    head_matrix = jnp.where(
        core == 0, jnp.stack([heads_own, heads_sib], axis=2), jnp.stack([heads_sib, heads_own], axis=2)
    ).reshape(HID, HEADP)
    bias = biases[:HID].reshape(grid.y, CORES, share)
    bias = jnp.where(core == 0, bias, bias[:, ::-1]).transpose(1, 0, 2).reshape(1, -1)
    pre_own, pre_send = first_layer(crops, weight)
    unit_at = [2 * y + c for c in (core, 1 - core) for y in range(grid.y)]
    g_own, g_send, gw2_own, gw2_send, gwh, _, sums, roi_count = heads_step(
        share,
        jnp.stack([jnp.asarray(v) for v in unit_at]).astype(jnp.int32),
        pre_own,
        grid.swap(pre_send),
        second_own,
        grid.swap(second_own),
        head_matrix,
        bias,
        biases[HID : 2 * HID].reshape(1, -1),
        jnp.pad(biases[2 * HID :], (0, HEADP - HEAD)).reshape(1, -1),
        tags,
    )
    grad = first_grad(crops, g_own, grid.swap(g_send), grid.y)
    grad = grad.reshape(grid.y, grid.wide, feats, cols).transpose(1, 0, 2, 3)
    first_total = collect_stacked(grid, grad.reshape(grid.z, grid.x, grid.y, feats, cols), "yxz")
    gw2 = gw2_own + grid.swap(gw2_send).astype(f32)
    gwh = gwh.reshape(grid.wide, grid.y, CORES, head_rows, HEADP)
    gwh = lax.dynamic_index_in_dim(gwh, core, 2, keepdims=False) + grid.swap(
        lax.dynamic_index_in_dim(gwh, 1 - core, 2, keepdims=False)
    )
    gw2 = gw2.astype(bf16).reshape(grid.y, share, grid.wide, second_cols).transpose(2, 0, 1, 3)
    small_grad = jnp.concatenate(
        [
            gw2.reshape(grid.wide, grid.y, second_rows, cols),
            gwh.astype(bf16).reshape(grid.wide, grid.y, -1, cols),
        ],
        axis=2,
    ).reshape(grid.z, grid.x, grid.y, -1, cols)
    small_total = collect_stacked(grid, small_grad, "yxz")
    second_total = small_total[:second_rows].reshape(share, second_cols)
    heads_total = small_total[second_rows:].reshape(head_rows, HEADP)[:, :HEAD]
    sums = all_sum(sums)
    return roi_count.reshape(()), sums, first_total, second_total, heads_total


def shards(
    maps,
    roi_image,
    roi_level,
    roi_corner,
    roi_weights,
    crowd,
    labels,
    box_targets,
    w_first,
    m_first,
    v_first,
    w_second,
    m_second,
    v_second,
    w_heads,
    m_heads,
    v_heads,
    biases,
    bias_m,
    bias_v,
):
    grid = Grid()
    rows = crowd.shape[0]

    images, levels, height, width, channels = maps.shape
    base = ((roi_image * levels + roi_level) * height + roi_corner[:, 0]).astype(jnp.int32)
    col = roi_corner[:, 1].astype(jnp.int32)
    flat_maps = maps.reshape(images * levels * height, width, channels)
    padded = jnp.pad(roi_weights, ((0, 0), (0, 0), (0, 1), (0, 0)))
    row_w = padded[:, 0].reshape(rows * 8, WIN)
    col_w = padded[:, 1].reshape(rows * 8, WIN)
    step = rows // CHUNKS
    tags = jnp.concatenate(
        [box_targets.astype(f32), labels[:, None].astype(f32), crowd[:, None].astype(f32)], axis=1
    )

    def make_crops(i):
        return window_crops(flat_maps, base, col, row_w, col_w, i * step, step)

    shapes = (*w_first.shape, *w_second.shape, w_heads.shape[0], channels, rows)
    run = blocks_step if by_blocks(grid, *shapes) else stacked_step
    roi_count, sums, first_total, second_total, heads_total = run(
        grid, make_crops, w_first, w_second, w_heads, biases, crowd, tags
    )
    loss_total = sums[0, 2 * HID + HEAD]
    bias_grad = sums[0, : 2 * HID + HEAD]

    first_out = adam_update(w_first, first_total, m_first, v_first, rate_first)
    second_out = adam_update(w_second, second_total, m_second, v_second, rate_second)
    heads_out = adam_update(w_heads, heads_total, m_heads, v_heads, rate_heads)
    bias_out = adam_update(biases, bias_grad, bias_m, bias_v, rate_biases)
    return (loss_total, roi_count, *first_out, *second_out, *heads_out, *bias_out)


def solution(mesh):
    rows = P(("wide", "tp"))
    both = P("wide", "tp")
    turned = P("tp", "wide")
    return jax.shard_map(
        shards,
        mesh=mesh,
        in_specs=(rows,) * 8 + (both,) * 3 + (turned,) * 3 + (rows,) * 3 + (P(),) * 3,
        out_specs=(P(), P()) + (both,) * 3 + (turned,) * 3 + (rows,) * 3 + (P(),) * 3,
        check_vma=False,
    )
```

```python
import functools

import jax
import jax.numpy as jnp
import numpy as np
from jax import lax
from jax.experimental import pallas as pl
from jax.experimental.pallas import tpu as pltpu
from jax.sharding import PartitionSpec as P

HID = 1024
CLS = 81
POOL = 7
CELLS = POOL * POOL
WIN = 16
STEP = 10
HEAD = 401
HEADP = 512
CORES = 2
CHUNKS = 4
GROUP = 32
KSTEP = 7
LATE_OUT = 192
LATE_BACK = 208
TERMS = 3
EXTRA = 16
WIDE = 60
MIB = 2**20
LIGHT = pl.CostEstimate(flops=0, bytes_accessed=1024, transcendentals=0)

AXES = ("wide", "tp")
rate_first = 0.02
rate_second = 0.06
rate_heads = 0.06
rate_biases = 0.3
decay_one = 0.9
decay_two = 0.999
epsilon = 1e-08
weight_decay = 0.1
GELU_A = 0.7978845608028654
GELU_B = 0.044715

f32 = jnp.float32
bf16 = jnp.bfloat16


def dot(a, b, contract=((1,), (0,))):
    return lax.dot_general(a, b, (contract, ((), ())), preferred_element_type=f32)


def crop_kernel(first, base_ref, col_ref, maps_ref, wr_ref, wc_ref, rep_ref, tile_ref, *refs):
    out_ref, rows_s, cols_s, left, right = refs
    step = pl.program_id(0)
    lanes = rows_s.shape[1]
    halves = (left, right)
    rows_s[...] = dot(wr_ref[...], rep_ref[...])
    cols_s[...] = dot(wc_ref[...], tile_ref[...])

    def one(i, carry):
        r = first + step * GROUP + i
        at = pl.multiple_of(i * 8, 8)
        rows = rows_s[pl.ds(at, 8), :]
        x0 = col_ref[r]
        cols = jnp.concatenate(
            [pltpu.roll(cols_s[pl.ds(at, 8), k : k + 128], x0, 1) for k in range(0, lanes, 128)], axis=1
        )
        both = jnp.concatenate([rows[a : a + 1, :] * cols for a in range(POOL)], axis=0)
        high = both.astype(bf16)
        low = (both - high.astype(f32)).astype(bf16)
        window = maps_ref[pl.ds(base_ref[r], WIN), :, :].reshape(lanes, maps_ref.shape[2])
        got = dot(jnp.concatenate([high, low], axis=0), window)
        got = got[: POOL * 8] + got[POOL * 8 :]
        for h, half in enumerate(halves):
            half[pl.ds(pl.multiple_of(i * POOL * 8, 8), POOL * 8), :] = got[:, h * 128 : (h + 1) * 128]
        return carry

    lax.fori_loop(0, GROUP, one, 0, unroll=4)
    for a in range(POOL):
        for b in range(POOL):
            for h, half in enumerate(halves):
                out_ref[a * POOL + b, :, h * 128 : (h + 1) * 128] = half[
                    pl.ds(a * 8 + b, GROUP, stride=POOL * 8), :
                ].astype(bf16)


def window_crops(maps, base, col, wr, wc, first, count):
    rows, width, channels = maps.shape
    lanes = WIN * width
    lane = np.arange(lanes)[None]
    unit = np.arange(WIN)[:, None]
    rep = jnp.asarray(lane // width == unit, bf16)
    til = jnp.asarray(lane % width == unit, bf16)
    return pl.pallas_call(
        functools.partial(crop_kernel, first),
        grid_spec=pltpu.PrefetchScalarGridSpec(
            num_scalar_prefetch=2,
            grid=(count // GROUP,),
            in_specs=[
                pl.BlockSpec(maps.shape, lambda i, *_: (0, 0, 0)),
                pl.BlockSpec((GROUP * 8, WIN), lambda i, *_: (first // GROUP + i, 0)),
                pl.BlockSpec((GROUP * 8, WIN), lambda i, *_: (first // GROUP + i, 0)),
                pl.BlockSpec(rep.shape, lambda i, *_: (0, 0)),
                pl.BlockSpec(til.shape, lambda i, *_: (0, 0)),
            ],
            out_specs=pl.BlockSpec((CELLS, GROUP, channels), lambda i, *_: (0, i, 0)),
            scratch_shapes=[
                pltpu.VMEM((GROUP * 8, lanes), f32),
                pltpu.VMEM((GROUP * 8, lanes), f32),
                pltpu.VMEM((GROUP * POOL * 8, 128), f32),
                pltpu.VMEM((GROUP * POOL * 8, 128), f32),
            ],
        ),
        out_shape=jax.ShapeDtypeStruct((CELLS, count, channels), bf16),
        compiler_params=pltpu.CompilerParams(vmem_limit_bytes=18 * MIB),
        cost_estimate=LIGHT,
        name="crops",
    )(base, col, maps, wr, wc, rep, til)


def first_kernel(parts, *refs):
    crops, weight, own, send = refs[:parts], refs[parts], refs[parts + 1], refs[parts + 2]
    step = pl.program_id(0)
    blocks, depth, cols = weight.shape
    channels = crops[0].shape[2]

    @pl.when(step == 0)
    def _():
        own[...] = jnp.zeros_like(own)
        send[...] = jnp.zeros_like(send)

    for out, refs_half in ((own, crops[: parts // 2]), (send, crops[parts // 2 :])):
        lhs = jnp.concatenate(
            [jnp.concatenate([ref[j] for ref in refs_half], axis=0) for j in range(depth // channels)], axis=1
        )
        for y in range(blocks):
            out[:, y * cols : (y + 1) * cols] += dot(lhs, weight[y])


def first_layer(crops, weight):
    parts = len(crops)
    blocks, feats, cols = weight.shape
    channels = crops[0].shape[2]
    rows = sum(c.shape[1] for c in crops) // 2
    return pl.pallas_call(
        functools.partial(first_kernel, parts),
        grid=(CELLS // KSTEP,),
        in_specs=[pl.BlockSpec((KSTEP,) + c.shape[1:], lambda i: (i, 0, 0)) for c in crops]
        + [pl.BlockSpec((blocks, KSTEP * channels, cols), lambda i: (0, i, 0))],
        out_specs=[pl.BlockSpec((rows, blocks * cols), lambda i: (0, 0))] * 2,
        out_shape=[jax.ShapeDtypeStruct((rows, blocks * cols), f32)] * 2,
        compiler_params=pltpu.CompilerParams(vmem_limit_bytes=60 * MIB),
        cost_estimate=LIGHT,
        name="first_layer",
    )(*crops, weight)


def first_grad_kernel(parts, cols, *refs):
    crops, own, got, out = refs[:parts], refs[parts], refs[parts + 1], refs[parts + 2]
    channels = crops[0].shape[2]
    grads = jnp.concatenate([own[...], got[...]], axis=0)
    for j in range(crops[0].shape[0]):
        lhs = jnp.concatenate([ref[j] for ref in crops], axis=0)
        res = dot(lhs, grads, ((0,), (0,))).astype(bf16)
        for y in range(out.shape[0]):
            out[y, j * channels : (j + 1) * channels, :] = res[:, y * cols : (y + 1) * cols]


def first_grad(crops, own, got, blocks):
    parts = len(crops)
    rows, units = own.shape
    cols = units // blocks
    channels = crops[0].shape[2]
    return pl.pallas_call(
        functools.partial(first_grad_kernel, parts, cols),
        grid=(CELLS // KSTEP,),
        in_specs=[pl.BlockSpec((KSTEP,) + c.shape[1:], lambda i: (i, 0, 0)) for c in crops]
        + [pl.BlockSpec((rows, units), lambda i: (0, 0))] * 2,
        out_specs=pl.BlockSpec((blocks, KSTEP * channels, cols), lambda i: (0, i, 0)),
        out_shape=jax.ShapeDtypeStruct((blocks, CELLS * channels, cols), bf16),
        compiler_params=pltpu.CompilerParams(vmem_limit_bytes=60 * MIB),
        cost_estimate=LIGHT,
        name="first_grad",
    )(*crops, own, got)


def block_span(feats, wide, channels):
    span = max(-(-((w * feats) % channels + feats) // channels) for w in range(wide))
    return span if all(w * feats // channels + span <= CELLS for w in range(wide)) else 0


def cell_copies(crops, start, span, cells, sems):
    found = []
    at = 0
    for n, ref in enumerate(crops):
        rows = ref.shape[1]
        found.append(pltpu.make_async_copy(ref.at[pl.ds(start, span)], cells.at[:, pl.ds(at, rows)], sems.at[n]))
        at += rows
    return found


def block_kernel(span, items, feats, most, parts, fresh, place, *refs):
    count = len(items)
    crops, rest = refs[:parts], refs[parts:]
    own, send, pad, cells, sems = rest[-5:]
    before, inputs = (None, rest[:-5]) if fresh else (rest[:2], rest[2:-5])
    step = pl.program_id(0)
    rows = own.shape[0]
    channels = cells.shape[3]
    cols = inputs[0].shape[1]
    firsts = [sum(len(ys) + 1 for _, ys in items[:i]) for i in range(count)]

    def copies(i):
        slot = i % 2
        start = place[i] * feats
        at = pl.multiple_of(start % channels, 16)
        side, ys = items[i]
        found = cell_copies(crops, start // channels, span, cells.at[slot], sems.at[slot])
        group = inputs[firsts[i] : firsts[i] + len(ys) + 1]
        for k, y in enumerate(ys):
            lanes = pl.ds(y * cols, cols)
            found.append(
                pltpu.make_async_copy(
                    group[k].at[pl.ds(0, most)], pad.at[slot, pl.ds(at, most), lanes], sems.at[slot, parts + 2 * k]
                )
            )
            found.append(
                pltpu.make_async_copy(
                    group[-1].at[y, side, pl.ds(0, feats - most)],
                    pad.at[slot, pl.ds(pl.multiple_of(at + most, 16), feats - most), lanes],
                    sems.at[slot, parts + 1 + 2 * k],
                )
            )
        return found

    def edges(i):
        pad[i % 2, :channels, :] = jnp.zeros((channels, pad.shape[2]), bf16)
        pad[i % 2, pad.shape[1] - channels :, :] = jnp.zeros((channels, pad.shape[2]), bf16)

    @pl.when(step == 0)
    def _():
        edges(0)
        for copy in copies(0):
            copy.start()
        if fresh:
            own[...] = jnp.zeros_like(own)
            send[...] = jnp.zeros_like(send)
        else:
            own[...] = before[0][...]
            send[...] = before[1][...]

    def multiply(lanes):
        slot = lax.rem(step, 2)
        got = dot(jnp.concatenate([cells[slot, j] for j in range(span)], axis=1), pad[slot, :, lanes])
        own[:, lanes] += got[:rows]
        send[:, lanes] += got[rows:]

    for i in range(count):

        @pl.when(step == i)
        def _(i=i):
            if i + 1 < count:
                edges(i + 1)
                for copy in copies(i + 1):
                    copy.start()
            for copy in copies(i):
                copy.wait()

    every = tuple(range(pad.shape[2] // cols))
    for ys in sorted({ys for _, ys in items}):
        here = [i for i, item in enumerate(items) if item[1] == ys]
        lanes = slice(0, pad.shape[2]) if ys == every else slice(ys[0] * cols, (ys[0] + 1) * cols)

        @pl.when(functools.reduce(jnp.logical_or, [step == i for i in here]))
        def _(lanes=lanes):
            multiply(lanes)


def whole(shape):
    return pl.BlockSpec(shape, lambda i, place: (0,) * len(shape))


def first_blocks(place, crops, inputs, items, feats, most, span, blocks, before):
    rows = sum(c.shape[1] for c in crops) // 2
    channels = crops[0].shape[2]
    units = blocks * inputs[0].shape[1]
    lead = [] if before is None else list(before)
    away = pl.BlockSpec(memory_space=pl.ANY)
    parts = len(crops)
    return pl.pallas_call(
        functools.partial(block_kernel, span, items, feats, most, parts, before is None),
        grid_spec=pltpu.PrefetchScalarGridSpec(
            num_scalar_prefetch=1,
            grid=(len(items),),
            in_specs=[away] * parts + [whole((rows, units))] * len(lead) + [away] * len(inputs),
            out_specs=[whole((rows, units))] * 2,
            scratch_shapes=[
                pltpu.VMEM((2, span * channels, units), bf16),
                pltpu.VMEM((2, span, 2 * rows, channels), bf16),
                pltpu.SemaphoreType.DMA((2, parts + 2 * blocks)),
            ],
        ),
        out_shape=[jax.ShapeDtypeStruct((rows, units), f32)] * 2,
        input_output_aliases={} if before is None else {1 + parts: 0, 2 + parts: 1},
        compiler_params=pltpu.CompilerParams(vmem_limit_bytes=WIDE * MIB),
        cost_estimate=LIGHT,
        name="first_blocks",
    )(place, *crops, *lead, *inputs)


def block_grad_kernel(span, feats, blocks, parts, place, *refs):
    crops, (own, got), rest = refs[:parts], refs[parts : parts + 2], refs[parts + 2 :]
    outs, (full, cells, in_sems, out_sems) = rest[:-4], rest[-4:]
    step = pl.program_id(0)
    count = len(outs) // (2 * blocks)
    channels = cells.shape[3]
    cols = full.shape[2] // blocks

    def loads(i):
        return cell_copies(crops, (place[i] * feats) // channels, span, cells.at[i % 2], in_sems.at[i % 2])

    def stores(i):
        at = pl.multiple_of((place[i] * feats) % channels, 16)
        found = []
        for y in range(blocks):
            main, late = outs[(i * blocks + y) * 2], outs[(i * blocks + y) * 2 + 1]
            most = main.shape[0]
            lanes = pl.ds(y * cols, cols)
            found.append(pltpu.make_async_copy(full.at[i % 2, pl.ds(at, most), lanes], main, out_sems.at[i % 2, 2 * y]))
            found.append(
                pltpu.make_async_copy(
                    full.at[i % 2, pl.ds(pl.multiple_of(at + most, 16), feats - most), lanes],
                    late,
                    out_sems.at[i % 2, 2 * y + 1],
                )
            )
        return found

    @pl.when(step == 0)
    def _():
        for copy in loads(0):
            copy.start()

    for i in range(count):

        @pl.when(step == i)
        def _(i=i):
            if i + 1 < count:
                for copy in loads(i + 1):
                    copy.start()
            for copy in loads(i):
                copy.wait()
            if i >= 2:
                for copy in stores(i - 2):
                    copy.wait()

    slot = lax.rem(step, 2)
    grads = jnp.concatenate([own[...], got[...]], axis=0)
    for j in range(span):
        full[slot, j * channels : (j + 1) * channels, :] = dot(cells[slot, j], grads, ((0,), (0,))).astype(bf16)

    for i in range(count):

        @pl.when(step == i)
        def _(i=i):
            for copy in stores(i):
                copy.start()
            if i == count - 1:
                for k in range(max(0, count - 2), count):
                    for copy in stores(k):
                        copy.wait()


def first_grad_blocks(place, crops, own, got, feats, late, blocks, span):
    rows, units = own.shape
    channels = crops[0].shape[2]
    cols = units // blocks
    count = place.shape[0]
    parts = len(crops)
    outs = [(feats - late, cols), (late, cols)] * (count * blocks)
    away = pl.BlockSpec(memory_space=pl.ANY)
    return pl.pallas_call(
        functools.partial(block_grad_kernel, span, feats, blocks, parts),
        grid_spec=pltpu.PrefetchScalarGridSpec(
            num_scalar_prefetch=1,
            grid=(count,),
            in_specs=[away] * parts + [whole((rows, units))] * 2,
            out_specs=[away] * len(outs),
            scratch_shapes=[
                pltpu.VMEM((2, span * channels, units), bf16),
                pltpu.VMEM((2, span, 2 * rows, channels), bf16),
                pltpu.SemaphoreType.DMA((2, parts)),
                pltpu.SemaphoreType.DMA((2, 2 * blocks)),
            ],
        ),
        out_shape=[jax.ShapeDtypeStruct(v, bf16) for v in outs],
        compiler_params=pltpu.CompilerParams(vmem_limit_bytes=WIDE * MIB),
        cost_estimate=LIGHT,
        name="first_grad",
    )(place, *crops, own, got)


def small_place(half, begin, end):
    lane = 0 if end <= half else 128
    back = half if lane else 0
    return slice(begin - back, end - back), slice(lane, lane + 128)


def prepare_kernel(first, second, heads, crowd, mine, low, wide_heads):
    feats = first.shape[0]
    share = second.shape[0]
    rows = heads.shape[0]
    half = mine.shape[0] - feats
    value = first[...].astype(bf16)
    mine[:feats, :] = value
    low[...] = value[: low.shape[0], :]
    kept = jnp.sum(1 - crowd[...], axis=1, keepdims=True)
    wide_heads[...] = jnp.zeros_like(wide_heads)
    wide_heads[:, :HEAD] = heads[...]
    lane = lax.broadcasted_iota(jnp.int32, (rows, 128), 1)
    row = lax.broadcasted_iota(jnp.int32, (rows, 128), 0)
    marks = jnp.where(lane == 127, kept % 128, jnp.where(lane == 126, kept // 128, 0))
    wide_heads[:, HEADP - 128 :] += jnp.where(row == 0, marks, 0).astype(f32)
    for begin, end in ((0, min(share, half)), (half, share)):
        if begin < end:
            at, lanes = small_place(half, begin, end)
            mine[feats + at.start : feats + at.stop, lanes] = second[begin:end, :].astype(bf16)
    for k in range(HEADP // 128):
        at, lanes = small_place(half, share + k * rows, share + (k + 1) * rows)
        mine[feats + at.start : feats + at.stop, lanes] = wide_heads[:, k * 128 : (k + 1) * 128].astype(bf16)


def prepare(first, second, heads, crowd, most):
    feats, cols = first.shape
    half = (second.shape[0] + heads.shape[0] * HEADP // 128) // 2
    vmem = pl.BlockSpec(memory_space=pltpu.VMEM)
    return pl.pallas_call(
        prepare_kernel,
        in_specs=[vmem] * 4,
        out_specs=[vmem] * 2,
        out_shape=[jax.ShapeDtypeStruct((feats + half, cols), bf16), jax.ShapeDtypeStruct((most, cols), bf16)],
        scratch_shapes=[pltpu.VMEM((heads.shape[0], HEADP), f32)],
        cost_estimate=LIGHT,
        compiler_params=pltpu.CompilerParams(vmem_limit_bytes=16 * MIB),
        name="prepare",
    )(first, second, heads, crowd[None, :])


def unpack_kernel(depth, core_ref, wide_ref, *refs):
    stacks = refs[: 2 * depth]
    w2_own, w2_sib, wh, small, sems = refs[2 * depth :]
    _, blocks, xs, half, _ = small.shape
    share = w2_own.shape[0] // blocks
    count = depth * xs
    rows = wh.shape[0] // (count * blocks * CORES)
    copies = [
        pltpu.make_async_copy(ref.at[:, :, pl.ds(ref.shape[2] - half, half)], small.at[n], sems.at[n])
        for n, ref in enumerate(stacks)
    ]
    for copy in copies:
        copy.start()
    for copy in copies:
        copy.wait()
    for n in range(count):
        at = wide_ref[n]
        lanes = pl.ds(pl.multiple_of(at * 128, 128), 128)
        for y in range(blocks):
            turned = lax.rem(wide_ref[count] + blocks - y, blocks)
            for first, w2, side in ((0, w2_own, core_ref[0]), (depth, w2_sib, 1 - core_ref[0])):

                def piece(begin, end):
                    rows_at, lanes_at = small_place(half, begin, end)
                    return small[first + n // xs, y, n % xs, rows_at, lanes_at]

                for begin, end in ((0, min(share, half)), (half, share)):
                    if begin < end:
                        w2[y * share + begin : y * share + end, lanes] = piece(begin, end)
                to = pl.multiple_of(((at * blocks + turned) * CORES + side) * rows, rows)
                for k in range(HEADP // 128):
                    wh[pl.ds(to, rows), k * 128 : (k + 1) * 128] = piece(share + k * rows, share + (k + 1) * rows)


def unpack(core, wide, own, sib, half, units):
    smem = pl.BlockSpec(memory_space=pltpu.SMEM)
    vmem = pl.BlockSpec(memory_space=pltpu.VMEM)
    count = 2 * len(own)
    blocks, xs, _, cols = own[0].shape
    return pl.pallas_call(
        functools.partial(unpack_kernel, len(own)),
        in_specs=[smem, smem] + [pl.BlockSpec(memory_space=pl.ANY)] * count,
        out_specs=[vmem] * 3,
        out_shape=[jax.ShapeDtypeStruct((units, HID), bf16)] * 2 + [jax.ShapeDtypeStruct((HID, HEADP), bf16)],
        scratch_shapes=[pltpu.VMEM((count, blocks, xs, half, cols), bf16), pltpu.SemaphoreType.DMA((count,))],
        cost_estimate=LIGHT,
        compiler_params=pltpu.CompilerParams(vmem_limit_bytes=WIDE * MIB),
        name="unpack",
    )(core, wide, *own, *sib)


def pack_kernel(wide_ref, gw2, gw2_got, gwh, gwh_got, sums, out):
    depth, blocks, xs, half, _ = out.shape
    half -= EXTRA
    share = gw2.shape[0] // blocks
    count = depth * xs
    rows = gwh.shape[0] // (count * blocks)
    for n in range(count):
        at = wide_ref[n]
        lanes = pl.ds(pl.multiple_of(at * 128, 128), 128)
        for y in range(blocks):

            def small(begin, end, value):
                rows_at, lanes_at = small_place(half, begin, end)
                out[n // xs, y, n % xs, rows_at, lanes_at] = value.astype(bf16)

            ahead = lax.rem(wide_ref[count] + y, blocks)
            turned = (blocks - y) % blocks
            for begin, end in ((0, min(share, half)), (half, share)):
                if begin < end:
                    part = slice(turned * share + begin, turned * share + end)
                    small(begin, end, gw2[part, lanes].astype(f32) + gw2_got[part, lanes].astype(f32))
            here = pl.ds(pl.multiple_of((at * blocks + ahead) * rows, rows), rows)
            for k in range(HEADP // 128):
                group = slice(k * 128, (k + 1) * 128)
                both = gwh[here, group].astype(f32) + gwh_got[here, group].astype(f32)
                small(share + k * rows, share + (k + 1) * rows, both)
    rest = sums[...]
    rows_left = []
    for _ in range(TERMS):
        term = rest.astype(bf16).astype(f32)
        rest = rest - term
        rows_left += [term[:, k : k + 256] for k in range(0, term.shape[1], 256)]
    rows_left += [jnp.zeros_like(rows_left[0])] * (-len(rows_left) % 8)
    each = len(rows_left) // (blocks * xs)
    for y in range(blocks):
        for x in range(xs):
            n = y * xs + x
            some = rows_left[n * each : (n + 1) * each] + [jnp.zeros_like(rows_left[0])] * (EXTRA - each)
            some = jnp.concatenate(some, axis=0).astype(bf16)
            for dz in range(depth):
                out[dz, y, x, half:, :] = some if dz >= 2 else jnp.zeros_like(some)


def pack(wide, gw2, gw2_got, gwh, gwh_got, sums, shape):
    smem = pl.BlockSpec(memory_space=pltpu.SMEM)
    vmem = pl.BlockSpec(memory_space=pltpu.VMEM)
    return pl.pallas_call(
        pack_kernel,
        in_specs=[smem] + [vmem] * 5,
        out_specs=vmem,
        out_shape=jax.ShapeDtypeStruct(shape, bf16),
        cost_estimate=LIGHT,
        compiler_params=pltpu.CompilerParams(vmem_limit_bytes=WIDE * MIB),
        name="pack",
    )(wide, gw2, gw2_got, gwh, gwh_got, sums)


def gelu(x):
    return 0.5 * x * (1.0 + jnp.tanh(GELU_A * (x + GELU_B * x * x * x)))


def gelu_slope(x):
    t = jnp.tanh(GELU_A * (x + GELU_B * x * x * x))
    return 0.5 * (1.0 + t) + 0.5 * x * (1.0 - t * t) * (GELU_A * (1.0 + 3.0 * GELU_B * x * x))


def head_kernel(
    share,
    wide,
    at_ref,
    pre_own,
    pre_sib,
    w2_own,
    w2_sib,
    wh,
    b1,
    b2,
    bh,
    tags,
    g_own,
    g_sib,
    gw2_own,
    gw2_sib,
    gwh_own,
    gwh_sib,
    sums,
    count,
    h1,
    pre2,
    gpre2,
    gwh,
):
    rows, units = pre_own.shape
    sides = ((pre_own, w2_own, g_own, gw2_own, 0), (pre_sib, w2_sib, g_sib, gw2_sib, units))
    pre2[...] = jnp.zeros_like(pre2) + b2[...]
    for pre, w2, _, _, at in sides:
        h1[:, at : at + units] = gelu(pre[...] + b1[:, at : at + units]).astype(bf16)
        for k in range(0, units, share):
            part = dot(h1[:, at + k : at + k + share], w2[k : k + share, :])
            pre2[...] += part.astype(bf16).astype(f32)
    h2 = gelu(pre2[...]).astype(bf16)
    out = dot(h2, wh[...]) + bh[...]
    col = lax.broadcasted_iota(jnp.int32, out.shape, 1)
    label = tags[:, 4:5].astype(jnp.int32)
    valid = 1.0 - tags[:, 5:6]
    fore = jnp.where(label > 0, valid, 0.0)
    is_logit = col < CLS
    onehot = jnp.where(col == label, 1.0, 0.0)
    masked = jnp.where(is_logit, out, -jnp.inf)
    top = jnp.max(masked, axis=1, keepdims=True)
    shifted = jnp.exp(masked - top)
    total = jnp.sum(shifted, axis=1, keepdims=True)
    row_loss = valid * (jnp.log(total) + top - jnp.sum(onehot * out, axis=1, keepdims=True))
    ends = jnp.sum(wh[:, HEADP - 128 :].astype(f32), axis=0, keepdims=True)
    kept = 128.0 * ends[:, 126:127] + ends[:, 127:128]
    count[...] = kept
    scale = 1.0 / kept
    grad = (shifted / total - onehot) * (valid * scale)
    base = CLS + 4 * (label - 1)
    for j in range(4):
        mark = (col == base + j) & (col >= CLS)
        err = jnp.sum(jnp.where(mark, out, 0.0), axis=1, keepdims=True) - tags[:, j : j + 1]
        size = jnp.abs(err)
        row_loss += fore * jnp.where(size < 1.0, 0.5 * err * err, size - 0.5)
        grad += jnp.where(mark, jnp.clip(err, -1.0, 1.0) * (fore * scale), 0.0)
    g_out = grad.astype(bf16)
    head_sums = jnp.sum(g_out.astype(f32), axis=0, keepdims=True)
    lane = lax.broadcasted_iota(jnp.int32, head_sums.shape, 1)
    loss = jnp.sum(row_loss, axis=0, keepdims=True)
    sums[:, 2 * HID : 2 * HID + HEADP] = jnp.where(lane == HEAD, loss, head_sums)
    gwh[...] = dot(h2, g_out, ((0,), (0,)))
    each = HID // (HID // share * wide)
    for side in range(CORES):

        @pl.when(at_ref[HID // share] == side)
        def _(side=side):
            for n in range(HID // each // CORES):
                for c, part in ((side, gwh_own), (1 - side, gwh_sib)):
                    row = (n * CORES + c) * each
                    part[n * each : (n + 1) * each, :] = gwh[row : row + each, :].astype(bf16)

    g_h2 = dot(g_out, wh[...], ((1,), (1,)))
    g2 = (g_h2 * gelu_slope(pre2[...])).astype(bf16)
    sums[:, HID : 2 * HID] = jnp.sum(g2.astype(f32), axis=0, keepdims=True)
    gpre2[...] = g2
    for n, (pre, w2, g1, gw2, at) in enumerate(sides):
        g_h1 = dot(gpre2[...], w2[...], ((1,), (1,)))
        g = (g_h1 * gelu_slope(pre[...] + b1[:, at : at + units])).astype(bf16)
        g1[...] = g
        columns = jnp.sum(g.astype(f32), axis=0, keepdims=True)
        for k in range(units // share):
            to = pl.multiple_of(at_ref[n * (units // share) + k] * share, share)
            sums[:, pl.ds(to, share)] = columns[:, k * share : (k + 1) * share]
        gw2[...] = dot(h1[:, at : at + units], gpre2[...], ((0,), (0,))).astype(gw2.dtype)


def heads_step(share, wide, at, pre_own, pre_sib, w2_own, w2_sib, wh, b1, b2, bh, tags):
    rows, units = pre_own.shape
    vmem = pl.BlockSpec(memory_space=pltpu.VMEM)
    shape = jax.ShapeDtypeStruct
    return pl.pallas_call(
        functools.partial(head_kernel, share, wide),
        in_specs=[pl.BlockSpec(memory_space=pltpu.SMEM)] + [vmem] * 9,
        out_specs=[vmem] * 8,
        out_shape=[
            shape((rows, units), bf16),
            shape((rows, units), bf16),
            shape((units, HID), bf16),
            shape((units, HID), bf16),
            shape((HID // CORES, HEADP), bf16),
            shape((HID // CORES, HEADP), bf16),
            shape((1, 2 * HID + HEADP), f32),
            shape((1, 1), f32),
        ],
        scratch_shapes=[
            pltpu.VMEM((rows, HID), bf16),
            pltpu.VMEM((rows, HID), f32),
            pltpu.VMEM((rows, HID), bf16),
            pltpu.VMEM((HID, HEADP), f32),
        ],
        compiler_params=pltpu.CompilerParams(vmem_limit_bytes=WIDE * MIB),
        cost_estimate=LIGHT,
        name="heads",
    )(at, pre_own, pre_sib, w2_own, w2_sib, wh, b1, b2, bh, tags)


class Grid:
    def __init__(self):
        self.wide = lax.axis_size("wide")
        self.tp = lax.axis_size("tp")
        self.y = self.tp // CORES
        self.x = self.y if self.wide % self.y == 0 else 1
        self.z = self.wide // self.x
        self.size = {"z": self.z, "x": self.x, "y": self.y, "c": CORES}
        wide, tp = lax.axis_index("wide"), lax.axis_index("tp")
        self.at = {"z": wide // self.x, "x": wide % self.x, "y": tp // CORES, "c": tp % CORES}

    def move(self, value, axis, by):
        pairs = []
        for z in range(self.z):
            for x in range(self.x):
                for y in range(self.y):
                    for c in range(CORES):
                        to = {"z": z, "x": x, "y": y, "c": c}
                        for a in axis:
                            to[a] = (to[a] + by) % self.size[a]
                        pairs.append((self.index(z, x, y, c), self.index(to["z"], to["x"], to["y"], to["c"])))
        return lax.ppermute(value, AXES, pairs)

    def flip(self, value, axis, bit):
        unit = {"c": 1, "y": CORES, "x": CORES * self.y, "z": CORES * self.y * self.x}
        step = bit * sum(unit[a] for a in axis)
        return lax.ppermute(value, AXES, [(i, i ^ step) for i in range(self.wide * self.tp)])

    def index(self, z, x, y, c):
        return ((z * self.x + x) * self.y + y) * CORES + c

    def swap(self, value):
        return self.move(value, "c", 1)


def spread_stacked(grid, value, order):
    stack = value[None, None, None]
    for axis in order:
        place = "zxy".index(axis)
        stack = jnp.concatenate([stack] + [grid.move(stack, axis, by) for by in range(1, grid.size[axis])], axis=place)
    for place, axis in enumerate("zxy"):
        if grid.size[axis] > 1:
            back = (grid.at[axis] - jnp.arange(grid.size[axis])) % grid.size[axis]
            stack = jnp.take(stack, back, axis=place, mode="clip")
    return stack


def collect_stacked(grid, stack, order):
    left = "zxy"
    total = stack
    for axis in order:
        place = left.index(axis)
        total = total.astype(bf16)

        def block(by):
            at = (grid.at[axis] + by) % grid.size[axis]
            return lax.dynamic_index_in_dim(total, at, place, keepdims=False)

        mine = block(0).astype(f32)
        for by in range(1, grid.size[axis]):
            mine = mine + grid.move(block(by), axis, by).astype(f32)
        total = mine
        left = left.replace(axis, "")
    return total


def all_sum(value):
    count = lax.axis_size("wide") * lax.axis_size("tp")
    if count & (count - 1):
        return lax.psum(value, AXES)
    bit = 1
    while bit < count:
        value = value + lax.ppermute(value, AXES, [(i, i ^ bit) for i in range(count)])
        bit *= 2
    return value


def after(value, *others):
    return lax.optimization_barrier((value, *others))[0]


class Links:
    def __init__(self, grid, in_step):
        self.grid = grid
        self.in_step = in_step
        self.last = {}
        self.slots = [{}, {}]

    def next(self):
        self.slots.append({})

    def send(self, value, axis, by=1):
        before = [self.slots[-2]["x"]] if self.in_step and axis == "z" and "x" in self.slots[-2] else []
        if axis in self.last:
            before.append(self.last[axis])
        sent = self.grid.move(after(value, *before) if before else value, axis, by)
        self.last[axis] = self.slots[-1][axis] = sent
        return sent


def adam_update(weight, grad, first, second, rate):
    first_new = decay_one * first + (1.0 - decay_one) * grad
    second_new = decay_two * second + (1.0 - decay_two) * grad * grad
    first_hat = first_new / (1.0 - decay_one**STEP)
    second_hat = second_new / (1.0 - decay_two**STEP)
    weight_new = weight - rate * (first_hat / (jnp.sqrt(second_hat) + epsilon) + weight_decay * weight)
    return (weight_new, first_new, second_new)


def by_blocks(grid, feats, cols, share, second_cols, head_rows, channels, rows):
    return (
        (grid.z, grid.x, grid.y) == (4, 2, 2)
        and feats % 16 == 0
        and feats > max(LATE_OUT, LATE_BACK)
        and cols == channels == 256
        and second_cols == 128
        and (share, head_rows) == (256, 32)
        and rows % (CHUNKS * GROUP) == 0
        and block_span(feats, grid.wide, channels) > 0
    )


def wide_places(grid, sign):
    places = [
        ((grid.at["z"] + sign * dz) % grid.z) * grid.x + (grid.at["x"] + sign * dx) % grid.x
        for dz in range(grid.z)
        for dx in range(grid.x)
    ]
    return jnp.stack(places + [grid.at["y"]]).astype(jnp.int32)


def low_sum(first, *others):
    total = first.astype(f32)
    for value in others:
        total = total + value.astype(f32)
    return total.astype(bf16)


def terms(value):
    found = []
    for _ in range(TERMS):
        found.append(lax.optimization_barrier(value.astype(bf16)))
        value = value - found[-1].astype(f32)
    return jnp.concatenate(found, axis=0)


def from_terms(rows):
    count = rows.shape[0] // TERMS
    total = rows[:count].astype(f32)
    for k in range(1, TERMS):
        total = total + rows[k * count : (k + 1) * count].astype(f32)
    return total


def blocks_step(grid, make_crops, w_first, w_second, w_heads, biases, crowd, tags):
    feats, cols = w_first.shape
    share, _ = w_second.shape
    head_rows = w_heads.shape[0]
    core = grid.at["c"]
    core_ref = core.reshape(1).astype(jnp.int32)

    links = Links(grid, True)
    most = feats - LATE_OUT
    mine, first_low = prepare(w_first, w_second, w_heads, crowd, most)
    half = mine.shape[0] - feats
    m = {(0, 0, 0): mine}
    stacks = {}

    m[0, 1, 0] = grid.move(mine, "x", 1)
    m[0, 0, 1] = grid.move(mine, "y", 1)
    m[0, 1, 1] = grid.move(mine, "xy", 1)
    m[1, 0, 0] = grid.move(first_low, "z", 1)
    m[3, 0, 0] = grid.move(first_low, "z", 3)
    own_crops = [make_crops(i) for i in range(CHUNKS - 1)]
    own_crops.append(make_crops(CHUNKS - 1, m[1, 0, 0]))
    made = own_crops + [m[key] for key in ((0, 1, 0), (0, 0, 1), (0, 1, 1), (1, 0, 0), (3, 0, 0))]
    stacks[0] = jnp.stack([jnp.stack([m[0, x, y][most:] for x in range(grid.x)]) for y in range(grid.y)])
    m[2, 0, 0] = links.send(m[1, 0, 0], "z", 1)
    m[1, 1, 0] = links.send(after(m[1, 0, 0], *made), "x")
    m[1, 0, 1] = links.send(after(m[1, 0, 0], *made), "y")
    links.next()
    stacks[1] = links.send(stacks[0], "z", 1)
    m[3, 1, 0] = links.send(m[3, 0, 0], "x")
    m[3, 0, 1] = links.send(m[3, 0, 0], "y")
    links.next()
    stacks[3] = links.send(stacks[0], "z", 3)
    m[2, 1, 0] = links.send(m[2, 0, 0], "x")
    m[2, 0, 1] = links.send(m[2, 0, 0], "y")
    links.next()
    stacks[2] = links.send(stacks[1], "z", 1)
    m[1, 1, 1] = links.send(m[1, 0, 1], "x")
    m[2, 1, 1] = links.send(m[2, 1, 0], "y")
    links.next()
    sib_crops = []
    for chunk in own_crops:
        sib_crops.append(grid.swap(after(chunk, *made)))
    crops = own_crops + sib_crops

    def place(dz, dx, sign):
        z = (grid.at["z"] + sign * dz) % grid.z
        x = (grid.at["x"] + sign * dx) % grid.x
        return z * grid.x + x

    def places(keys, sign):
        return jnp.stack([place(*key, sign) for key in keys]).astype(jnp.int32)

    span = block_span(feats, grid.wide, cols)
    both = (0, 1)

    def products(work, before, *wait):
        inputs = [v for dz, dx, ys in work for v in [m[dz, dx, y] for y in ys] + [stacks[dz]]]
        where = after(places([(dz, dx) for dz, dx, _ in work], -1), *wait)
        items = tuple((dx, ys) for _, dx, ys in work)
        return first_blocks(where, crops, inputs, items, feats, most, span, grid.y, before)

    m[3, 1, 1] = links.send(m[3, 0, 1], "x")
    pre = products([(0, 0, both), (0, 1, both), (1, 0, both), (3, 0, both), (1, 1, both), (3, 1, (0,))], None)
    first_pre = pre[0]
    pre = products([(2, 0, both), (2, 1, both), (3, 1, (1,))], pre)
    sib_stacks = {2: grid.swap(after(stacks[2], first_pre))}
    sib_stacks[0] = grid.swap(stacks[0])
    sib_stacks[1] = grid.swap(after(stacks[1], sib_stacks[0]))
    sib_stacks[3] = grid.swap(after(stacks[3], sib_stacks[1], first_pre))
    second_own, second_sib, head_matrix = unpack(
        core_ref,
        wide_places(grid, -1),
        [stacks[z] for z in range(4)],
        [sib_stacks[z] for z in range(4)],
        half,
        HID // CORES,
    )
    bias = biases[:HID].reshape(grid.y, CORES, share)
    bias = jnp.where(grid.at["y"] == 0, bias, bias[::-1])
    bias = jnp.where(core == 0, bias, bias[:, ::-1]).transpose(1, 0, 2).reshape(1, -1)
    unit_at = [2 * ((grid.at["y"] + y) % grid.y) + c for c in (core, 1 - core) for y in range(grid.y)]
    g_own, g_send, gw2, gw2_send, gwh, gwh_send, sums, roi_count = heads_step(
        share,
        grid.wide,
        jnp.stack(unit_at + [core]).astype(jnp.int32),
        pre[0],
        grid.swap(pre[1]),
        second_own,
        second_sib,
        head_matrix,
        bias,
        biases[HID : 2 * HID].reshape(1, -1),
        jnp.pad(biases[2 * HID :], (0, HEADP - HEAD)).reshape(1, -1),
        tags,
    )

    g_got = grid.swap(g_send)
    m = {}
    parts = {}

    def gradients(keys, wait=()):
        where = places(keys, 1)
        outs = first_grad_blocks(after(where, *wait), crops, g_own, g_got, feats, LATE_BACK, grid.y, span)
        for i, (dz, dx) in enumerate(keys):
            for y in range(grid.y):
                m[dz, dx, y], parts[dz, dx, y] = outs[(i * grid.y + y) * 2 : (i * grid.y + y) * 2 + 2]

    gradients([(2, 1), (2, 0), (3, 1), (3, 0)])
    shape = (grid.z, grid.y, grid.x, half + EXTRA, cols)
    packed = pack(wide_places(grid, 1), gw2, grid.swap(gw2_send), gwh, grid.swap(gwh_send), sums, shape)

    def stack_of(dz):
        first = jnp.stack([jnp.stack([parts[dz, dx, y] for dx in range(grid.x)]) for y in range(grid.y)])
        return jnp.concatenate([first, packed[dz]], axis=2)

    links = Links(grid, False)
    far = stack_of(2)
    gradients([(1, 1), (1, 0), (0, 1), (0, 0)], [far])
    begun = (far, m[3, 1, 1])
    z0 = links.send(after(far, *begun[1:]), "z", 1)
    y0 = links.send(after(m[2, 1, 1], *begun), "y")
    x0 = links.send(after(m[3, 1, 1], *begun[:1]), "x")
    z1 = links.send(stack_of(3), "z", 3)
    y1 = links.send(m[2, 0, 1], "y")
    x1 = links.send(m[3, 1, 0], "x")
    z2 = links.send(low_sum(stack_of(1), z0), "z", 1)
    x2 = links.send(low_sum(m[2, 1, 0], y0), "x")
    y2 = links.send(low_sum(m[3, 0, 1], x0), "y")
    z3 = links.send(low_sum(m[2, 0, 0], x2, y1), "z", 1)
    x3 = links.send(m[1, 1, 1], "x")
    y3 = links.send(m[0, 1, 1], "y")
    z4 = links.send(low_sum(m[3, 0, 0], x1, y2), "z", 3)
    x4 = links.send(m[1, 1, 0], "x")
    y4 = links.send(low_sum(m[1, 0, 1], x3), "y")

    def extra_rows(stack):
        rows = stack[:, :, -EXTRA : 8 - EXTRA].reshape(-1, cols)
        return from_terms(rows[: TERMS * (sums.shape[1] // cols)])

    odd = grid.at["z"] % 2 == 1
    below, above, opposite = extra_rows(z0), extra_rows(z1), extra_rows(z2)
    total = sums.reshape(-1, cols)
    total = (total + jnp.where(odd, below, above)) + (opposite + jnp.where(odd, above, below))
    count = TERMS * total.shape[0]
    late = low_sum(stack_of(0), z1, z2)
    x5 = links.send(jnp.concatenate([late[:, 1].reshape(-1, cols), terms(total)], axis=0), "x")
    x6 = links.send(low_sum(m[0, 1, 0], y3), "x")
    z5 = links.send(low_sum(m[1, 0, 0], x4, y4, z3), "z", 1)
    y5 = links.send(m[0, 0, 1], "y")
    total = total + from_terms(x5[-count:])
    late = low_sum(late[:, 0], x5[:-count].reshape(late[:, 0].shape))
    y6 = links.send(jnp.concatenate([late[1], terms(total)], axis=0), "y")
    total = total + from_terms(y6[-count:])
    total = total + grid.swap(total)
    sums = total.reshape(1, -1)
    main = m[0, 0, 0].astype(f32)
    for value in (x6, y5, z4, z5):
        main = main + value.astype(f32)
    late = late[0].astype(f32) + y6[:-count].astype(f32)

    first_total = jnp.concatenate([main, late[:LATE_BACK]], axis=0)
    late = late[LATE_BACK : LATE_BACK + half]
    total = jnp.concatenate([late[:, :128], late[:, 128:]], axis=0)
    heads_total = jnp.concatenate(
        [total[share + k * head_rows : share + (k + 1) * head_rows] for k in range(HEADP // 128)], axis=1
    )[:, :HEAD]
    return roi_count.reshape(()), sums, first_total, total[:share], heads_total


def stacked_step(grid, make_crops, w_first, w_second, w_heads, biases, crowd, tags):
    feats, cols = w_first.shape
    share, second_cols = w_second.shape
    head_rows = w_heads.shape[0]
    units = HID // CORES
    core = grid.at["c"]
    kept = jnp.sum(1 - crowd)
    head_block = jnp.pad(w_heads, ((0, 0), (0, HEADP - HEAD)))
    spot = (lax.broadcasted_iota(jnp.int32, head_block.shape, 0) == 0) * 1
    lane = lax.broadcasted_iota(jnp.int32, head_block.shape, 1)
    head_block = head_block + (
        spot * (jnp.where(lane == HEADP - 1, kept % 128, 0) + jnp.where(lane == HEADP - 2, kept // 128, 0))
    ).astype(f32)
    small = jnp.concatenate(
        [w_second.astype(bf16).reshape(-1, cols), head_block.astype(bf16).reshape(-1, cols)], axis=0
    )
    second_rows = share * second_cols // cols
    small_all = spread_stacked(grid, small, "zxy").reshape(grid.wide, grid.y, *small.shape)
    weight = spread_stacked(grid, w_first.astype(bf16), "zxy")
    weight = weight.transpose(2, 0, 1, 3, 4).reshape(grid.y, grid.wide * feats, cols)
    crops = [make_crops(i) for i in range(CHUNKS)]
    crops = crops + [grid.swap(c) for c in crops]
    second_own = (
        small_all[:, :, :second_rows]
        .reshape(grid.wide, grid.y, share, second_cols)
        .transpose(1, 2, 0, 3)
        .reshape(units, HID)
    )
    heads_own = small_all[:, :, second_rows:].reshape(grid.wide, grid.y, head_rows, HEADP)
    heads_sib = grid.swap(heads_own)
    head_matrix = jnp.where(
        core == 0, jnp.stack([heads_own, heads_sib], axis=2), jnp.stack([heads_sib, heads_own], axis=2)
    ).reshape(HID, HEADP)
    bias = biases[:HID].reshape(grid.y, CORES, share)
    bias = jnp.where(core == 0, bias, bias[:, ::-1]).transpose(1, 0, 2).reshape(1, -1)
    pre_own, pre_send = first_layer(crops, weight)
    unit_at = [2 * y + c for c in (core, 1 - core) for y in range(grid.y)]
    g_own, g_send, gw2_own, gw2_send, gwh, gwh_send, sums, roi_count = heads_step(
        share,
        grid.wide,
        jnp.stack([jnp.asarray(v) for v in unit_at + [core]]).astype(jnp.int32),
        pre_own,
        grid.swap(pre_send),
        second_own,
        grid.swap(second_own),
        head_matrix,
        bias,
        biases[HID : 2 * HID].reshape(1, -1),
        jnp.pad(biases[2 * HID :], (0, HEADP - HEAD)).reshape(1, -1),
        tags,
    )
    grad = first_grad(crops, g_own, grid.swap(g_send), grid.y)
    grad = grad.reshape(grid.y, grid.wide, feats, cols).transpose(1, 0, 2, 3)
    first_total = collect_stacked(grid, grad.reshape(grid.z, grid.x, grid.y, feats, cols), "yxz")
    gw2 = gw2_own.astype(f32) + grid.swap(gw2_send).astype(f32)
    gwh = gwh.astype(f32) + grid.swap(gwh_send).astype(f32)
    gw2 = gw2.astype(bf16).reshape(grid.y, share, grid.wide, second_cols).transpose(2, 0, 1, 3)
    small_grad = jnp.concatenate(
        [
            gw2.reshape(grid.wide, grid.y, second_rows, cols),
            gwh.astype(bf16).reshape(grid.wide, grid.y, -1, cols),
        ],
        axis=2,
    ).reshape(grid.z, grid.x, grid.y, -1, cols)
    small_total = collect_stacked(grid, small_grad, "yxz")
    second_total = small_total[:second_rows].reshape(share, second_cols)
    heads_total = small_total[second_rows:].reshape(head_rows, HEADP)[:, :HEAD]
    sums = all_sum(sums)
    return roi_count.reshape(()), sums, first_total, second_total, heads_total


def shards(
    maps,
    roi_image,
    roi_level,
    roi_corner,
    roi_weights,
    crowd,
    labels,
    box_targets,
    w_first,
    m_first,
    v_first,
    w_second,
    m_second,
    v_second,
    w_heads,
    m_heads,
    v_heads,
    biases,
    bias_m,
    bias_v,
):
    grid = Grid()
    rows = crowd.shape[0]

    images, levels, height, width, channels = maps.shape
    base = ((roi_image * levels + roi_level) * height + roi_corner[:, 0]).astype(jnp.int32)
    col = roi_corner[:, 1].astype(jnp.int32)
    flat_maps = maps.reshape(images * levels * height, width, channels)
    padded = jnp.pad(roi_weights, ((0, 0), (0, 0), (0, 1), (0, 0)))
    row_w = padded[:, 0].reshape(rows * 8, WIN)
    col_w = padded[:, 1].reshape(rows * 8, WIN)
    step = rows // CHUNKS
    tags = jnp.concatenate(
        [box_targets.astype(f32), labels[:, None].astype(f32), crowd[:, None].astype(f32)], axis=1
    )

    def make_crops(i, *wait):
        return window_crops(flat_maps, after(base, *wait) if wait else base, col, row_w, col_w, i * step, step)

    shapes = (*w_first.shape, *w_second.shape, w_heads.shape[0], channels, rows)
    run = blocks_step if by_blocks(grid, *shapes) else stacked_step
    roi_count, sums, first_total, second_total, heads_total = run(
        grid, make_crops, w_first, w_second, w_heads, biases, crowd, tags
    )
    loss_total = sums[0, 2 * HID + HEAD]
    bias_grad = sums[0, : 2 * HID + HEAD]

    first_out = adam_update(w_first, first_total, m_first, v_first, rate_first)
    second_out = adam_update(w_second, second_total, m_second, v_second, rate_second)
    heads_out = adam_update(w_heads, heads_total, m_heads, v_heads, rate_heads)
    bias_out = adam_update(biases, bias_grad, bias_m, bias_v, rate_biases)
    return (loss_total, roi_count, *first_out, *second_out, *heads_out, *bias_out)


def solution(mesh):
    rows = P(("wide", "tp"))
    both = P("wide", "tp")
    turned = P("tp", "wide")
    return jax.shard_map(
        shards,
        mesh=mesh,
        in_specs=(rows,) * 8 + (both,) * 3 + (turned,) * 3 + (rows,) * 3 + (P(),) * 3,
        out_specs=(P(), P()) + (both,) * 3 + (turned,) * 3 + (rows,) * 3 + (P(),) * 3,
        check_vma=False,
    )
```

```python
import functools

import jax
import jax.numpy as jnp
import numpy as np
from jax import lax
from jax.experimental import pallas as pl
from jax.experimental.pallas import tpu as pltpu
from jax.sharding import PartitionSpec as P

HID = 1024
CLS = 81
POOL = 7
CELLS = POOL * POOL
WIN = 16
STEP = 10
HEAD = 401
HEADP = 512
CORES = 2
CHUNKS = 4
EARLY = 2
GROUP = 32
KSTEP = 7
LATE_OUT = 192
LATE_BACK = 208
TERMS = 3
EXTRA = 16
WIDE = 60
MIB = 2**20
LIGHT = pl.CostEstimate(flops=0, bytes_accessed=1024, transcendentals=0)

AXES = ("wide", "tp")
rate_first = 0.02
rate_second = 0.06
rate_heads = 0.06
rate_biases = 0.3
decay_one = 0.9
decay_two = 0.999
epsilon = 1e-08
weight_decay = 0.1
GELU_A = 0.7978845608028654
GELU_B = 0.044715

f32 = jnp.float32
bf16 = jnp.bfloat16


def dot(a, b, contract=((1,), (0,))):
    return lax.dot_general(a, b, (contract, ((), ())), preferred_element_type=f32)


def crop_kernel(first, base_ref, col_ref, maps_ref, wr_ref, wc_ref, rep_ref, tile_ref, *refs):
    out_ref, rows_s, cols_s, left, right = refs
    step = pl.program_id(0)
    lanes = rows_s.shape[1]
    halves = (left, right)
    rows_s[...] = dot(wr_ref[...], rep_ref[...])
    cols_s[...] = dot(wc_ref[...], tile_ref[...])

    def one(i, carry):
        r = first + step * GROUP + i
        at = pl.multiple_of(i * 8, 8)
        rows = rows_s[pl.ds(at, 8), :]
        x0 = col_ref[r]
        cols = jnp.concatenate(
            [pltpu.roll(cols_s[pl.ds(at, 8), k : k + 128], x0, 1) for k in range(0, lanes, 128)], axis=1
        )
        both = jnp.concatenate([rows[a : a + 1, :] * cols for a in range(POOL)], axis=0)
        high = both.astype(bf16)
        low = (both - high.astype(f32)).astype(bf16)
        window = maps_ref[pl.ds(base_ref[r], WIN), :, :].reshape(lanes, maps_ref.shape[2])
        got = dot(jnp.concatenate([high, low], axis=0), window)
        got = got[: POOL * 8] + got[POOL * 8 :]
        for h, half in enumerate(halves):
            half[pl.ds(pl.multiple_of(i * POOL * 8, 8), POOL * 8), :] = got[:, h * 128 : (h + 1) * 128]
        return carry

    lax.fori_loop(0, GROUP, one, 0, unroll=4)
    for a in range(POOL):
        for b in range(POOL):
            for h, half in enumerate(halves):
                out_ref[a * POOL + b, :, h * 128 : (h + 1) * 128] = half[
                    pl.ds(a * 8 + b, GROUP, stride=POOL * 8), :
                ].astype(bf16)


def window_crops(maps, base, col, wr, wc, first, count):
    rows, width, channels = maps.shape
    lanes = WIN * width
    lane = np.arange(lanes)[None]
    unit = np.arange(WIN)[:, None]
    rep = jnp.asarray(lane // width == unit, bf16)
    til = jnp.asarray(lane % width == unit, bf16)
    return pl.pallas_call(
        functools.partial(crop_kernel, first),
        grid_spec=pltpu.PrefetchScalarGridSpec(
            num_scalar_prefetch=2,
            grid=(count // GROUP,),
            in_specs=[
                pl.BlockSpec(maps.shape, lambda i, *_: (0, 0, 0)),
                pl.BlockSpec((GROUP * 8, WIN), lambda i, *_: (first // GROUP + i, 0)),
                pl.BlockSpec((GROUP * 8, WIN), lambda i, *_: (first // GROUP + i, 0)),
                pl.BlockSpec(rep.shape, lambda i, *_: (0, 0)),
                pl.BlockSpec(til.shape, lambda i, *_: (0, 0)),
            ],
            out_specs=pl.BlockSpec((CELLS, GROUP, channels), lambda i, *_: (0, i, 0)),
            scratch_shapes=[
                pltpu.VMEM((GROUP * 8, lanes), f32),
                pltpu.VMEM((GROUP * 8, lanes), f32),
                pltpu.VMEM((GROUP * POOL * 8, 128), f32),
                pltpu.VMEM((GROUP * POOL * 8, 128), f32),
            ],
        ),
        out_shape=jax.ShapeDtypeStruct((CELLS, count, channels), bf16),
        compiler_params=pltpu.CompilerParams(vmem_limit_bytes=18 * MIB),
        cost_estimate=LIGHT,
        name="crops",
    )(base, col, maps, wr, wc, rep, til)


def first_kernel(parts, *refs):
    crops, weight, own, send = refs[:parts], refs[parts], refs[parts + 1], refs[parts + 2]
    step = pl.program_id(0)
    blocks, depth, cols = weight.shape
    channels = crops[0].shape[2]

    @pl.when(step == 0)
    def _():
        own[...] = jnp.zeros_like(own)
        send[...] = jnp.zeros_like(send)

    for out, refs_half in ((own, crops[: parts // 2]), (send, crops[parts // 2 :])):
        lhs = jnp.concatenate(
            [jnp.concatenate([ref[j] for ref in refs_half], axis=0) for j in range(depth // channels)], axis=1
        )
        for y in range(blocks):
            out[:, y * cols : (y + 1) * cols] += dot(lhs, weight[y])


def first_layer(crops, weight):
    parts = len(crops)
    blocks, feats, cols = weight.shape
    channels = crops[0].shape[2]
    rows = sum(c.shape[1] for c in crops) // 2
    return pl.pallas_call(
        functools.partial(first_kernel, parts),
        grid=(CELLS // KSTEP,),
        in_specs=[pl.BlockSpec((KSTEP,) + c.shape[1:], lambda i: (i, 0, 0)) for c in crops]
        + [pl.BlockSpec((blocks, KSTEP * channels, cols), lambda i: (0, i, 0))],
        out_specs=[pl.BlockSpec((rows, blocks * cols), lambda i: (0, 0))] * 2,
        out_shape=[jax.ShapeDtypeStruct((rows, blocks * cols), f32)] * 2,
        compiler_params=pltpu.CompilerParams(vmem_limit_bytes=60 * MIB),
        cost_estimate=LIGHT,
        name="first_layer",
    )(*crops, weight)


def first_grad_kernel(parts, cols, *refs):
    crops, own, got, out = refs[:parts], refs[parts], refs[parts + 1], refs[parts + 2]
    channels = crops[0].shape[2]
    grads = jnp.concatenate([own[...], got[...]], axis=0)
    for j in range(crops[0].shape[0]):
        lhs = jnp.concatenate([ref[j] for ref in crops], axis=0)
        res = dot(lhs, grads, ((0,), (0,))).astype(bf16)
        for y in range(out.shape[0]):
            out[y, j * channels : (j + 1) * channels, :] = res[:, y * cols : (y + 1) * cols]


def first_grad(crops, own, got, blocks):
    parts = len(crops)
    rows, units = own.shape
    cols = units // blocks
    channels = crops[0].shape[2]
    return pl.pallas_call(
        functools.partial(first_grad_kernel, parts, cols),
        grid=(CELLS // KSTEP,),
        in_specs=[pl.BlockSpec((KSTEP,) + c.shape[1:], lambda i: (i, 0, 0)) for c in crops]
        + [pl.BlockSpec((rows, units), lambda i: (0, 0))] * 2,
        out_specs=pl.BlockSpec((blocks, KSTEP * channels, cols), lambda i: (0, i, 0)),
        out_shape=jax.ShapeDtypeStruct((blocks, CELLS * channels, cols), bf16),
        compiler_params=pltpu.CompilerParams(vmem_limit_bytes=60 * MIB),
        cost_estimate=LIGHT,
        name="first_grad",
    )(*crops, own, got)


def block_span(feats, wide, channels):
    span = max(-(-((w * feats) % channels + feats) // channels) for w in range(wide))
    return span if all(w * feats // channels + span <= CELLS for w in range(wide)) else 0


def cell_copies(crops, start, span, cells, sems):
    found = []
    at = 0
    for n, ref in enumerate(crops):
        rows = ref.shape[1]
        found.append(pltpu.make_async_copy(ref.at[pl.ds(start, span)], cells.at[:, pl.ds(at, rows)], sems.at[n]))
        at += rows
    return found


def rows_of(kind, feats, most):
    return {"all": (0, feats), "most": (0, most), "last": (most, feats)}[kind]


def kind_span(kind, feats, most, wide, channels):
    begin, end = rows_of(kind, feats, most)
    return max(-(-((w * feats + begin) % channels + end - begin) // channels) for w in range(wide))


def block_kernel(items, feats, most, wide, parts, fresh, table, *refs):
    count = len(items)
    crops, rest = refs[:parts], refs[parts:]
    own, send, pad, cells, sems = rest[-5:]
    before, inputs = (None, rest[:-5]) if fresh else (rest[:2], rest[2:-5])
    step = pl.program_id(0)
    rows = own.shape[0]
    channels = cells.shape[3]
    cols = channels
    needs = [len(item[2]) * (item[3] != "last") + (item[3] != "most") for item in items]
    spans = [kind_span(item[3], feats, most, wide, channels) for item in items]

    def copies(i):
        slot = i % 2
        number, side, ys, kind = items[i]
        begin, end = rows_of(kind, feats, most)
        start = table[number] * feats + begin
        cell = jnp.minimum(start // channels, CELLS - spans[i])
        at = pl.multiple_of(start - cell * channels, 16)
        found = cell_copies(crops, cell, spans[i], cells.at[slot, pl.ds(0, spans[i])], sems.at[slot])
        group = inputs[sum(needs[:i]) : sum(needs[: i + 1])]
        for k, y in enumerate(ys):
            lanes = pl.ds(y * cols, cols)
            if kind != "last":
                source = group[k].at[pl.ds(0, most)]
                found.append(
                    pltpu.make_async_copy(source, pad.at[slot, pl.ds(at, most), lanes], sems.at[slot, parts + 2 * k])
                )
            if kind != "most":
                source = group[-1].at[y, side, pl.ds(0, feats - most)]
                to = pl.ds(pl.multiple_of(at + most - begin, 16), feats - most)
                found.append(pltpu.make_async_copy(source, pad.at[slot, to, lanes], sems.at[slot, parts + 1 + 2 * k]))
        return found

    def edges(i):
        begin, end = rows_of(items[i][3], feats, most)
        deep = spans[i] * channels
        low = (end - begin) // channels * channels
        lanes = pad.shape[2]
        if low:
            pad[i % 2, :channels, :] = jnp.zeros((channels, lanes), bf16)
        pad[i % 2, low:deep, :] = jnp.zeros((deep - low, lanes), bf16)

    @pl.when(step == 0)
    def _():
        edges(0)
        for copy in copies(0):
            copy.start()
        if fresh:
            own[...] = jnp.zeros_like(own)
            send[...] = jnp.zeros_like(send)
        else:
            own[...] = before[0][...]
            send[...] = before[1][...]

    for i in range(count):

        @pl.when(step == i)
        def _(i=i):
            if i + 1 < count:
                edges(i + 1)
                for copy in copies(i + 1):
                    copy.start()
            for copy in copies(i):
                copy.wait()

    slot = lax.rem(step, 2)
    forms = [(span, item[2]) for span, item in zip(spans, items)]
    for form in sorted(set(forms)):
        span, ys = form
        lanes = slice(ys[0] * cols, (ys[-1] + 1) * cols)

        @pl.when(functools.reduce(jnp.logical_or, [step == i for i in range(count) if forms[i] == form]))
        def _(span=span, lanes=lanes):
            lhs = jnp.concatenate([cells[slot, j] for j in range(span)], axis=1)
            got = dot(lhs, pad[slot, : span * channels, lanes])
            own[:, lanes] += got[:rows]
            send[:, lanes] += got[rows:]


def whole(shape):
    return pl.BlockSpec(shape, lambda i, place: (0,) * len(shape))


def first_blocks(table, crops, inputs, items, feats, most, wide, blocks, before):
    rows = sum(c.shape[1] for c in crops) // 2
    channels = crops[0].shape[2]
    units = blocks * channels
    lead = [] if before is None else list(before)
    away = pl.BlockSpec(memory_space=pl.ANY)
    parts = len(crops)
    span = kind_span("all", feats, most, wide, channels)
    return pl.pallas_call(
        functools.partial(block_kernel, items, feats, most, wide, parts, before is None),
        grid_spec=pltpu.PrefetchScalarGridSpec(
            num_scalar_prefetch=1,
            grid=(len(items),),
            in_specs=[away] * parts + [whole((rows, units))] * len(lead) + [away] * len(inputs),
            out_specs=[whole((rows, units))] * 2,
            scratch_shapes=[
                pltpu.VMEM((2, span * channels, units), bf16),
                pltpu.VMEM((2, span, 2 * rows, channels), bf16),
                pltpu.SemaphoreType.DMA((2, parts + 2 * blocks)),
            ],
        ),
        out_shape=[jax.ShapeDtypeStruct((rows, units), f32)] * 2,
        input_output_aliases={} if before is None else {1 + parts: 0, 2 + parts: 1},
        compiler_params=pltpu.CompilerParams(vmem_limit_bytes=WIDE * MIB),
        cost_estimate=LIGHT,
        name="first_blocks",
    )(table, *crops, *lead, *inputs)


def block_grad_kernel(span, numbers, feats, blocks, parts, table, *refs):
    crops, (own, got), rest = refs[:parts], refs[parts : parts + 2], refs[parts + 2 :]
    outs, (full, cells, in_sems, out_sems) = rest[:-4], rest[-4:]
    step = pl.program_id(0)
    count = len(outs) // (2 * blocks)
    channels = cells.shape[3]
    cols = full.shape[2] // blocks

    def loads(i):
        return cell_copies(crops, (table[numbers[i]] * feats) // channels, span, cells.at[i % 2], in_sems.at[i % 2])

    def stores(i):
        at = pl.multiple_of((table[numbers[i]] * feats) % channels, 16)
        found = []
        for y in range(blocks):
            main, late = outs[(i * blocks + y) * 2], outs[(i * blocks + y) * 2 + 1]
            most = main.shape[0]
            lanes = pl.ds(y * cols, cols)
            found.append(pltpu.make_async_copy(full.at[i % 2, pl.ds(at, most), lanes], main, out_sems.at[i % 2, 2 * y]))
            found.append(
                pltpu.make_async_copy(
                    full.at[i % 2, pl.ds(pl.multiple_of(at + most, 16), feats - most), lanes],
                    late,
                    out_sems.at[i % 2, 2 * y + 1],
                )
            )
        return found

    @pl.when(step == 0)
    def _():
        for copy in loads(0):
            copy.start()

    for i in range(count):

        @pl.when(step == i)
        def _(i=i):
            if i + 1 < count:
                for copy in loads(i + 1):
                    copy.start()
            for copy in loads(i):
                copy.wait()
            if i >= 2:
                for copy in stores(i - 2):
                    copy.wait()

    slot = lax.rem(step, 2)
    grads = jnp.concatenate([own[...], got[...]], axis=0)
    for j in range(span):
        full[slot, j * channels : (j + 1) * channels, :] = dot(cells[slot, j], grads, ((0,), (0,))).astype(bf16)

    for i in range(count):

        @pl.when(step == i)
        def _(i=i):
            for copy in stores(i):
                copy.start()
            if i == count - 1:
                for k in range(max(0, count - 2), count):
                    for copy in stores(k):
                        copy.wait()


def first_grad_blocks(table, numbers, crops, own, got, feats, late, blocks, span):
    rows, units = own.shape
    channels = crops[0].shape[2]
    cols = units // blocks
    count = len(numbers)
    parts = len(crops)
    outs = [(feats - late, cols), (late, cols)] * (count * blocks)
    away = pl.BlockSpec(memory_space=pl.ANY)
    return pl.pallas_call(
        functools.partial(block_grad_kernel, span, numbers, feats, blocks, parts),
        grid_spec=pltpu.PrefetchScalarGridSpec(
            num_scalar_prefetch=1,
            grid=(count,),
            in_specs=[away] * parts + [whole((rows, units))] * 2,
            out_specs=[away] * len(outs),
            scratch_shapes=[
                pltpu.VMEM((2, span * channels, units), bf16),
                pltpu.VMEM((2, span, 2 * rows, channels), bf16),
                pltpu.SemaphoreType.DMA((2, parts)),
                pltpu.SemaphoreType.DMA((2, 2 * blocks)),
            ],
        ),
        out_shape=[jax.ShapeDtypeStruct(v, bf16) for v in outs],
        compiler_params=pltpu.CompilerParams(vmem_limit_bytes=WIDE * MIB),
        cost_estimate=LIGHT,
        name="first_grad",
    )(table, *crops, own, got)


def small_place(half, begin, end):
    lane = 0 if end <= half else 128
    back = half if lane else 0
    return slice(begin - back, end - back), slice(lane, lane + 128)


def prepare_kernel(first, second, heads, crowd, mine, low, wide_heads):
    feats = first.shape[0]
    share = second.shape[0]
    rows = heads.shape[0]
    half = mine.shape[0] - feats
    value = first[...].astype(bf16)
    mine[:feats, :] = value
    low[...] = value[: low.shape[0], :]
    kept = jnp.sum(1 - crowd[...], axis=1, keepdims=True)
    wide_heads[...] = jnp.zeros_like(wide_heads)
    wide_heads[:, :HEAD] = heads[...]
    lane = lax.broadcasted_iota(jnp.int32, (rows, 128), 1)
    row = lax.broadcasted_iota(jnp.int32, (rows, 128), 0)
    marks = jnp.where(lane == 127, kept % 128, jnp.where(lane == 126, kept // 128, 0))
    wide_heads[:, HEADP - 128 :] += jnp.where(row == 0, marks, 0).astype(f32)
    for begin, end in ((0, min(share, half)), (half, share)):
        if begin < end:
            at, lanes = small_place(half, begin, end)
            mine[feats + at.start : feats + at.stop, lanes] = second[begin:end, :].astype(bf16)
    for k in range(HEADP // 128):
        at, lanes = small_place(half, share + k * rows, share + (k + 1) * rows)
        mine[feats + at.start : feats + at.stop, lanes] = wide_heads[:, k * 128 : (k + 1) * 128].astype(bf16)


def prepare(first, second, heads, crowd, most):
    feats, cols = first.shape
    half = (second.shape[0] + heads.shape[0] * HEADP // 128) // 2
    vmem = pl.BlockSpec(memory_space=pltpu.VMEM)
    return pl.pallas_call(
        prepare_kernel,
        in_specs=[vmem] * 4,
        out_specs=[vmem] * 2,
        out_shape=[jax.ShapeDtypeStruct((feats + half, cols), bf16), jax.ShapeDtypeStruct((most, cols), bf16)],
        scratch_shapes=[pltpu.VMEM((heads.shape[0], HEADP), f32)],
        cost_estimate=LIGHT,
        compiler_params=pltpu.CompilerParams(vmem_limit_bytes=16 * MIB),
        name="prepare",
    )(first, second, heads, crowd[None, :])


def pack_kernel(table, *refs):
    lates, sides, sums = refs[:8], refs[8:12], refs[12]
    stack_two, stack_three, near_out, near, far, gw2s, gwhs, late_sems, in_sems, small_sems = refs[13:]
    gw2, gw2_got, gwh, gwh_got = gw2s.at[0], gw2s.at[1], gwhs.at[0], gwhs.at[1]
    arrive = [
        pltpu.make_async_copy(ref, to, in_sems.at[n]) for n, (ref, to) in enumerate(zip(sides, (gw2, gw2_got, gwh, gwh_got)))
    ]
    for copy in arrive:
        copy.start()
    depth = near.shape[0] + far.shape[0]
    _, blocks, xs, tall, _ = near.shape
    half = tall - EXTRA
    share = gw2.shape[0] // blocks
    count = depth * xs
    rows = gwh.shape[0] // (count * blocks)
    long = lates[0].shape[0]
    stacks = (stack_two, stack_three)
    copies = []
    for d in range(2):
        for y in range(blocks):
            for x in range(xs):
                n = (d * blocks + y) * xs + x
                copies.append(pltpu.make_async_copy(lates[n], far.at[d, y, x, pl.ds(0, long)], late_sems.at[n]))
    for copy in copies:
        copy.start()
    rest = sums[...]
    rows_left = []
    for _ in range(TERMS):
        term = rest.astype(bf16).astype(f32)
        rest = rest - term
        rows_left += [term[:, k : k + 256] for k in range(0, term.shape[1], 256)]
    rows_left += [jnp.zeros_like(rows_left[0])] * (-len(rows_left) % (blocks * xs))
    each = len(rows_left) // (blocks * xs)
    for copy in arrive:
        copy.wait()
    for dz in (2, 3, 1, 0):
        out, at, skip = (far, dz - 2, long) if dz >= 2 else (near, dz, 0)
        for y in range(blocks):
            for x in range(xs):
                here = table[count + dz * xs + x]
                lanes = pl.ds(pl.multiple_of(here * 128, 128), 128)

                def small(begin, end, value):
                    rows_at, lanes_at = small_place(half, begin, end)
                    out[at, y, x, skip + rows_at.start : skip + rows_at.stop, lanes_at] = value.astype(bf16)

                turned = (blocks - y) % blocks
                for begin, end in ((0, min(share, half)), (half, share)):
                    if begin < end:
                        part = slice(turned * share + begin, turned * share + end)
                        small(begin, end, gw2[part, lanes].astype(f32) + gw2_got[part, lanes].astype(f32))
                ahead = lax.rem(table[2 * count] + y, blocks)
                block = pl.ds(pl.multiple_of((here * blocks + ahead) * rows, rows), rows)
                for k in range(HEADP // 128):
                    group = slice(k * 128, (k + 1) * 128)
                    value = gwh[block, group].astype(f32) + gwh_got[block, group].astype(f32)
                    small(share + k * rows, share + (k + 1) * rows, value)
                n = y * xs + x
                some = rows_left[n * each : (n + 1) * each] + [jnp.zeros_like(rows_left[0])] * (EXTRA - each)
                some = jnp.concatenate(some, axis=0).astype(bf16)
                out[at, y, x, skip + half :, :] = some if dz >= 2 else jnp.zeros_like(some)
        if dz >= 2:
            for copy in copies[at * blocks * xs : (at + 1) * blocks * xs]:
                copy.wait()
            pltpu.make_async_copy(far.at[at], stacks[at], small_sems.at[at]).start()
    last = pltpu.make_async_copy(near, near_out, small_sems.at[2])
    last.start()
    for at in range(2):
        pltpu.make_async_copy(far.at[at], stacks[at], small_sems.at[at]).wait()
    last.wait()


def pack(table, lates, gw2, gwh, sums, half, places):
    smem = pl.BlockSpec(memory_space=pltpu.SMEM)
    vmem = pl.BlockSpec(memory_space=pltpu.VMEM)
    away = pl.BlockSpec(memory_space=pl.ANY)
    long, cols = lates[0].shape
    tall = half + EXTRA
    stack = jax.ShapeDtypeStruct((*places, long + tall, cols), bf16)
    return pl.pallas_call(
        pack_kernel,
        in_specs=[smem] + [away] * (len(lates) + 4) + [vmem],
        out_specs=[away] * 3,
        out_shape=[stack, stack, jax.ShapeDtypeStruct((2, *places, tall, cols), bf16)],
        scratch_shapes=[
            pltpu.VMEM((2, *places, tall, cols), bf16),
            pltpu.VMEM((2, *places, long + tall, cols), bf16),
            pltpu.VMEM((2, *gw2[0].shape), bf16),
            pltpu.VMEM((2, *gwh[0].shape), bf16),
            pltpu.SemaphoreType.DMA((len(lates),)),
            pltpu.SemaphoreType.DMA((4,)),
            pltpu.SemaphoreType.DMA((3,)),
        ],
        cost_estimate=LIGHT,
        compiler_params=pltpu.CompilerParams(vmem_limit_bytes=WIDE * MIB),
        name="pack",
    )(table, *lates, *gw2, *gwh, sums)


def gelu(x):
    return 0.5 * x * (1.0 + jnp.tanh(GELU_A * (x + GELU_B * x * x * x)))


def gelu_slope(x):
    t = jnp.tanh(GELU_A * (x + GELU_B * x * x * x))
    return 0.5 * (1.0 + t) + 0.5 * x * (1.0 - t * t) * (GELU_A * (1.0 + 3.0 * GELU_B * x * x))


def kept_count(wh):
    ends = jnp.sum(wh[:, HEADP - 128 :].astype(f32), axis=0, keepdims=True)
    return 128.0 * ends[:, 126:127] + ends[:, 127:128]


def losses(out, label, valid, targets, kept):
    col = lax.broadcasted_iota(jnp.int32, out.shape, 1)
    fore = jnp.where(label > 0, valid, 0.0)
    is_logit = col < CLS
    onehot = jnp.where(col == label, 1.0, 0.0)
    masked = jnp.where(is_logit, out, -jnp.inf)
    top = jnp.max(masked, axis=1, keepdims=True)
    shifted = jnp.exp(masked - top)
    total = jnp.sum(shifted, axis=1, keepdims=True)
    row_loss = valid * (jnp.log(total) + top - jnp.sum(onehot * out, axis=1, keepdims=True))
    scale = 1.0 / kept
    grad = (shifted / total - onehot) * (valid * scale)
    base = CLS + 4 * (label - 1)
    for j in range(4):
        mark = (col == base + j) & (col >= CLS)
        err = jnp.sum(jnp.where(mark, out, 0.0), axis=1, keepdims=True) - targets[:, j : j + 1]
        size = jnp.abs(err)
        row_loss += fore * jnp.where(size < 1.0, 0.5 * err * err, size - 0.5)
        grad += jnp.where(mark, jnp.clip(err, -1.0, 1.0) * (fore * scale), 0.0)
    return row_loss, grad


def head_blocks_kernel(share, depth, table, *refs):
    stacks, (pre_own, pre_sib, biases, labels, crowd, targets) = refs[: 2 * depth], refs[2 * depth : 2 * depth + 6]
    g_outs, gw2_outs, gwh_outs = refs[2 * depth + 6 : 2 * depth + 8], refs[2 * depth + 8 : 2 * depth + 10], refs[
        2 * depth + 10 : 2 * depth + 12
    ]
    sums, kept_out, small, w2, wh, pre1, h1, pre2, gpre2, gwh, g, gw2, gwhs, bias, in_sems, out_sems = refs[2 * depth + 12 :]
    rows, units = pre_own.shape
    blocks, xs, half, _ = small.shape[1:]
    count = depth * xs
    each = HID // (count * blocks * CORES)
    copies = [
        pltpu.make_async_copy(ref.at[:, :, pl.ds(ref.shape[2] - half, half)], small.at[n], in_sems.at[n])
        for n, ref in enumerate(stacks)
    ]
    for copy in copies:
        copy.start()
    core = table[2 * count + 1]
    for side, pre in enumerate((pre_own, pre_sib)):
        for k in range(blocks):
            unit = table[2 * count + 2 + side * blocks + k]
            lanes = slice(side * units + k * share, side * units + (k + 1) * share)
            first_bias = biases[:, pl.ds(pl.multiple_of(unit * share, share), share)]
            pre1[:, lanes] = pre[:, k * share : (k + 1) * share] + first_bias
        lanes = slice(side * units, (side + 1) * units)
        h1[:, lanes] = gelu(pre1[:, lanes]).astype(bf16)
    for copy in copies:
        copy.wait()
    for n in range(count):
        at = table[n]
        lanes = pl.ds(pl.multiple_of(at * 128, 128), 128)
        for y in range(blocks):
            turned = lax.rem(table[2 * count] + blocks - y, blocks)
            for side in range(CORES):

                def piece(begin, end):
                    rows_at, lanes_at = small_place(half, begin, end)
                    return small[side * depth + n // xs, y, n % xs, rows_at, lanes_at]

                for begin, end in ((0, min(share, half)), (half, share)):
                    if begin < end:
                        w2[side, y * share + begin : y * share + end, lanes] = piece(begin, end)
                owner = core if side == 0 else 1 - core
                to = pl.multiple_of(((at * blocks + turned) * CORES + owner) * each, each)
                for k in range(HEADP // 128):
                    wh[pl.ds(to, each), k * 128 : (k + 1) * 128] = piece(share + k * each, share + (k + 1) * each)
    bias[...] = jnp.zeros_like(bias)
    bias[:, :HEAD] = biases[:, 2 * HID :]
    pre2[...] = jnp.zeros_like(pre2) + biases[:, HID : 2 * HID]
    for side in range(CORES):
        for k in range(0, units, share):
            part = dot(h1[:, side * units + k : side * units + k + share], w2[side, k : k + share, :])
            pre2[...] += part.astype(bf16).astype(f32)
    h2 = gelu(pre2[...]).astype(bf16)
    out = dot(h2, wh[...]) + bias[...]
    flags = jnp.concatenate([labels[...], crowd[...]], axis=0).astype(f32)
    flags = jnp.concatenate([flags, targets[...].astype(f32), jnp.zeros((2, rows), f32)], axis=0)
    flags = jnp.transpose(flags)
    kept = kept_count(wh)
    kept_out[...] = kept
    row_loss, grad = losses(out, flags[:, 0:1].astype(jnp.int32), 1.0 - flags[:, 1:2], flags[:, 2:6], kept)
    g_out = grad.astype(bf16)
    g_h2 = dot(g_out, wh[...], ((1,), (1,)))
    g2 = (g_h2 * gelu_slope(pre2[...])).astype(bf16)
    gpre2[...] = g2
    sums[:, HID : 2 * HID] = jnp.sum(g2.astype(f32), axis=0, keepdims=True)
    sent = []
    for side in (1, 0):
        lanes = slice(side * units, (side + 1) * units)
        g_h1 = dot(gpre2[...], w2[side], ((1,), (1,)))
        g[side] = (g_h1 * gelu_slope(pre1[:, lanes])).astype(bf16)
        sent.append(pltpu.make_async_copy(g.at[side], g_outs[side], out_sems.at[side]))
        sent[-1].start()
    for side in (1, 0):
        lanes = slice(side * units, (side + 1) * units)
        gw2[side] = dot(h1[:, lanes], gpre2[...], ((0,), (0,))).astype(bf16)
        sent.append(pltpu.make_async_copy(gw2.at[side], gw2_outs[side], out_sems.at[CORES + side]))
        sent[-1].start()
    gwh[...] = dot(h2, g_out, ((0,), (0,)))
    for n in range(count * blocks):
        for side in (1, 0):
            owner = core if side == 0 else 1 - core
            row = pl.multiple_of((n * CORES + owner) * each, each)
            gwhs[side, n * each : (n + 1) * each, :] = gwh[pl.ds(row, each), :].astype(bf16)
    for side in (1, 0):
        sent.append(pltpu.make_async_copy(gwhs.at[side], gwh_outs[side], out_sems.at[2 * CORES + side]))
        sent[-1].start()
    for side in range(CORES):
        columns = jnp.sum(g[side].astype(f32), axis=0, keepdims=True)
        for k in range(blocks):
            unit = table[2 * count + 2 + side * blocks + k]
            sums[:, pl.ds(pl.multiple_of(unit * share, share), share)] = columns[:, k * share : (k + 1) * share]
    head_sums = jnp.sum(g_out.astype(f32), axis=0, keepdims=True)
    lane = lax.broadcasted_iota(jnp.int32, head_sums.shape, 1)
    loss = jnp.sum(row_loss, axis=0, keepdims=True)
    sums[:, 2 * HID : 2 * HID + HEADP] = jnp.where(lane == HEAD, loss, head_sums)
    for copy in sent:
        copy.wait()


def heads_blocks(share, half, table, own, sib, pre_own, pre_sib, biases, labels, crowd, targets):
    rows, units = pre_own.shape
    depth = len(own)
    blocks, xs, _, cols = own[0].shape
    smem = pl.BlockSpec(memory_space=pltpu.SMEM)
    vmem = pl.BlockSpec(memory_space=pltpu.VMEM)
    away = pl.BlockSpec(memory_space=pl.ANY)
    shape = jax.ShapeDtypeStruct
    return pl.pallas_call(
        functools.partial(head_blocks_kernel, share, depth),
        in_specs=[smem] + [away] * (2 * depth) + [vmem] * 6,
        out_specs=[away] * 6 + [vmem] * 2,
        out_shape=[shape((rows, units), bf16)] * 2
        + [shape((units, HID), bf16)] * 2
        + [shape((HID // CORES, HEADP), bf16)] * 2
        + [shape((1, 2 * HID + HEADP), f32), shape((1, 1), f32)],
        scratch_shapes=[
            pltpu.VMEM((2 * depth, blocks, xs, half, cols), bf16),
            pltpu.VMEM((CORES, units, HID), bf16),
            pltpu.VMEM((HID, HEADP), bf16),
            pltpu.VMEM((rows, HID), f32),
            pltpu.VMEM((rows, HID), bf16),
            pltpu.VMEM((rows, HID), f32),
            pltpu.VMEM((rows, HID), bf16),
            pltpu.VMEM((HID, HEADP), f32),
            pltpu.VMEM((CORES, rows, units), bf16),
            pltpu.VMEM((CORES, units, HID), bf16),
            pltpu.VMEM((CORES, HID // CORES, HEADP), bf16),
            pltpu.VMEM((1, HEADP), f32),
            pltpu.SemaphoreType.DMA((2 * depth,)),
            pltpu.SemaphoreType.DMA((3 * CORES,)),
        ],
        compiler_params=pltpu.CompilerParams(vmem_limit_bytes=WIDE * MIB),
        cost_estimate=LIGHT,
        name="heads",
    )(table, *own, *sib, pre_own, pre_sib, biases, labels, crowd, targets)


def head_kernel(
    share,
    wide,
    at_ref,
    pre_own,
    pre_sib,
    w2_own,
    w2_sib,
    wh,
    b1,
    b2,
    bh,
    tags,
    g_own,
    g_sib,
    gw2_own,
    gw2_sib,
    gwh_own,
    gwh_sib,
    sums,
    count,
    h1,
    pre2,
    gpre2,
    gwh,
):
    rows, units = pre_own.shape
    sides = ((pre_own, w2_own, g_own, gw2_own, 0), (pre_sib, w2_sib, g_sib, gw2_sib, units))
    pre2[...] = jnp.zeros_like(pre2) + b2[...]
    for pre, w2, _, _, at in sides:
        h1[:, at : at + units] = gelu(pre[...] + b1[:, at : at + units]).astype(bf16)
        for k in range(0, units, share):
            part = dot(h1[:, at + k : at + k + share], w2[k : k + share, :])
            pre2[...] += part.astype(bf16).astype(f32)
    h2 = gelu(pre2[...]).astype(bf16)
    out = dot(h2, wh[...]) + bh[...]
    label = tags[:, 4:5].astype(jnp.int32)
    kept = kept_count(wh)
    count[...] = kept
    row_loss, grad = losses(out, label, 1.0 - tags[:, 5:6], tags[:, :4], kept)
    g_out = grad.astype(bf16)
    head_sums = jnp.sum(g_out.astype(f32), axis=0, keepdims=True)
    lane = lax.broadcasted_iota(jnp.int32, head_sums.shape, 1)
    loss = jnp.sum(row_loss, axis=0, keepdims=True)
    sums[:, 2 * HID : 2 * HID + HEADP] = jnp.where(lane == HEAD, loss, head_sums)
    gwh[...] = dot(h2, g_out, ((0,), (0,)))
    each = HID // (HID // share * wide)
    for side in range(CORES):

        @pl.when(at_ref[HID // share] == side)
        def _(side=side):
            for n in range(HID // each // CORES):
                for c, part in ((side, gwh_own), (1 - side, gwh_sib)):
                    row = (n * CORES + c) * each
                    part[n * each : (n + 1) * each, :] = gwh[row : row + each, :].astype(bf16)

    g_h2 = dot(g_out, wh[...], ((1,), (1,)))
    g2 = (g_h2 * gelu_slope(pre2[...])).astype(bf16)
    sums[:, HID : 2 * HID] = jnp.sum(g2.astype(f32), axis=0, keepdims=True)
    gpre2[...] = g2
    for n, (pre, w2, g1, gw2, at) in enumerate(sides):
        g_h1 = dot(gpre2[...], w2[...], ((1,), (1,)))
        g = (g_h1 * gelu_slope(pre[...] + b1[:, at : at + units])).astype(bf16)
        g1[...] = g
        columns = jnp.sum(g.astype(f32), axis=0, keepdims=True)
        for k in range(units // share):
            to = pl.multiple_of(at_ref[n * (units // share) + k] * share, share)
            sums[:, pl.ds(to, share)] = columns[:, k * share : (k + 1) * share]
        gw2[...] = dot(h1[:, at : at + units], gpre2[...], ((0,), (0,))).astype(gw2.dtype)


def heads_step(share, wide, at, pre_own, pre_sib, w2_own, w2_sib, wh, b1, b2, bh, tags):
    rows, units = pre_own.shape
    vmem = pl.BlockSpec(memory_space=pltpu.VMEM)
    shape = jax.ShapeDtypeStruct
    return pl.pallas_call(
        functools.partial(head_kernel, share, wide),
        in_specs=[pl.BlockSpec(memory_space=pltpu.SMEM)] + [vmem] * 9,
        out_specs=[vmem] * 8,
        out_shape=[
            shape((rows, units), bf16),
            shape((rows, units), bf16),
            shape((units, HID), bf16),
            shape((units, HID), bf16),
            shape((HID // CORES, HEADP), bf16),
            shape((HID // CORES, HEADP), bf16),
            shape((1, 2 * HID + HEADP), f32),
            shape((1, 1), f32),
        ],
        scratch_shapes=[
            pltpu.VMEM((rows, HID), bf16),
            pltpu.VMEM((rows, HID), f32),
            pltpu.VMEM((rows, HID), bf16),
            pltpu.VMEM((HID, HEADP), f32),
        ],
        compiler_params=pltpu.CompilerParams(vmem_limit_bytes=WIDE * MIB),
        cost_estimate=LIGHT,
        name="heads",
    )(at, pre_own, pre_sib, w2_own, w2_sib, wh, b1, b2, bh, tags)


class Grid:
    def __init__(self):
        self.wide = lax.axis_size("wide")
        self.tp = lax.axis_size("tp")
        self.y = self.tp // CORES
        self.x = self.y if self.wide % self.y == 0 else 1
        self.z = self.wide // self.x
        self.size = {"z": self.z, "x": self.x, "y": self.y, "c": CORES}
        wide, tp = lax.axis_index("wide"), lax.axis_index("tp")
        self.at = {"z": wide // self.x, "x": wide % self.x, "y": tp // CORES, "c": tp % CORES}

    def move(self, value, axis, by):
        pairs = []
        for z in range(self.z):
            for x in range(self.x):
                for y in range(self.y):
                    for c in range(CORES):
                        to = {"z": z, "x": x, "y": y, "c": c}
                        for a in axis:
                            to[a] = (to[a] + by) % self.size[a]
                        pairs.append((self.index(z, x, y, c), self.index(to["z"], to["x"], to["y"], to["c"])))
        return lax.ppermute(value, AXES, pairs)

    def flip(self, value, axis, bit):
        unit = {"c": 1, "y": CORES, "x": CORES * self.y, "z": CORES * self.y * self.x}
        step = bit * sum(unit[a] for a in axis)
        return lax.ppermute(value, AXES, [(i, i ^ step) for i in range(self.wide * self.tp)])

    def index(self, z, x, y, c):
        return ((z * self.x + x) * self.y + y) * CORES + c

    def swap(self, value):
        return self.move(value, "c", 1)


def spread_stacked(grid, value, order):
    stack = value[None, None, None]
    for axis in order:
        place = "zxy".index(axis)
        stack = jnp.concatenate([stack] + [grid.move(stack, axis, by) for by in range(1, grid.size[axis])], axis=place)
    for place, axis in enumerate("zxy"):
        if grid.size[axis] > 1:
            back = (grid.at[axis] - jnp.arange(grid.size[axis])) % grid.size[axis]
            stack = jnp.take(stack, back, axis=place, mode="clip")
    return stack


def collect_stacked(grid, stack, order):
    left = "zxy"
    total = stack
    for axis in order:
        place = left.index(axis)
        total = total.astype(bf16)

        def block(by):
            at = (grid.at[axis] + by) % grid.size[axis]
            return lax.dynamic_index_in_dim(total, at, place, keepdims=False)

        mine = block(0).astype(f32)
        for by in range(1, grid.size[axis]):
            mine = mine + grid.move(block(by), axis, by).astype(f32)
        total = mine
        left = left.replace(axis, "")
    return total


def all_sum(value):
    count = lax.axis_size("wide") * lax.axis_size("tp")
    if count & (count - 1):
        return lax.psum(value, AXES)
    bit = 1
    while bit < count:
        value = value + lax.ppermute(value, AXES, [(i, i ^ bit) for i in range(count)])
        bit *= 2
    return value


def after(value, *others):
    return lax.optimization_barrier((value, *others))[0]


class Links:
    def __init__(self, grid, in_step):
        self.grid = grid
        self.in_step = in_step
        self.last = {}
        self.slots = [{}, {}]

    def next(self):
        self.slots.append({})

    def send(self, value, axis, by=1):
        before = [self.slots[-2]["x"]] if self.in_step and axis == "z" and "x" in self.slots[-2] else []
        if axis in self.last:
            before.append(self.last[axis])
        sent = self.grid.move(after(value, *before) if before else value, axis, by)
        self.last[axis] = self.slots[-1][axis] = sent
        return sent


def adam_update(weight, grad, first, second, rate):
    first_new = decay_one * first + (1.0 - decay_one) * grad
    second_new = decay_two * second + (1.0 - decay_two) * grad * grad
    first_hat = first_new / (1.0 - decay_one**STEP)
    second_hat = second_new / (1.0 - decay_two**STEP)
    weight_new = weight - rate * (first_hat / (jnp.sqrt(second_hat) + epsilon) + weight_decay * weight)
    return (weight_new, first_new, second_new)


def by_blocks(grid, feats, cols, share, second_cols, head_rows, channels, rows):
    return (
        (grid.z, grid.x, grid.y) == (4, 2, 2)
        and feats % 16 == 0
        and feats > max(LATE_OUT, LATE_BACK)
        and cols == channels == 256
        and second_cols == 128
        and (share, head_rows) == (256, 32)
        and rows % (CHUNKS * GROUP) == 0
        and block_span(feats, grid.wide, channels) > 0
    )


def place_table(grid):
    found = []
    for sign in (-1, 1):
        for dz in range(grid.z):
            for dx in range(grid.x):
                z, x = (grid.at["z"] + sign * dz) % grid.z, (grid.at["x"] + sign * dx) % grid.x
                found.append(z * grid.x + x)
    y, core = grid.at["y"], grid.at["c"]
    found += [y, core]
    found += [CORES * ((y + k) % grid.y) + c for c in (core, 1 - core) for k in range(grid.y)]
    return jnp.stack(found).astype(jnp.int32)


def low_sum(first, *others):
    total = first.astype(f32)
    for value in others:
        total = total + value.astype(f32)
    return total.astype(bf16)


def terms(value):
    found = []
    for _ in range(TERMS):
        found.append(lax.optimization_barrier(value.astype(bf16)))
        value = value - found[-1].astype(f32)
    return jnp.concatenate(found, axis=0)


def from_terms(rows):
    count = rows.shape[0] // TERMS
    total = rows[:count].astype(f32)
    for k in range(1, TERMS):
        total = total + rows[k * count : (k + 1) * count].astype(f32)
    return total


def blocks_step(grid, make_crops, w_first, w_second, w_heads, biases, labels, crowd, targets):
    feats, cols = w_first.shape
    share, _ = w_second.shape
    head_rows = w_heads.shape[0]
    table = place_table(grid)
    count = grid.z * grid.x

    links = Links(grid, True)
    most = feats - LATE_OUT
    mine, first_low = prepare(w_first, w_second, w_heads, crowd, most)
    half = mine.shape[0] - feats
    m = {(0, 0, 0): mine}
    stacks = {}

    m[0, 1, 0] = grid.move(mine, "x", 1)
    m[0, 0, 1] = grid.move(mine, "y", 1)
    m[1, 0, 0] = grid.move(first_low, "z", 1)
    own_crops = [make_crops(i) for i in range(CHUNKS)]
    made = own_crops[:EARLY] + [m[key] for key in ((0, 1, 0), (0, 0, 1), (1, 0, 0))]
    m[3, 0, 0] = links.send(after(first_low, *made), "z", 3)
    m[1, 1, 0] = links.send(after(m[1, 0, 0], *made), "x")
    m[0, 1, 1] = links.send(after(m[0, 1, 0], *made), "y")
    stacks[0] = jnp.stack([jnp.stack([m[0, x, y][most:] for x in range(grid.x)]) for y in range(grid.y)])
    links.next()
    m[2, 0, 0] = links.send(m[1, 0, 0], "z", 1)
    m[3, 1, 0] = links.send(m[3, 0, 0], "x")
    m[1, 0, 1] = links.send(m[1, 0, 0], "y")
    links.next()
    stacks[1] = links.send(stacks[0], "z", 1)
    m[2, 1, 0] = links.send(m[2, 0, 0], "x")
    m[3, 0, 1] = links.send(m[3, 0, 0], "y")
    links.next()
    stacks[3] = links.send(stacks[0], "z", 3)
    m[1, 1, 1] = links.send(m[1, 0, 1], "x")
    m[2, 0, 1] = links.send(m[2, 0, 0], "y")
    links.next()
    stacks[2] = links.send(stacks[1], "z", 1)
    m[3, 1, 1] = links.send(m[3, 0, 1], "x")
    m[2, 1, 1] = links.send(m[2, 1, 0], "y")
    sib_crops = []
    for chunk in own_crops:
        sib_crops.append(grid.swap(after(chunk, *made)))
    crops = own_crops + sib_crops

    span = block_span(feats, grid.wide, cols)
    both = (0, 1)

    def products(work, before):
        inputs = []
        for dz, dx, ys, kind in work:
            inputs += [m[dz, dx, y] for y in ys if kind != "last"] + [stacks[dz]] * (kind != "most")
        items = tuple((dz * grid.x + dx, dx, ys, kind) for dz, dx, ys, kind in work)
        return first_blocks(table, crops, inputs, items, feats, most, grid.wide, grid.y, before)

    work = [(dz, dx, both, "all") for dz, dx in ((0, 0), (0, 1), (1, 0), (3, 0), (1, 1))]
    first_pre = products(work + [(3, 1, (0,), "all"), (2, 0, both, "most"), (2, 1, (0,), "most")], None)
    work = [(2, 0, both, "last"), (2, 1, both, "last"), (2, 1, (1,), "most"), (3, 1, (1,), "all")]
    pre = products(work, first_pre)
    sib_stacks = {2: grid.swap(after(stacks[2], first_pre[0]))}
    sib_stacks[0] = grid.swap(stacks[0])
    sib_stacks[1] = grid.swap(after(stacks[1], sib_stacks[0]))
    sib_stacks[3] = grid.swap(after(stacks[3], sib_stacks[1], first_pre[0]))
    g_own, g_send, gw2, gw2_send, gwh, gwh_send, sums, roi_count = heads_blocks(
        share,
        half,
        table,
        [stacks[z] for z in range(4)],
        [sib_stacks[z] for z in range(4)],
        pre[0],
        grid.swap(pre[1]),
        biases[None, :],
        labels[None, :],
        crowd[None, :],
        targets.T,
    )

    g_got = grid.swap(g_send)
    m = {}
    parts = {}

    def gradients(keys, wait=()):
        numbers = tuple(count + dz * grid.x + dx for dz, dx in keys)
        outs = first_grad_blocks(after(table, *wait), numbers, crops, g_own, g_got, feats, LATE_BACK, grid.y, span)
        for i, (dz, dx) in enumerate(keys):
            for y in range(grid.y):
                m[dz, dx, y], parts[dz, dx, y] = outs[(i * grid.y + y) * 2 : (i * grid.y + y) * 2 + 2]

    gradients([(2, 1), (2, 0), (3, 1), (3, 0)])
    lates = [parts[dz, dx, y] for dz in (2, 3) for y in range(grid.y) for dx in range(grid.x)]
    packed = pack(
        table,
        lates,
        (gw2, grid.swap(after(gw2_send, g_got))),
        (gwh, grid.swap(after(gwh_send, g_got))),
        sums,
        half,
        (grid.y, grid.x),
    )

    def stack_of(dz):
        if dz >= 2:
            return packed[dz - 2]
        first = jnp.stack([jnp.stack([parts[dz, dx, y] for dx in range(grid.x)]) for y in range(grid.y)])
        return jnp.concatenate([first, packed[2][dz]], axis=2)

    links = Links(grid, False)
    far = stack_of(2)
    gradients([(1, 1), (1, 0), (0, 1), (0, 0)], [far])
    begun = (far, m[3, 1, 1])
    z0 = links.send(after(far, *begun[1:]), "z", 1)
    y0 = links.send(after(m[2, 1, 1], *begun), "y")
    x0 = links.send(after(m[3, 1, 1], *begun[:1]), "x")
    z1 = links.send(stack_of(3), "z", 3)
    y1 = links.send(m[2, 0, 1], "y")
    x1 = links.send(m[3, 1, 0], "x")
    z2 = links.send(low_sum(stack_of(1), z0), "z", 1)
    x2 = links.send(low_sum(m[2, 1, 0], y0), "x")
    y2 = links.send(low_sum(m[3, 0, 1], x0), "y")
    z3 = links.send(low_sum(m[2, 0, 0], x2, y1), "z", 1)
    x3 = links.send(m[1, 1, 1], "x")
    y3 = links.send(m[0, 1, 1], "y")
    z4 = links.send(low_sum(m[3, 0, 0], x1, y2), "z", 3)
    x4 = links.send(m[1, 1, 0], "x")
    y4 = links.send(low_sum(m[1, 0, 1], x3), "y")

    def extra_rows(stack):
        rows = stack[:, :, -EXTRA : 8 - EXTRA].reshape(-1, cols)
        return from_terms(rows[: TERMS * (sums.shape[1] // cols)])

    odd = grid.at["z"] % 2 == 1
    below, above, opposite = extra_rows(z0), extra_rows(z1), extra_rows(z2)
    total = sums.reshape(-1, cols)
    total = (total + jnp.where(odd, below, above)) + (opposite + jnp.where(odd, above, below))
    extra = TERMS * total.shape[0]
    late = low_sum(stack_of(0), z1, z2)
    x5 = links.send(jnp.concatenate([late[:, 1].reshape(-1, cols), terms(total)], axis=0), "x")
    x6 = links.send(low_sum(m[0, 1, 0], y3), "x")
    z5 = links.send(low_sum(m[1, 0, 0], x4, y4, z3), "z", 1)
    y5 = links.send(m[0, 0, 1], "y")
    total = total + from_terms(x5[-extra:])
    late = low_sum(late[:, 0], x5[:-extra].reshape(late[:, 0].shape))
    y6 = links.send(jnp.concatenate([late[1], terms(total)], axis=0), "y")
    total = total + from_terms(y6[-extra:])
    total = total + grid.swap(total)
    sums = total.reshape(1, -1)
    main = m[0, 0, 0].astype(f32)
    for value in (x6, y5, z4, z5):
        main = main + value.astype(f32)
    late = late[0].astype(f32) + y6[:-extra].astype(f32)

    first_total = jnp.concatenate([main, late[:LATE_BACK]], axis=0)
    late = late[LATE_BACK : LATE_BACK + half]
    total = jnp.concatenate([late[:, :128], late[:, 128:]], axis=0)
    heads_total = jnp.concatenate(
        [total[share + k * head_rows : share + (k + 1) * head_rows] for k in range(HEADP // 128)], axis=1
    )[:, :HEAD]
    return roi_count.reshape(()), sums, first_total, total[:share], heads_total


def stacked_step(grid, make_crops, w_first, w_second, w_heads, biases, labels, crowd, targets):
    tags = jnp.concatenate(
        [targets.astype(f32), labels[:, None].astype(f32), crowd[:, None].astype(f32)], axis=1
    )
    feats, cols = w_first.shape
    share, second_cols = w_second.shape
    head_rows = w_heads.shape[0]
    units = HID // CORES
    core = grid.at["c"]
    kept = jnp.sum(1 - crowd)
    head_block = jnp.pad(w_heads, ((0, 0), (0, HEADP - HEAD)))
    spot = (lax.broadcasted_iota(jnp.int32, head_block.shape, 0) == 0) * 1
    lane = lax.broadcasted_iota(jnp.int32, head_block.shape, 1)
    head_block = head_block + (
        spot * (jnp.where(lane == HEADP - 1, kept % 128, 0) + jnp.where(lane == HEADP - 2, kept // 128, 0))
    ).astype(f32)
    small = jnp.concatenate(
        [w_second.astype(bf16).reshape(-1, cols), head_block.astype(bf16).reshape(-1, cols)], axis=0
    )
    second_rows = share * second_cols // cols
    small_all = spread_stacked(grid, small, "zxy").reshape(grid.wide, grid.y, *small.shape)
    weight = spread_stacked(grid, w_first.astype(bf16), "zxy")
    weight = weight.transpose(2, 0, 1, 3, 4).reshape(grid.y, grid.wide * feats, cols)
    crops = [make_crops(i) for i in range(CHUNKS)]
    crops = crops + [grid.swap(c) for c in crops]
    second_own = (
        small_all[:, :, :second_rows]
        .reshape(grid.wide, grid.y, share, second_cols)
        .transpose(1, 2, 0, 3)
        .reshape(units, HID)
    )
    heads_own = small_all[:, :, second_rows:].reshape(grid.wide, grid.y, head_rows, HEADP)
    heads_sib = grid.swap(heads_own)
    head_matrix = jnp.where(
        core == 0, jnp.stack([heads_own, heads_sib], axis=2), jnp.stack([heads_sib, heads_own], axis=2)
    ).reshape(HID, HEADP)
    bias = biases[:HID].reshape(grid.y, CORES, share)
    bias = jnp.where(core == 0, bias, bias[:, ::-1]).transpose(1, 0, 2).reshape(1, -1)
    pre_own, pre_send = first_layer(crops, weight)
    unit_at = [2 * y + c for c in (core, 1 - core) for y in range(grid.y)]
    g_own, g_send, gw2_own, gw2_send, gwh, gwh_send, sums, roi_count = heads_step(
        share,
        grid.wide,
        jnp.stack([jnp.asarray(v) for v in unit_at + [core]]).astype(jnp.int32),
        pre_own,
        grid.swap(pre_send),
        second_own,
        grid.swap(second_own),
        head_matrix,
        bias,
        biases[HID : 2 * HID].reshape(1, -1),
        jnp.pad(biases[2 * HID :], (0, HEADP - HEAD)).reshape(1, -1),
        tags,
    )
    grad = first_grad(crops, g_own, grid.swap(g_send), grid.y)
    grad = grad.reshape(grid.y, grid.wide, feats, cols).transpose(1, 0, 2, 3)
    first_total = collect_stacked(grid, grad.reshape(grid.z, grid.x, grid.y, feats, cols), "yxz")
    gw2 = gw2_own.astype(f32) + grid.swap(gw2_send).astype(f32)
    gwh = gwh.astype(f32) + grid.swap(gwh_send).astype(f32)
    gw2 = gw2.astype(bf16).reshape(grid.y, share, grid.wide, second_cols).transpose(2, 0, 1, 3)
    small_grad = jnp.concatenate(
        [
            gw2.reshape(grid.wide, grid.y, second_rows, cols),
            gwh.astype(bf16).reshape(grid.wide, grid.y, -1, cols),
        ],
        axis=2,
    ).reshape(grid.z, grid.x, grid.y, -1, cols)
    small_total = collect_stacked(grid, small_grad, "yxz")
    second_total = small_total[:second_rows].reshape(share, second_cols)
    heads_total = small_total[second_rows:].reshape(head_rows, HEADP)[:, :HEAD]
    sums = all_sum(sums)
    return roi_count.reshape(()), sums, first_total, second_total, heads_total


def shards(
    maps,
    roi_image,
    roi_level,
    roi_corner,
    roi_weights,
    crowd,
    labels,
    box_targets,
    w_first,
    m_first,
    v_first,
    w_second,
    m_second,
    v_second,
    w_heads,
    m_heads,
    v_heads,
    biases,
    bias_m,
    bias_v,
):
    grid = Grid()
    rows = crowd.shape[0]

    images, levels, height, width, channels = maps.shape
    base = ((roi_image * levels + roi_level) * height + roi_corner[:, 0]).astype(jnp.int32)
    col = roi_corner[:, 1].astype(jnp.int32)
    flat_maps = maps.reshape(images * levels * height, width, channels)
    padded = jnp.pad(roi_weights, ((0, 0), (0, 0), (0, 1), (0, 0)))
    row_w = padded[:, 0].reshape(rows * 8, WIN)
    col_w = padded[:, 1].reshape(rows * 8, WIN)
    step = rows // CHUNKS
    def make_crops(i, *wait):
        return window_crops(flat_maps, after(base, *wait) if wait else base, col, row_w, col_w, i * step, step)

    shapes = (*w_first.shape, *w_second.shape, w_heads.shape[0], channels, rows)
    run = blocks_step if by_blocks(grid, *shapes) else stacked_step
    roi_count, sums, first_total, second_total, heads_total = run(
        grid, make_crops, w_first, w_second, w_heads, biases, labels, crowd, box_targets
    )
    loss_total = sums[0, 2 * HID + HEAD]
    bias_grad = sums[0, : 2 * HID + HEAD]

    first_out = adam_update(w_first, first_total, m_first, v_first, rate_first)
    second_out = adam_update(w_second, second_total, m_second, v_second, rate_second)
    heads_out = adam_update(w_heads, heads_total, m_heads, v_heads, rate_heads)
    bias_out = adam_update(biases, bias_grad, bias_m, bias_v, rate_biases)
    return (loss_total, roi_count, *first_out, *second_out, *heads_out, *bias_out)


def solution(mesh):
    rows = P(("wide", "tp"))
    both = P("wide", "tp")
    turned = P("tp", "wide")
    return jax.shard_map(
        shards,
        mesh=mesh,
        in_specs=(rows,) * 8 + (both,) * 3 + (turned,) * 3 + (rows,) * 3 + (P(),) * 3,
        out_specs=(P(), P()) + (both,) * 3 + (turned,) * 3 + (rows,) * 3 + (P(),) * 3,
        check_vma=False,
    )
```

```python
import functools

import jax
import jax.numpy as jnp
import numpy as np
from jax import lax
from jax.experimental import pallas as pl
from jax.experimental.pallas import tpu as pltpu
from jax.sharding import PartitionSpec as P

HID = 1024
CLS = 81
POOL = 7
CELLS = POOL * POOL
WIN = 16
STEP = 10
HEAD = 401
HEADP = 512
CORES = 2
CHUNKS = 8
EARLY = 4
GROUP = 32
KSTEP = 7
LATE_OUT = 192
LATE_BACK = 208
TERMS = 3
EXTRA = 16
WIDE = 60
MIB = 2**20
LIGHT = pl.CostEstimate(flops=0, bytes_accessed=1024, transcendentals=0)

AXES = ("wide", "tp")
rate_first = 0.02
rate_second = 0.06
rate_heads = 0.06
rate_biases = 0.3
decay_one = 0.9
decay_two = 0.999
epsilon = 1e-08
weight_decay = 0.1
GELU_A = 0.7978845608028654
GELU_B = 0.044715

f32 = jnp.float32
bf16 = jnp.bfloat16


def dot(a, b, contract=((1,), (0,))):
    return lax.dot_general(a, b, (contract, ((), ())), preferred_element_type=f32)


def crop_kernel(first, base_ref, col_ref, maps_ref, wr_ref, wc_ref, rep_ref, tile_ref, *refs):
    out_ref, rows_s, cols_s, left, right = refs
    step = pl.program_id(0)
    lanes = rows_s.shape[1]
    halves = (left, right)
    rows_s[...] = dot(wr_ref[...], rep_ref[...])
    cols_s[...] = dot(wc_ref[...], tile_ref[...])

    def one(i, carry):
        r = first + step * GROUP + i
        at = pl.multiple_of(i * 8, 8)
        rows = rows_s[pl.ds(at, 8), :]
        x0 = col_ref[r]
        cols = jnp.concatenate(
            [pltpu.roll(cols_s[pl.ds(at, 8), k : k + 128], x0, 1) for k in range(0, lanes, 128)], axis=1
        )
        both = jnp.concatenate([rows[a : a + 1, :] * cols for a in range(POOL)], axis=0)
        high = both.astype(bf16)
        low = (both - high.astype(f32)).astype(bf16)
        window = maps_ref[pl.ds(base_ref[r], WIN), :, :].reshape(lanes, maps_ref.shape[2])
        got = dot(jnp.concatenate([high, low], axis=0), window)
        got = got[: POOL * 8] + got[POOL * 8 :]
        for h, half in enumerate(halves):
            half[pl.ds(pl.multiple_of(i * POOL * 8, 8), POOL * 8), :] = got[:, h * 128 : (h + 1) * 128]
        return carry

    lax.fori_loop(0, GROUP, one, 0, unroll=8)
    for a in range(POOL):
        for b in range(POOL):
            for h, half in enumerate(halves):
                out_ref[a * POOL + b, :, h * 128 : (h + 1) * 128] = half[
                    pl.ds(a * 8 + b, GROUP, stride=POOL * 8), :
                ].astype(bf16)


def window_crops(maps, base, col, wr, wc, first, count):
    rows, width, channels = maps.shape
    lanes = WIN * width
    lane = np.arange(lanes)[None]
    unit = np.arange(WIN)[:, None]
    rep = jnp.asarray(lane // width == unit, bf16)
    til = jnp.asarray(lane % width == unit, bf16)
    return pl.pallas_call(
        functools.partial(crop_kernel, first),
        grid_spec=pltpu.PrefetchScalarGridSpec(
            num_scalar_prefetch=2,
            grid=(count // GROUP,),
            in_specs=[
                pl.BlockSpec(maps.shape, lambda i, *_: (0, 0, 0)),
                pl.BlockSpec((GROUP * 8, WIN), lambda i, *_: (first // GROUP + i, 0)),
                pl.BlockSpec((GROUP * 8, WIN), lambda i, *_: (first // GROUP + i, 0)),
                pl.BlockSpec(rep.shape, lambda i, *_: (0, 0)),
                pl.BlockSpec(til.shape, lambda i, *_: (0, 0)),
            ],
            out_specs=pl.BlockSpec((CELLS, GROUP, channels), lambda i, *_: (0, i, 0)),
            scratch_shapes=[
                pltpu.VMEM((GROUP * 8, lanes), f32),
                pltpu.VMEM((GROUP * 8, lanes), f32),
                pltpu.VMEM((GROUP * POOL * 8, 128), f32),
                pltpu.VMEM((GROUP * POOL * 8, 128), f32),
            ],
        ),
        out_shape=jax.ShapeDtypeStruct((CELLS, count, channels), bf16),
        compiler_params=pltpu.CompilerParams(vmem_limit_bytes=18 * MIB),
        cost_estimate=LIGHT,
        name="crops",
    )(base, col, maps, wr, wc, rep, til)


def first_kernel(parts, *refs):
    crops, weight, own, send = refs[:parts], refs[parts], refs[parts + 1], refs[parts + 2]
    step = pl.program_id(0)
    blocks, depth, cols = weight.shape
    channels = crops[0].shape[2]

    @pl.when(step == 0)
    def _():
        own[...] = jnp.zeros_like(own)
        send[...] = jnp.zeros_like(send)

    for out, refs_half in ((own, crops[: parts // 2]), (send, crops[parts // 2 :])):
        lhs = jnp.concatenate(
            [jnp.concatenate([ref[j] for ref in refs_half], axis=0) for j in range(depth // channels)], axis=1
        )
        for y in range(blocks):
            out[:, y * cols : (y + 1) * cols] += dot(lhs, weight[y])


def first_layer(crops, weight):
    parts = len(crops)
    blocks, feats, cols = weight.shape
    channels = crops[0].shape[2]
    rows = sum(c.shape[1] for c in crops) // 2
    return pl.pallas_call(
        functools.partial(first_kernel, parts),
        grid=(CELLS // KSTEP,),
        in_specs=[pl.BlockSpec((KSTEP,) + c.shape[1:], lambda i: (i, 0, 0)) for c in crops]
        + [pl.BlockSpec((blocks, KSTEP * channels, cols), lambda i: (0, i, 0))],
        out_specs=[pl.BlockSpec((rows, blocks * cols), lambda i: (0, 0))] * 2,
        out_shape=[jax.ShapeDtypeStruct((rows, blocks * cols), f32)] * 2,
        compiler_params=pltpu.CompilerParams(vmem_limit_bytes=60 * MIB),
        cost_estimate=LIGHT,
        name="first_layer",
    )(*crops, weight)


def first_grad_kernel(parts, cols, *refs):
    crops, own, got, out = refs[:parts], refs[parts], refs[parts + 1], refs[parts + 2]
    channels = crops[0].shape[2]
    grads = jnp.concatenate([own[...], got[...]], axis=0)
    for j in range(crops[0].shape[0]):
        lhs = jnp.concatenate([ref[j] for ref in crops], axis=0)
        res = dot(lhs, grads, ((0,), (0,))).astype(bf16)
        for y in range(out.shape[0]):
            out[y, j * channels : (j + 1) * channels, :] = res[:, y * cols : (y + 1) * cols]


def first_grad(crops, own, got, blocks):
    parts = len(crops)
    rows, units = own.shape
    cols = units // blocks
    channels = crops[0].shape[2]
    return pl.pallas_call(
        functools.partial(first_grad_kernel, parts, cols),
        grid=(CELLS // KSTEP,),
        in_specs=[pl.BlockSpec((KSTEP,) + c.shape[1:], lambda i: (i, 0, 0)) for c in crops]
        + [pl.BlockSpec((rows, units), lambda i: (0, 0))] * 2,
        out_specs=pl.BlockSpec((blocks, KSTEP * channels, cols), lambda i: (0, i, 0)),
        out_shape=jax.ShapeDtypeStruct((blocks, CELLS * channels, cols), bf16),
        compiler_params=pltpu.CompilerParams(vmem_limit_bytes=60 * MIB),
        cost_estimate=LIGHT,
        name="first_grad",
    )(*crops, own, got)


def block_span(feats, wide, channels):
    span = max(-(-((w * feats) % channels + feats) // channels) for w in range(wide))
    return span if all(w * feats // channels + span <= CELLS for w in range(wide)) else 0


def cell_copies(crops, start, span, cells, sems):
    found = []
    at = 0
    for n, ref in enumerate(crops):
        rows = ref.shape[1]
        found.append(pltpu.make_async_copy(ref.at[pl.ds(start, span)], cells.at[:, pl.ds(at, rows)], sems.at[n]))
        at += rows
    return found


def rows_of(kind, feats, most):
    return {"all": (0, feats), "most": (0, most), "last": (most, feats)}[kind]


def kind_span(kind, feats, most, wide, channels):
    begin, end = rows_of(kind, feats, most)
    return max(-(-((w * feats + begin) % channels + end - begin) // channels) for w in range(wide))


def block_kernel(items, feats, most, wide, parts, fresh, table, *refs):
    count = len(items)
    crops, rest = refs[:parts], refs[parts:]
    own, send, pad, cells, sems = rest[-5:]
    before, inputs = (None, rest[:-5]) if fresh else (rest[:2], rest[2:-5])
    step = pl.program_id(0)
    rows = own.shape[0]
    channels = cells.shape[3]
    cols = channels
    needs = [len(item[2]) * (item[3] != "last") + (item[3] != "most") for item in items]
    spans = [kind_span(item[3], feats, most, wide, channels) for item in items]

    def copies(i):
        slot = i % 2
        number, side, ys, kind = items[i]
        begin, end = rows_of(kind, feats, most)
        start = table[number] * feats + begin
        cell = jnp.minimum(start // channels, CELLS - spans[i])
        at = pl.multiple_of(start - cell * channels, 16)
        found = cell_copies(crops, cell, spans[i], cells.at[slot, pl.ds(0, spans[i])], sems.at[slot])
        group = inputs[sum(needs[:i]) : sum(needs[: i + 1])]
        for k, y in enumerate(ys):
            lanes = pl.ds(y * cols, cols)
            if kind != "last":
                source = group[k].at[pl.ds(0, most)]
                found.append(
                    pltpu.make_async_copy(source, pad.at[slot, pl.ds(at, most), lanes], sems.at[slot, parts + 2 * k])
                )
            if kind != "most":
                source = group[-1].at[y, side, pl.ds(0, feats - most)]
                to = pl.ds(pl.multiple_of(at + most - begin, 16), feats - most)
                found.append(pltpu.make_async_copy(source, pad.at[slot, to, lanes], sems.at[slot, parts + 1 + 2 * k]))
        return found

    def edges(i):
        begin, end = rows_of(items[i][3], feats, most)
        deep = spans[i] * channels
        low = (end - begin) // channels * channels
        lanes = pad.shape[2]
        if low:
            pad[i % 2, :channels, :] = jnp.zeros((channels, lanes), bf16)
        pad[i % 2, low:deep, :] = jnp.zeros((deep - low, lanes), bf16)

    @pl.when(step == 0)
    def _():
        edges(0)
        for copy in copies(0):
            copy.start()
        if fresh:
            own[...] = jnp.zeros_like(own)
            send[...] = jnp.zeros_like(send)
        else:
            own[...] = before[0][...]
            send[...] = before[1][...]

    for i in range(count):

        @pl.when(step == i)
        def _(i=i):
            if i + 1 < count:
                edges(i + 1)
                for copy in copies(i + 1):
                    copy.start()
            for copy in copies(i):
                copy.wait()

    slot = lax.rem(step, 2)
    forms = [(span, item[2]) for span, item in zip(spans, items)]
    for form in sorted(set(forms)):
        span, ys = form
        lanes = slice(ys[0] * cols, (ys[-1] + 1) * cols)

        @pl.when(functools.reduce(jnp.logical_or, [step == i for i in range(count) if forms[i] == form]))
        def _(span=span, lanes=lanes):
            lhs = jnp.concatenate([cells[slot, j] for j in range(span)], axis=1)
            got = dot(lhs, pad[slot, : span * channels, lanes])
            own[:, lanes] += got[:rows]
            send[:, lanes] += got[rows:]


def whole(shape):
    return pl.BlockSpec(shape, lambda i, place: (0,) * len(shape))


def first_blocks(table, crops, inputs, items, feats, most, wide, blocks, before):
    rows = sum(c.shape[1] for c in crops) // 2
    channels = crops[0].shape[2]
    units = blocks * channels
    lead = [] if before is None else list(before)
    away = pl.BlockSpec(memory_space=pl.ANY)
    parts = len(crops)
    span = kind_span("all", feats, most, wide, channels)
    return pl.pallas_call(
        functools.partial(block_kernel, items, feats, most, wide, parts, before is None),
        grid_spec=pltpu.PrefetchScalarGridSpec(
            num_scalar_prefetch=1,
            grid=(len(items),),
            in_specs=[away] * parts + [whole((rows, units))] * len(lead) + [away] * len(inputs),
            out_specs=[whole((rows, units))] * 2,
            scratch_shapes=[
                pltpu.VMEM((2, span * channels, units), bf16),
                pltpu.VMEM((2, span, 2 * rows, channels), bf16),
                pltpu.SemaphoreType.DMA((2, parts + 2 * blocks)),
            ],
        ),
        out_shape=[jax.ShapeDtypeStruct((rows, units), f32)] * 2,
        input_output_aliases={} if before is None else {1 + parts: 0, 2 + parts: 1},
        compiler_params=pltpu.CompilerParams(vmem_limit_bytes=WIDE * MIB),
        cost_estimate=LIGHT,
        name="first_blocks",
    )(table, *crops, *lead, *inputs)


def block_grad_kernel(span, numbers, feats, blocks, parts, table, *refs):
    crops, (own, got), rest = refs[:parts], refs[parts : parts + 2], refs[parts + 2 :]
    outs, (full, cells, in_sems, out_sems) = rest[:-4], rest[-4:]
    step = pl.program_id(0)
    count = len(outs) // (2 * blocks)
    channels = cells.shape[3]
    cols = full.shape[2] // blocks

    def loads(i):
        return cell_copies(crops, (table[numbers[i]] * feats) // channels, span, cells.at[i % 2], in_sems.at[i % 2])

    def stores(i):
        at = pl.multiple_of((table[numbers[i]] * feats) % channels, 16)
        found = []
        for y in range(blocks):
            main, late = outs[(i * blocks + y) * 2], outs[(i * blocks + y) * 2 + 1]
            most = main.shape[0]
            lanes = pl.ds(y * cols, cols)
            found.append(pltpu.make_async_copy(full.at[i % 2, pl.ds(at, most), lanes], main, out_sems.at[i % 2, 2 * y]))
            found.append(
                pltpu.make_async_copy(
                    full.at[i % 2, pl.ds(pl.multiple_of(at + most, 16), feats - most), lanes],
                    late,
                    out_sems.at[i % 2, 2 * y + 1],
                )
            )
        return found

    @pl.when(step == 0)
    def _():
        for copy in loads(0):
            copy.start()

    for i in range(count):

        @pl.when(step == i)
        def _(i=i):
            if i + 1 < count:
                for copy in loads(i + 1):
                    copy.start()
            for copy in loads(i):
                copy.wait()
            if i >= 2:
                for copy in stores(i - 2):
                    copy.wait()

    slot = lax.rem(step, 2)
    grads = jnp.concatenate([own[...], got[...]], axis=0)
    for j in range(span):
        full[slot, j * channels : (j + 1) * channels, :] = dot(cells[slot, j], grads, ((0,), (0,))).astype(bf16)

    for i in range(count):

        @pl.when(step == i)
        def _(i=i):
            for copy in stores(i):
                copy.start()
            if i == count - 1:
                for k in range(max(0, count - 2), count):
                    for copy in stores(k):
                        copy.wait()


def first_grad_blocks(table, numbers, crops, own, got, feats, late, blocks, span):
    rows, units = own.shape
    channels = crops[0].shape[2]
    cols = units // blocks
    count = len(numbers)
    parts = len(crops)
    outs = [(feats - late, cols), (late, cols)] * (count * blocks)
    away = pl.BlockSpec(memory_space=pl.ANY)
    return pl.pallas_call(
        functools.partial(block_grad_kernel, span, numbers, feats, blocks, parts),
        grid_spec=pltpu.PrefetchScalarGridSpec(
            num_scalar_prefetch=1,
            grid=(count,),
            in_specs=[away] * parts + [whole((rows, units))] * 2,
            out_specs=[away] * len(outs),
            scratch_shapes=[
                pltpu.VMEM((2, span * channels, units), bf16),
                pltpu.VMEM((2, span, 2 * rows, channels), bf16),
                pltpu.SemaphoreType.DMA((2, parts)),
                pltpu.SemaphoreType.DMA((2, 2 * blocks)),
            ],
        ),
        out_shape=[jax.ShapeDtypeStruct(v, bf16) for v in outs],
        compiler_params=pltpu.CompilerParams(vmem_limit_bytes=WIDE * MIB),
        cost_estimate=LIGHT,
        name="first_grad",
    )(table, *crops, own, got)


def small_place(half, begin, end):
    lane = 0 if end <= half else 128
    back = half if lane else 0
    return slice(begin - back, end - back), slice(lane, lane + 128)


def prepare_kernel(first, second, heads, crowd, mine, low, first_s, second_s, heads_s, crowd_s, wide_heads, low_s, in_sems, out_sems):
    feats = first.shape[0]
    share = second.shape[0]
    rows = heads.shape[0]
    half = mine.shape[0] - feats
    most = low.shape[0]
    cuts = [feats * k // 4 // 16 * 16 for k in range(4)] + [feats]
    loads = [
        pltpu.make_async_copy(first.at[pl.ds(a, b - a)], first_s.at[pl.ds(a, b - a)], in_sems.at[k])
        for k, (a, b) in enumerate(zip(cuts, cuts[1:]))
    ]
    others = [
        pltpu.make_async_copy(ref, to, in_sems.at[4 + k])
        for k, (ref, to) in enumerate(((second, second_s), (heads, heads_s), (crowd, crowd_s)))
    ]
    for copy in others + loads:
        copy.start()
    for copy in others:
        copy.wait()
    kept = jnp.sum(1 - crowd_s[...], axis=1, keepdims=True)
    wide_heads[...] = jnp.zeros_like(wide_heads)
    wide_heads[:, :HEAD] = heads_s[...]
    lane = lax.broadcasted_iota(jnp.int32, (rows, 128), 1)
    row = lax.broadcasted_iota(jnp.int32, (rows, 128), 0)
    marks = jnp.where(lane == 127, kept % 128, jnp.where(lane == 126, kept // 128, 0))
    wide_heads[:, HEADP - 128 :] += jnp.where(row == 0, marks, 0).astype(f32)
    for begin, end in ((0, min(share, half)), (half, share)):
        if begin < end:
            at, lanes = small_place(half, begin, end)
            low_s[feats + at.start : feats + at.stop, lanes] = second_s[begin:end, :].astype(bf16)
    for k in range(HEADP // 128):
        at, lanes = small_place(half, share + k * rows, share + (k + 1) * rows)
        low_s[feats + at.start : feats + at.stop, lanes] = wide_heads[:, k * 128 : (k + 1) * 128].astype(bf16)
    stores = []
    for k, (a, b) in enumerate(zip(cuts, cuts[1:])):
        loads[k].wait()
        low_s[a:b, :] = first_s[a:b, :].astype(bf16)
        end = mine.shape[0] if b == feats else b
        stores.append(pltpu.make_async_copy(low_s.at[pl.ds(a, end - a)], mine.at[pl.ds(a, end - a)], out_sems.at[k]))
        stores[-1].start()
    stores.append(pltpu.make_async_copy(low_s.at[pl.ds(0, most)], low, out_sems.at[4]))
    stores[-1].start()
    for copy in stores:
        copy.wait()


def prepare(first, second, heads, crowd, most):
    feats, cols = first.shape
    half = (second.shape[0] + heads.shape[0] * HEADP // 128) // 2
    away = pl.BlockSpec(memory_space=pl.ANY)
    crowd = crowd[None, :]
    return pl.pallas_call(
        prepare_kernel,
        in_specs=[away] * 4,
        out_specs=[away] * 2,
        out_shape=[jax.ShapeDtypeStruct((feats + half, cols), bf16), jax.ShapeDtypeStruct((most, cols), bf16)],
        scratch_shapes=[
            pltpu.VMEM(first.shape, f32),
            pltpu.VMEM(second.shape, f32),
            pltpu.VMEM(heads.shape, f32),
            pltpu.VMEM(crowd.shape, jnp.int32),
            pltpu.VMEM((heads.shape[0], HEADP), f32),
            pltpu.VMEM((feats + half, cols), bf16),
            pltpu.SemaphoreType.DMA((7,)),
            pltpu.SemaphoreType.DMA((5,)),
        ],
        cost_estimate=LIGHT,
        compiler_params=pltpu.CompilerParams(vmem_limit_bytes=WIDE * MIB),
        name="prepare",
    )(first, second, heads, crowd)


def pack_kernel(table, *refs):
    lates, sides, sums = refs[:8], refs[8:12], refs[12]
    stack_two, stack_three, near_out, near, far, gw2s, gwhs, late_sems, in_sems, small_sems = refs[13:]
    gw2, gw2_got, gwh, gwh_got = gw2s.at[0], gw2s.at[1], gwhs.at[0], gwhs.at[1]
    arrive = [
        pltpu.make_async_copy(ref, to, in_sems.at[n]) for n, (ref, to) in enumerate(zip(sides, (gw2, gw2_got, gwh, gwh_got)))
    ]
    for copy in arrive:
        copy.start()
    depth = near.shape[0] + far.shape[0]
    _, blocks, xs, tall, _ = near.shape
    half = tall - EXTRA
    share = gw2.shape[0] // blocks
    count = depth * xs
    rows = gwh.shape[0] // (count * blocks)
    long = lates[0].shape[0]
    stacks = (stack_two, stack_three)
    copies = []
    for d in range(2):
        for y in range(blocks):
            for x in range(xs):
                n = (d * blocks + y) * xs + x
                copies.append(pltpu.make_async_copy(lates[n], far.at[d, y, x, pl.ds(0, long)], late_sems.at[n]))
    for copy in copies:
        copy.start()
    rest = sums[...]
    rows_left = []
    for _ in range(TERMS):
        term = rest.astype(bf16).astype(f32)
        rest = rest - term
        rows_left += [term[:, k : k + 256] for k in range(0, term.shape[1], 256)]
    rows_left += [jnp.zeros_like(rows_left[0])] * (-len(rows_left) % (blocks * xs))
    each = len(rows_left) // (blocks * xs)
    for copy in arrive:
        copy.wait()
    for dz in (2, 3, 1, 0):
        out, at, skip = (far, dz - 2, long) if dz >= 2 else (near, dz, 0)
        for y in range(blocks):
            for x in range(xs):
                here = table[count + dz * xs + x]
                lanes = pl.ds(pl.multiple_of(here * 128, 128), 128)

                def small(begin, end, value):
                    rows_at, lanes_at = small_place(half, begin, end)
                    out[at, y, x, skip + rows_at.start : skip + rows_at.stop, lanes_at] = value.astype(bf16)

                turned = (blocks - y) % blocks
                for begin, end in ((0, min(share, half)), (half, share)):
                    if begin < end:
                        part = slice(turned * share + begin, turned * share + end)
                        small(begin, end, gw2[part, lanes].astype(f32) + gw2_got[part, lanes].astype(f32))
                ahead = lax.rem(table[2 * count] + y, blocks)
                block = pl.ds(pl.multiple_of((here * blocks + ahead) * rows, rows), rows)
                for k in range(HEADP // 128):
                    group = slice(k * 128, (k + 1) * 128)
                    value = gwh[block, group].astype(f32) + gwh_got[block, group].astype(f32)
                    small(share + k * rows, share + (k + 1) * rows, value)
                n = y * xs + x
                some = rows_left[n * each : (n + 1) * each] + [jnp.zeros_like(rows_left[0])] * (EXTRA - each)
                some = jnp.concatenate(some, axis=0).astype(bf16)
                out[at, y, x, skip + half :, :] = some if dz >= 2 else jnp.zeros_like(some)
        if dz >= 2:
            for copy in copies[at * blocks * xs : (at + 1) * blocks * xs]:
                copy.wait()
            pltpu.make_async_copy(far.at[at], stacks[at], small_sems.at[at]).start()
    last = pltpu.make_async_copy(near, near_out, small_sems.at[2])
    last.start()
    for at in range(2):
        pltpu.make_async_copy(far.at[at], stacks[at], small_sems.at[at]).wait()
    last.wait()


def pack(table, lates, gw2, gwh, sums, half, places):
    smem = pl.BlockSpec(memory_space=pltpu.SMEM)
    vmem = pl.BlockSpec(memory_space=pltpu.VMEM)
    away = pl.BlockSpec(memory_space=pl.ANY)
    long, cols = lates[0].shape
    tall = half + EXTRA
    stack = jax.ShapeDtypeStruct((*places, long + tall, cols), bf16)
    return pl.pallas_call(
        pack_kernel,
        in_specs=[smem] + [away] * (len(lates) + 4) + [vmem],
        out_specs=[away] * 3,
        out_shape=[stack, stack, jax.ShapeDtypeStruct((2, *places, tall, cols), bf16)],
        scratch_shapes=[
            pltpu.VMEM((2, *places, tall, cols), bf16),
            pltpu.VMEM((2, *places, long + tall, cols), bf16),
            pltpu.VMEM((2, *gw2[0].shape), bf16),
            pltpu.VMEM((2, *gwh[0].shape), bf16),
            pltpu.SemaphoreType.DMA((len(lates),)),
            pltpu.SemaphoreType.DMA((4,)),
            pltpu.SemaphoreType.DMA((3,)),
        ],
        cost_estimate=LIGHT,
        compiler_params=pltpu.CompilerParams(vmem_limit_bytes=WIDE * MIB),
        name="pack",
    )(table, *lates, *gw2, *gwh, sums)


def gelu(x):
    return 0.5 * x * (1.0 + jnp.tanh(GELU_A * (x + GELU_B * x * x * x)))


def gelu_slope(x):
    t = jnp.tanh(GELU_A * (x + GELU_B * x * x * x))
    return 0.5 * (1.0 + t) + 0.5 * x * (1.0 - t * t) * (GELU_A * (1.0 + 3.0 * GELU_B * x * x))


def kept_count(wh):
    ends = jnp.sum(wh[:, HEADP - 128 :].astype(f32), axis=0, keepdims=True)
    return 128.0 * ends[:, 126:127] + ends[:, 127:128]


def losses(out, flags, kept):
    rows, width = out.shape
    label = flags[:, 0:1].astype(jnp.int32)
    valid = 1.0 - flags[:, 1:2]
    fore = jnp.where(label > 0, valid, 0.0)
    scale = 1.0 / kept
    lane = lax.broadcasted_iota(jnp.int32, flags.shape, 1)
    onehot = jnp.where(lane == label, 1.0, 0.0)
    logits = out[:, : flags.shape[1]]
    masked = jnp.where(lane < CLS, logits, -jnp.inf)
    top = jnp.max(masked, axis=1, keepdims=True)
    shifted = jnp.exp(masked - top)
    total = jnp.sum(shifted, axis=1, keepdims=True)
    cross = jnp.log(total) + top - jnp.sum(onehot * logits, axis=1, keepdims=True)
    col = lax.broadcasted_iota(jnp.int32, out.shape, 1)
    base = CLS + 4 * (label - 1)
    row = jnp.where((col >= base) & (col < base + 4) & (col >= CLS), 1.0, 0.0)
    at = lax.broadcasted_iota(jnp.int32, (width, flags.shape[1]), 0) - CLS
    to = lax.broadcasted_iota(jnp.int32, (width, flags.shape[1]), 1) - 2
    bring = jnp.where((at >= 0) & (at < HEAD - CLS) & ((at & 3) == to), 1.0, 0.0)
    full = functools.partial(lax.dot_general, precision=lax.Precision.HIGHEST, preferred_element_type=f32)
    boxes = full(out * row, bring, (((1,), (0,)), ((), ())))
    error = jnp.where((lane >= 2) & (lane < 6), boxes - flags, 0.0)
    size = jnp.abs(error)
    smooth = jnp.sum(jnp.where(size < 1.0, 0.5 * error * error, size - 0.5 * jnp.where(size > 0.0, 1.0, 0.0)), axis=1, keepdims=True)
    back = full(jnp.clip(error, -1.0, 1.0) * (fore * scale), bring, (((1,), (1,)), ((), ())))
    grad = back * row
    first = (shifted / total - onehot) * (valid * scale) + grad[:, : flags.shape[1]]
    return valid * cross + fore * smooth, jnp.concatenate([first, grad[:, flags.shape[1] :]], axis=1)


def head_blocks_kernel(share, depth, table, *refs):
    stacks, (pre_own, pre_sib, biases, labels, crowd, targets) = refs[: 2 * depth], refs[2 * depth : 2 * depth + 6]
    g_outs, gw2_outs, gwh_outs = refs[2 * depth + 6 : 2 * depth + 8], refs[2 * depth + 8 : 2 * depth + 10], refs[
        2 * depth + 10 : 2 * depth + 12
    ]
    sums, kept_out, small, pres, w2, wh, pre1, h1, pre2, gpre2, gwh, g, gw2, gwhs, bias, in_sems, out_sems = refs[
        2 * depth + 12 :
    ]
    rows, units = pre_own.shape
    blocks, xs, half, _ = small.shape[1:]
    count = depth * xs
    each = HID // (count * blocks * CORES)
    copies = [
        pltpu.make_async_copy(ref.at[:, :, pl.ds(ref.shape[2] - half, half)], small.at[n], in_sems.at[n])
        for n, ref in enumerate(stacks)
    ]
    early = [pltpu.make_async_copy(ref, pres.at[n], in_sems.at[2 * depth + n]) for n, ref in enumerate((pre_own, pre_sib))]
    for copy in early + copies:
        copy.start()
    core = table[2 * count + 1]
    for copy in early:
        copy.wait()
    for side, pre in enumerate((pres.at[0], pres.at[1])):
        for k in range(blocks):
            unit = table[2 * count + 2 + side * blocks + k]
            lanes = slice(side * units + k * share, side * units + (k + 1) * share)
            first_bias = biases[:, pl.ds(pl.multiple_of(unit * share, share), share)]
            pre1[:, lanes] = pre[:, k * share : (k + 1) * share] + first_bias
        lanes = slice(side * units, (side + 1) * units)
        h1[:, lanes] = gelu(pre1[:, lanes]).astype(bf16)
    for copy in copies:
        copy.wait()
    for n in range(count):
        at = table[n]
        lanes = pl.ds(pl.multiple_of(at * 128, 128), 128)
        for y in range(blocks):
            turned = lax.rem(table[2 * count] + blocks - y, blocks)
            for side in range(CORES):

                def piece(begin, end):
                    rows_at, lanes_at = small_place(half, begin, end)
                    return small[side * depth + n // xs, y, n % xs, rows_at, lanes_at]

                for begin, end in ((0, min(share, half)), (half, share)):
                    if begin < end:
                        w2[side, y * share + begin : y * share + end, lanes] = piece(begin, end)
                owner = core if side == 0 else 1 - core
                to = pl.multiple_of(((at * blocks + turned) * CORES + owner) * each, each)
                for k in range(HEADP // 128):
                    wh[pl.ds(to, each), k * 128 : (k + 1) * 128] = piece(share + k * each, share + (k + 1) * each)
    bias[...] = jnp.zeros_like(bias)
    bias[:, :HEAD] = biases[:, 2 * HID :]
    pre2[...] = jnp.zeros_like(pre2) + biases[:, HID : 2 * HID]
    for side in range(CORES):
        for k in range(0, units, share):
            part = dot(h1[:, side * units + k : side * units + k + share], w2[side, k : k + share, :])
            pre2[...] += part.astype(bf16).astype(f32)
    h2 = gelu(pre2[...]).astype(bf16)
    out = dot(h2, wh[...]) + bias[...]
    flags = jnp.concatenate([labels[...], crowd[...]], axis=0).astype(f32)
    flags = jnp.concatenate([flags, targets[...].astype(f32), jnp.zeros((122, rows), f32)], axis=0)
    flags = jnp.transpose(flags)
    kept = kept_count(wh)
    kept_out[...] = kept
    row_loss, grad = losses(out, flags, kept)
    g_out = grad.astype(bf16)
    g_h2 = dot(g_out, wh[...], ((1,), (1,)))
    g2 = (g_h2 * gelu_slope(pre2[...])).astype(bf16)
    gpre2[...] = g2
    sums[:, HID : 2 * HID] = jnp.sum(g2.astype(f32), axis=0, keepdims=True)
    sent = []
    for side in (1, 0):
        lanes = slice(side * units, (side + 1) * units)
        g_h1 = dot(gpre2[...], w2[side], ((1,), (1,)))
        g[side] = (g_h1 * gelu_slope(pre1[:, lanes])).astype(bf16)
        sent.append(pltpu.make_async_copy(g.at[side], g_outs[side], out_sems.at[side]))
        sent[-1].start()
    for side in (1, 0):
        lanes = slice(side * units, (side + 1) * units)
        gw2[side] = dot(h1[:, lanes], gpre2[...], ((0,), (0,))).astype(bf16)
        sent.append(pltpu.make_async_copy(gw2.at[side], gw2_outs[side], out_sems.at[CORES + side]))
        sent[-1].start()
    gwh[...] = dot(h2, g_out, ((0,), (0,)))
    for n in range(count * blocks):
        for side in (1, 0):
            owner = core if side == 0 else 1 - core
            row = pl.multiple_of((n * CORES + owner) * each, each)
            gwhs[side, n * each : (n + 1) * each, :] = gwh[pl.ds(row, each), :].astype(bf16)
    for side in (1, 0):
        sent.append(pltpu.make_async_copy(gwhs.at[side], gwh_outs[side], out_sems.at[2 * CORES + side]))
        sent[-1].start()
    for side in range(CORES):
        columns = jnp.sum(g[side].astype(f32), axis=0, keepdims=True)
        for k in range(blocks):
            unit = table[2 * count + 2 + side * blocks + k]
            sums[:, pl.ds(pl.multiple_of(unit * share, share), share)] = columns[:, k * share : (k + 1) * share]
    head_sums = jnp.sum(g_out.astype(f32), axis=0, keepdims=True)
    lane = lax.broadcasted_iota(jnp.int32, head_sums.shape, 1)
    loss = jnp.sum(row_loss, axis=0, keepdims=True)
    sums[:, 2 * HID : 2 * HID + HEADP] = jnp.where(lane == HEAD, loss, head_sums)
    for copy in sent:
        copy.wait()


def heads_blocks(share, half, table, own, sib, pre_own, pre_sib, biases, labels, crowd, targets):
    rows, units = pre_own.shape
    depth = len(own)
    blocks, xs, _, cols = own[0].shape
    smem = pl.BlockSpec(memory_space=pltpu.SMEM)
    vmem = pl.BlockSpec(memory_space=pltpu.VMEM)
    away = pl.BlockSpec(memory_space=pl.ANY)
    shape = jax.ShapeDtypeStruct
    return pl.pallas_call(
        functools.partial(head_blocks_kernel, share, depth),
        in_specs=[smem] + [away] * (2 * depth + 2) + [vmem] * 4,
        out_specs=[away] * 6 + [vmem] * 2,
        out_shape=[shape((rows, units), bf16)] * 2
        + [shape((units, HID), bf16)] * 2
        + [shape((HID // CORES, HEADP), bf16)] * 2
        + [shape((1, 2 * HID + HEADP), f32), shape((1, 1), f32)],
        scratch_shapes=[
            pltpu.VMEM((2 * depth, blocks, xs, half, cols), bf16),
            pltpu.VMEM((CORES, rows, units), f32),
            pltpu.VMEM((CORES, units, HID), bf16),
            pltpu.VMEM((HID, HEADP), bf16),
            pltpu.VMEM((rows, HID), f32),
            pltpu.VMEM((rows, HID), bf16),
            pltpu.VMEM((rows, HID), f32),
            pltpu.VMEM((rows, HID), bf16),
            pltpu.VMEM((HID, HEADP), f32),
            pltpu.VMEM((CORES, rows, units), bf16),
            pltpu.VMEM((CORES, units, HID), bf16),
            pltpu.VMEM((CORES, HID // CORES, HEADP), bf16),
            pltpu.VMEM((1, HEADP), f32),
            pltpu.SemaphoreType.DMA((2 * depth + 2,)),
            pltpu.SemaphoreType.DMA((3 * CORES,)),
        ],
        compiler_params=pltpu.CompilerParams(vmem_limit_bytes=WIDE * MIB),
        cost_estimate=LIGHT,
        name="heads",
    )(table, *own, *sib, pre_own, pre_sib, biases, labels, crowd, targets)


def head_kernel(
    share,
    wide,
    at_ref,
    pre_own,
    pre_sib,
    w2_own,
    w2_sib,
    wh,
    b1,
    b2,
    bh,
    tags,
    g_own,
    g_sib,
    gw2_own,
    gw2_sib,
    gwh_own,
    gwh_sib,
    sums,
    count,
    h1,
    pre2,
    gpre2,
    gwh,
):
    rows, units = pre_own.shape
    sides = ((pre_own, w2_own, g_own, gw2_own, 0), (pre_sib, w2_sib, g_sib, gw2_sib, units))
    pre2[...] = jnp.zeros_like(pre2) + b2[...]
    for pre, w2, _, _, at in sides:
        h1[:, at : at + units] = gelu(pre[...] + b1[:, at : at + units]).astype(bf16)
        for k in range(0, units, share):
            part = dot(h1[:, at + k : at + k + share], w2[k : k + share, :])
            pre2[...] += part.astype(bf16).astype(f32)
    h2 = gelu(pre2[...]).astype(bf16)
    out = dot(h2, wh[...]) + bh[...]
    kept = kept_count(wh)
    count[...] = kept
    row_loss, grad = losses(out, tags[...], kept)
    g_out = grad.astype(bf16)
    head_sums = jnp.sum(g_out.astype(f32), axis=0, keepdims=True)
    lane = lax.broadcasted_iota(jnp.int32, head_sums.shape, 1)
    loss = jnp.sum(row_loss, axis=0, keepdims=True)
    sums[:, 2 * HID : 2 * HID + HEADP] = jnp.where(lane == HEAD, loss, head_sums)
    gwh[...] = dot(h2, g_out, ((0,), (0,)))
    each = HID // (HID // share * wide)
    for side in range(CORES):

        @pl.when(at_ref[HID // share] == side)
        def _(side=side):
            for n in range(HID // each // CORES):
                for c, part in ((side, gwh_own), (1 - side, gwh_sib)):
                    row = (n * CORES + c) * each
                    part[n * each : (n + 1) * each, :] = gwh[row : row + each, :].astype(bf16)

    g_h2 = dot(g_out, wh[...], ((1,), (1,)))
    g2 = (g_h2 * gelu_slope(pre2[...])).astype(bf16)
    sums[:, HID : 2 * HID] = jnp.sum(g2.astype(f32), axis=0, keepdims=True)
    gpre2[...] = g2
    for n, (pre, w2, g1, gw2, at) in enumerate(sides):
        g_h1 = dot(gpre2[...], w2[...], ((1,), (1,)))
        g = (g_h1 * gelu_slope(pre[...] + b1[:, at : at + units])).astype(bf16)
        g1[...] = g
        columns = jnp.sum(g.astype(f32), axis=0, keepdims=True)
        for k in range(units // share):
            to = pl.multiple_of(at_ref[n * (units // share) + k] * share, share)
            sums[:, pl.ds(to, share)] = columns[:, k * share : (k + 1) * share]
        gw2[...] = dot(h1[:, at : at + units], gpre2[...], ((0,), (0,))).astype(gw2.dtype)


def heads_step(share, wide, at, pre_own, pre_sib, w2_own, w2_sib, wh, b1, b2, bh, tags):
    rows, units = pre_own.shape
    vmem = pl.BlockSpec(memory_space=pltpu.VMEM)
    shape = jax.ShapeDtypeStruct
    return pl.pallas_call(
        functools.partial(head_kernel, share, wide),
        in_specs=[pl.BlockSpec(memory_space=pltpu.SMEM)] + [vmem] * 9,
        out_specs=[vmem] * 8,
        out_shape=[
            shape((rows, units), bf16),
            shape((rows, units), bf16),
            shape((units, HID), bf16),
            shape((units, HID), bf16),
            shape((HID // CORES, HEADP), bf16),
            shape((HID // CORES, HEADP), bf16),
            shape((1, 2 * HID + HEADP), f32),
            shape((1, 1), f32),
        ],
        scratch_shapes=[
            pltpu.VMEM((rows, HID), bf16),
            pltpu.VMEM((rows, HID), f32),
            pltpu.VMEM((rows, HID), bf16),
            pltpu.VMEM((HID, HEADP), f32),
        ],
        compiler_params=pltpu.CompilerParams(vmem_limit_bytes=WIDE * MIB),
        cost_estimate=LIGHT,
        name="heads",
    )(at, pre_own, pre_sib, w2_own, w2_sib, wh, b1, b2, bh, tags)


class Grid:
    def __init__(self):
        self.wide = lax.axis_size("wide")
        self.tp = lax.axis_size("tp")
        self.y = self.tp // CORES
        self.x = self.y if self.wide % self.y == 0 else 1
        self.z = self.wide // self.x
        self.size = {"z": self.z, "x": self.x, "y": self.y, "c": CORES}
        wide, tp = lax.axis_index("wide"), lax.axis_index("tp")
        self.at = {"z": wide // self.x, "x": wide % self.x, "y": tp // CORES, "c": tp % CORES}

    def move(self, value, axis, by):
        pairs = []
        for z in range(self.z):
            for x in range(self.x):
                for y in range(self.y):
                    for c in range(CORES):
                        to = {"z": z, "x": x, "y": y, "c": c}
                        for a in axis:
                            to[a] = (to[a] + by) % self.size[a]
                        pairs.append((self.index(z, x, y, c), self.index(to["z"], to["x"], to["y"], to["c"])))
        return lax.ppermute(value, AXES, pairs)

    def flip(self, value, axis, bit):
        unit = {"c": 1, "y": CORES, "x": CORES * self.y, "z": CORES * self.y * self.x}
        step = bit * sum(unit[a] for a in axis)
        return lax.ppermute(value, AXES, [(i, i ^ step) for i in range(self.wide * self.tp)])

    def index(self, z, x, y, c):
        return ((z * self.x + x) * self.y + y) * CORES + c

    def swap(self, value):
        return self.move(value, "c", 1)


def spread_stacked(grid, value, order):
    stack = value[None, None, None]
    for axis in order:
        place = "zxy".index(axis)
        stack = jnp.concatenate([stack] + [grid.move(stack, axis, by) for by in range(1, grid.size[axis])], axis=place)
    for place, axis in enumerate("zxy"):
        if grid.size[axis] > 1:
            back = (grid.at[axis] - jnp.arange(grid.size[axis])) % grid.size[axis]
            stack = jnp.take(stack, back, axis=place, mode="clip")
    return stack


def collect_stacked(grid, stack, order):
    left = "zxy"
    total = stack
    for axis in order:
        place = left.index(axis)
        total = total.astype(bf16)

        def block(by):
            at = (grid.at[axis] + by) % grid.size[axis]
            return lax.dynamic_index_in_dim(total, at, place, keepdims=False)

        mine = block(0).astype(f32)
        for by in range(1, grid.size[axis]):
            mine = mine + grid.move(block(by), axis, by).astype(f32)
        total = mine
        left = left.replace(axis, "")
    return total


def all_sum(value):
    count = lax.axis_size("wide") * lax.axis_size("tp")
    if count & (count - 1):
        return lax.psum(value, AXES)
    bit = 1
    while bit < count:
        value = value + lax.ppermute(value, AXES, [(i, i ^ bit) for i in range(count)])
        bit *= 2
    return value


def after(value, *others):
    return lax.optimization_barrier((value, *others))[0]


class Links:
    def __init__(self, grid, in_step):
        self.grid = grid
        self.in_step = in_step
        self.last = {}
        self.slots = [{}, {}]

    def next(self):
        self.slots.append({})

    def send(self, value, axis, by=1):
        before = [self.slots[-2]["x"]] if self.in_step and axis == "z" and "x" in self.slots[-2] else []
        if axis in self.last:
            before.append(self.last[axis])
        sent = self.grid.move(after(value, *before) if before else value, axis, by)
        self.last[axis] = self.slots[-1][axis] = sent
        return sent


def adam_update(weight, grad, first, second, rate):
    first_new = decay_one * first + (1.0 - decay_one) * grad
    second_new = decay_two * second + (1.0 - decay_two) * grad * grad
    first_hat = first_new / (1.0 - decay_one**STEP)
    second_hat = second_new / (1.0 - decay_two**STEP)
    weight_new = weight - rate * (first_hat / (jnp.sqrt(second_hat) + epsilon) + weight_decay * weight)
    return (weight_new, first_new, second_new)


def by_blocks(grid, feats, cols, share, second_cols, head_rows, channels, rows):
    return (
        (grid.z, grid.x, grid.y) == (4, 2, 2)
        and feats % 16 == 0
        and feats > max(LATE_OUT, LATE_BACK)
        and cols == channels == 256
        and second_cols == 128
        and (share, head_rows) == (256, 32)
        and rows % (CHUNKS * GROUP) == 0
        and block_span(feats, grid.wide, channels) > 0
    )


def place_table(grid):
    found = []
    for sign in (-1, 1):
        for dz in range(grid.z):
            for dx in range(grid.x):
                z, x = (grid.at["z"] + sign * dz) % grid.z, (grid.at["x"] + sign * dx) % grid.x
                found.append(z * grid.x + x)
    y, core = grid.at["y"], grid.at["c"]
    found += [y, core]
    found += [CORES * ((y + k) % grid.y) + c for c in (core, 1 - core) for k in range(grid.y)]
    return jnp.stack(found).astype(jnp.int32)


def low_sum(first, *others):
    total = first.astype(f32)
    for value in others:
        total = total + value.astype(f32)
    return total.astype(bf16)


def terms(value):
    found = []
    for _ in range(TERMS):
        found.append(lax.optimization_barrier(value.astype(bf16)))
        value = value - found[-1].astype(f32)
    return jnp.concatenate(found, axis=0)


def from_terms(rows):
    count = rows.shape[0] // TERMS
    total = rows[:count].astype(f32)
    for k in range(1, TERMS):
        total = total + rows[k * count : (k + 1) * count].astype(f32)
    return total


def blocks_step(grid, make_crops, w_first, w_second, w_heads, biases, labels, crowd, targets):
    feats, cols = w_first.shape
    share, _ = w_second.shape
    head_rows = w_heads.shape[0]
    table = place_table(grid)
    count = grid.z * grid.x

    links = Links(grid, True)
    most = feats - LATE_OUT
    mine, first_low = prepare(w_first, w_second, w_heads, crowd, most)
    half = mine.shape[0] - feats
    m = {(0, 0, 0): mine}
    stacks = {}

    m[0, 1, 0] = grid.move(mine, "x", 1)
    m[0, 0, 1] = grid.move(mine, "y", 1)
    m[1, 0, 0] = grid.move(first_low, "z", 1)
    own_crops = [make_crops(i) for i in range(CHUNKS)]
    made = own_crops[:EARLY] + [m[key] for key in ((0, 1, 0), (0, 0, 1), (1, 0, 0))]
    m[3, 0, 0] = links.send(after(first_low, *made), "z", 3)
    m[1, 1, 0] = links.send(after(m[1, 0, 0], *made), "x")
    m[0, 1, 1] = links.send(after(m[0, 1, 0], *made), "y")
    stacks[0] = jnp.stack([jnp.stack([m[0, x, y][most:] for x in range(grid.x)]) for y in range(grid.y)])
    links.next()
    m[2, 0, 0] = links.send(m[1, 0, 0], "z", 1)
    m[3, 1, 0] = links.send(m[3, 0, 0], "x")
    m[1, 0, 1] = links.send(m[1, 0, 0], "y")
    links.next()
    stacks[1] = links.send(stacks[0], "z", 1)
    m[2, 1, 0] = links.send(m[2, 0, 0], "x")
    m[3, 0, 1] = links.send(m[3, 0, 0], "y")
    links.next()
    stacks[3] = links.send(stacks[0], "z", 3)
    m[1, 1, 1] = links.send(m[1, 0, 1], "x")
    m[2, 0, 1] = links.send(m[2, 0, 0], "y")
    links.next()
    stacks[2] = links.send(stacks[1], "z", 1)
    m[3, 1, 1] = links.send(m[3, 0, 1], "x")
    m[2, 1, 1] = links.send(m[2, 1, 0], "y")
    sib_crops = []
    for chunk in own_crops:
        sib_crops.append(grid.swap(after(chunk, *made)))
    crops = own_crops + sib_crops

    span = block_span(feats, grid.wide, cols)
    both = (0, 1)

    def products(work, before):
        inputs = []
        for dz, dx, ys, kind in work:
            inputs += [m[dz, dx, y] for y in ys if kind != "last"] + [stacks[dz]] * (kind != "most")
        items = tuple((dz * grid.x + dx, dx, ys, kind) for dz, dx, ys, kind in work)
        return first_blocks(table, crops, inputs, items, feats, most, grid.wide, grid.y, before)

    work = [(dz, dx, both, "all") for dz, dx in ((0, 0), (0, 1), (1, 0), (3, 0), (1, 1))]
    first_pre = products(work + [(3, 1, (0,), "all"), (2, 0, both, "most"), (2, 1, (0,), "most")], None)
    work = [(2, 0, both, "last"), (2, 1, both, "last"), (2, 1, (1,), "most"), (3, 1, (1,), "all")]
    pre = products(work, first_pre)
    sib_stacks = {2: grid.swap(after(stacks[2], first_pre[0]))}
    sib_stacks[0] = grid.swap(stacks[0])
    sib_stacks[1] = grid.swap(after(stacks[1], sib_stacks[0]))
    sib_stacks[3] = grid.swap(after(stacks[3], sib_stacks[1], first_pre[0]))
    g_own, g_send, gw2, gw2_send, gwh, gwh_send, sums, roi_count = heads_blocks(
        share,
        half,
        table,
        [stacks[z] for z in range(4)],
        [sib_stacks[z] for z in range(4)],
        pre[0],
        grid.swap(pre[1]),
        biases[None, :],
        labels[None, :],
        crowd[None, :],
        targets.T,
    )

    g_got = grid.swap(g_send)
    m = {}
    parts = {}

    def gradients(keys, wait=()):
        numbers = tuple(count + dz * grid.x + dx for dz, dx in keys)
        outs = first_grad_blocks(after(table, *wait), numbers, crops, g_own, g_got, feats, LATE_BACK, grid.y, span)
        for i, (dz, dx) in enumerate(keys):
            for y in range(grid.y):
                m[dz, dx, y], parts[dz, dx, y] = outs[(i * grid.y + y) * 2 : (i * grid.y + y) * 2 + 2]

    gradients([(2, 1), (2, 0), (3, 1), (3, 0)])
    lates = [parts[dz, dx, y] for dz in (2, 3) for y in range(grid.y) for dx in range(grid.x)]
    packed = pack(
        table,
        lates,
        (gw2, grid.swap(after(gw2_send, g_got))),
        (gwh, grid.swap(after(gwh_send, g_got))),
        sums,
        half,
        (grid.y, grid.x),
    )

    def stack_of(dz):
        if dz >= 2:
            return packed[dz - 2]
        first = jnp.stack([jnp.stack([parts[dz, dx, y] for dx in range(grid.x)]) for y in range(grid.y)])
        return jnp.concatenate([first, packed[2][dz]], axis=2)

    links = Links(grid, False)
    far = stack_of(2)
    gradients([(1, 1), (1, 0), (0, 1), (0, 0)], [far])
    begun = (far, m[3, 1, 1])
    z0 = links.send(after(far, *begun[1:]), "z", 1)
    y0 = links.send(after(m[2, 1, 1], *begun), "y")
    x0 = links.send(after(m[3, 1, 1], *begun[:1]), "x")
    z1 = links.send(stack_of(3), "z", 3)
    y1 = links.send(m[2, 0, 1], "y")
    x1 = links.send(m[3, 1, 0], "x")
    z2 = links.send(low_sum(stack_of(1), z0), "z", 1)
    x2 = links.send(low_sum(m[2, 1, 0], y0), "x")
    y2 = links.send(low_sum(m[3, 0, 1], x0), "y")
    z3 = links.send(low_sum(m[2, 0, 0], x2, y1), "z", 1)
    x3 = links.send(m[1, 1, 1], "x")
    y3 = links.send(m[0, 1, 1], "y")
    z4 = links.send(low_sum(m[3, 0, 0], x1, y2), "z", 3)
    x4 = links.send(m[1, 1, 0], "x")
    y4 = links.send(low_sum(m[1, 0, 1], x3), "y")

    def extra_rows(stack):
        rows = stack[:, :, -EXTRA : 8 - EXTRA].reshape(-1, cols)
        return from_terms(rows[: TERMS * (sums.shape[1] // cols)])

    odd = grid.at["z"] % 2 == 1
    below, above, opposite = extra_rows(z0), extra_rows(z1), extra_rows(z2)
    total = sums.reshape(-1, cols)
    total = (total + jnp.where(odd, below, above)) + (opposite + jnp.where(odd, above, below))
    extra = TERMS * total.shape[0]
    late = low_sum(stack_of(0), z1, z2)
    x5 = links.send(jnp.concatenate([late[:, 1].reshape(-1, cols), terms(total)], axis=0), "x")
    x6 = links.send(low_sum(m[0, 1, 0], y3), "x")
    z5 = links.send(low_sum(m[1, 0, 0], x4, y4, z3), "z", 1)
    y5 = links.send(m[0, 0, 1], "y")
    total = total + from_terms(x5[-extra:])
    late = low_sum(late[:, 0], x5[:-extra].reshape(late[:, 0].shape))
    y6 = links.send(jnp.concatenate([late[1], terms(total)], axis=0), "y")
    total = total + from_terms(y6[-extra:])
    total = total + grid.swap(total)
    sums = total.reshape(1, -1)
    main = m[0, 0, 0].astype(f32)
    for value in (x6, y5, z4, z5):
        main = main + value.astype(f32)
    late = late[0].astype(f32) + y6[:-extra].astype(f32)

    first_total = jnp.concatenate([main, late[:LATE_BACK]], axis=0)
    late = late[LATE_BACK : LATE_BACK + half]
    total = jnp.concatenate([late[:, :128], late[:, 128:]], axis=0)
    heads_total = jnp.concatenate(
        [total[share + k * head_rows : share + (k + 1) * head_rows] for k in range(HEADP // 128)], axis=1
    )[:, :HEAD]
    return roi_count.reshape(()), sums, first_total, total[:share], heads_total


def stacked_step(grid, make_crops, w_first, w_second, w_heads, biases, labels, crowd, targets):
    tags = jnp.concatenate([labels[:, None].astype(f32), crowd[:, None].astype(f32), targets.astype(f32)], axis=1)
    tags = jnp.pad(tags, ((0, 0), (0, 122)))
    feats, cols = w_first.shape
    share, second_cols = w_second.shape
    head_rows = w_heads.shape[0]
    units = HID // CORES
    core = grid.at["c"]
    kept = jnp.sum(1 - crowd)
    head_block = jnp.pad(w_heads, ((0, 0), (0, HEADP - HEAD)))
    spot = (lax.broadcasted_iota(jnp.int32, head_block.shape, 0) == 0) * 1
    lane = lax.broadcasted_iota(jnp.int32, head_block.shape, 1)
    head_block = head_block + (
        spot * (jnp.where(lane == HEADP - 1, kept % 128, 0) + jnp.where(lane == HEADP - 2, kept // 128, 0))
    ).astype(f32)
    small = jnp.concatenate(
        [w_second.astype(bf16).reshape(-1, cols), head_block.astype(bf16).reshape(-1, cols)], axis=0
    )
    second_rows = share * second_cols // cols
    small_all = spread_stacked(grid, small, "zxy").reshape(grid.wide, grid.y, *small.shape)
    weight = spread_stacked(grid, w_first.astype(bf16), "zxy")
    weight = weight.transpose(2, 0, 1, 3, 4).reshape(grid.y, grid.wide * feats, cols)
    crops = [make_crops(i) for i in range(CHUNKS)]
    crops = crops + [grid.swap(c) for c in crops]
    second_own = (
        small_all[:, :, :second_rows]
        .reshape(grid.wide, grid.y, share, second_cols)
        .transpose(1, 2, 0, 3)
        .reshape(units, HID)
    )
    heads_own = small_all[:, :, second_rows:].reshape(grid.wide, grid.y, head_rows, HEADP)
    heads_sib = grid.swap(heads_own)
    head_matrix = jnp.where(
        core == 0, jnp.stack([heads_own, heads_sib], axis=2), jnp.stack([heads_sib, heads_own], axis=2)
    ).reshape(HID, HEADP)
    bias = biases[:HID].reshape(grid.y, CORES, share)
    bias = jnp.where(core == 0, bias, bias[:, ::-1]).transpose(1, 0, 2).reshape(1, -1)
    pre_own, pre_send = first_layer(crops, weight)
    unit_at = [2 * y + c for c in (core, 1 - core) for y in range(grid.y)]
    g_own, g_send, gw2_own, gw2_send, gwh, gwh_send, sums, roi_count = heads_step(
        share,
        grid.wide,
        jnp.stack([jnp.asarray(v) for v in unit_at + [core]]).astype(jnp.int32),
        pre_own,
        grid.swap(pre_send),
        second_own,
        grid.swap(second_own),
        head_matrix,
        bias,
        biases[HID : 2 * HID].reshape(1, -1),
        jnp.pad(biases[2 * HID :], (0, HEADP - HEAD)).reshape(1, -1),
        tags,
    )
    grad = first_grad(crops, g_own, grid.swap(g_send), grid.y)
    grad = grad.reshape(grid.y, grid.wide, feats, cols).transpose(1, 0, 2, 3)
    first_total = collect_stacked(grid, grad.reshape(grid.z, grid.x, grid.y, feats, cols), "yxz")
    gw2 = gw2_own.astype(f32) + grid.swap(gw2_send).astype(f32)
    gwh = gwh.astype(f32) + grid.swap(gwh_send).astype(f32)
    gw2 = gw2.astype(bf16).reshape(grid.y, share, grid.wide, second_cols).transpose(2, 0, 1, 3)
    small_grad = jnp.concatenate(
        [
            gw2.reshape(grid.wide, grid.y, second_rows, cols),
            gwh.astype(bf16).reshape(grid.wide, grid.y, -1, cols),
        ],
        axis=2,
    ).reshape(grid.z, grid.x, grid.y, -1, cols)
    small_total = collect_stacked(grid, small_grad, "yxz")
    second_total = small_total[:second_rows].reshape(share, second_cols)
    heads_total = small_total[second_rows:].reshape(head_rows, HEADP)[:, :HEAD]
    sums = all_sum(sums)
    return roi_count.reshape(()), sums, first_total, second_total, heads_total


def shards(
    maps,
    roi_image,
    roi_level,
    roi_corner,
    roi_weights,
    crowd,
    labels,
    box_targets,
    w_first,
    m_first,
    v_first,
    w_second,
    m_second,
    v_second,
    w_heads,
    m_heads,
    v_heads,
    biases,
    bias_m,
    bias_v,
):
    grid = Grid()
    rows = crowd.shape[0]

    images, levels, height, width, channels = maps.shape
    base = ((roi_image * levels + roi_level) * height + roi_corner[:, 0]).astype(jnp.int32)
    col = roi_corner[:, 1].astype(jnp.int32)
    flat_maps = maps.reshape(images * levels * height, width, channels)
    padded = jnp.pad(roi_weights, ((0, 0), (0, 0), (0, 1), (0, 0)))
    row_w = padded[:, 0].reshape(rows * 8, WIN)
    col_w = padded[:, 1].reshape(rows * 8, WIN)
    step = rows // CHUNKS
    def make_crops(i, *wait):
        return window_crops(flat_maps, after(base, *wait) if wait else base, col, row_w, col_w, i * step, step)

    shapes = (*w_first.shape, *w_second.shape, w_heads.shape[0], channels, rows)
    run = blocks_step if by_blocks(grid, *shapes) else stacked_step
    roi_count, sums, first_total, second_total, heads_total = run(
        grid, make_crops, w_first, w_second, w_heads, biases, labels, crowd, box_targets
    )
    loss_total = sums[0, 2 * HID + HEAD]
    bias_grad = sums[0, : 2 * HID + HEAD]

    first_out = adam_update(w_first, first_total, m_first, v_first, rate_first)
    second_out = adam_update(w_second, second_total, m_second, v_second, rate_second)
    heads_out = adam_update(w_heads, heads_total, m_heads, v_heads, rate_heads)
    bias_out = adam_update(biases, bias_grad, bias_m, bias_v, rate_biases)
    return (loss_total, roi_count, *first_out, *second_out, *heads_out, *bias_out)


def solution(mesh):
    rows = P(("wide", "tp"))
    both = P("wide", "tp")
    turned = P("tp", "wide")
    return jax.shard_map(
        shards,
        mesh=mesh,
        in_specs=(rows,) * 8 + (both,) * 3 + (turned,) * 3 + (rows,) * 3 + (P(),) * 3,
        out_specs=(P(), P()) + (both,) * 3 + (turned,) * 3 + (rows,) * 3 + (P(),) * 3,
        check_vma=False,
    )
```

```python
import functools

import jax
import jax.numpy as jnp
import numpy as np
from jax import lax
from jax.experimental import pallas as pl
from jax.experimental.pallas import tpu as pltpu
from jax.sharding import PartitionSpec as P

HID = 1024
CLS = 81
POOL = 7
CELLS = POOL * POOL
WIN = 16
STEP = 10
HEAD = 401
HEADP = 512
CORES = 2
CHUNKS = 8
EARLY = 4
GROUP = 32
KSTEP = 7
LATE_OUT = 192
LATE_BACK = 208
TERMS = 3
EXTRA = 16
WIDE = 60
MIB = 2**20
LIGHT = pl.CostEstimate(flops=0, bytes_accessed=1024, transcendentals=0)

AXES = ("wide", "tp")
rate_first = 0.02
rate_second = 0.06
rate_heads = 0.06
rate_biases = 0.3
decay_one = 0.9
decay_two = 0.999
epsilon = 1e-08
weight_decay = 0.1
GELU_A = 0.7978845608028654
GELU_B = 0.044715

f32 = jnp.float32
bf16 = jnp.bfloat16


def dot(a, b, contract=((1,), (0,))):
    return lax.dot_general(a, b, (contract, ((), ())), preferred_element_type=f32)


def crop_kernel(first, base_ref, col_ref, maps_ref, wr_ref, wc_ref, rep_ref, tile_ref, *refs):
    out_ref, rows_s, cols_s, left, right = refs
    step = pl.program_id(0)
    lanes = rows_s.shape[1]
    halves = (left, right)
    rows_s[...] = dot(wr_ref[...], rep_ref[...])
    cols_s[...] = dot(wc_ref[...], tile_ref[...])

    def one(i, carry):
        r = first + step * GROUP + i
        at = pl.multiple_of(i * 8, 8)
        rows = rows_s[pl.ds(at, 8), :]
        x0 = col_ref[r]
        cols = jnp.concatenate(
            [pltpu.roll(cols_s[pl.ds(at, 8), k : k + 128], x0, 1) for k in range(0, lanes, 128)], axis=1
        )
        both = jnp.concatenate([rows[a : a + 1, :] * cols for a in range(POOL)], axis=0)
        high = both.astype(bf16)
        low = (both - high.astype(f32)).astype(bf16)
        window = maps_ref[pl.ds(base_ref[r], WIN), :, :].reshape(lanes, maps_ref.shape[2])
        got = dot(jnp.concatenate([high, low], axis=0), window)
        got = got[: POOL * 8] + got[POOL * 8 :]
        for h, half in enumerate(halves):
            half[pl.ds(pl.multiple_of(i * POOL * 8, 8), POOL * 8), :] = got[:, h * 128 : (h + 1) * 128]
        return carry

    lax.fori_loop(0, GROUP, one, 0, unroll=8)
    for a in range(POOL):
        for b in range(POOL):
            for h, half in enumerate(halves):
                out_ref[a * POOL + b, :, h * 128 : (h + 1) * 128] = half[
                    pl.ds(a * 8 + b, GROUP, stride=POOL * 8), :
                ].astype(bf16)


def window_crops(maps, base, col, wr, wc, first, count):
    rows, width, channels = maps.shape
    lanes = WIN * width
    lane = np.arange(lanes)[None]
    unit = np.arange(WIN)[:, None]
    rep = jnp.asarray(lane // width == unit, bf16)
    til = jnp.asarray(lane % width == unit, bf16)
    return pl.pallas_call(
        functools.partial(crop_kernel, first),
        grid_spec=pltpu.PrefetchScalarGridSpec(
            num_scalar_prefetch=2,
            grid=(count // GROUP,),
            in_specs=[
                pl.BlockSpec(maps.shape, lambda i, *_: (0, 0, 0)),
                pl.BlockSpec((GROUP * 8, WIN), lambda i, *_: (first // GROUP + i, 0)),
                pl.BlockSpec((GROUP * 8, WIN), lambda i, *_: (first // GROUP + i, 0)),
                pl.BlockSpec(rep.shape, lambda i, *_: (0, 0)),
                pl.BlockSpec(til.shape, lambda i, *_: (0, 0)),
            ],
            out_specs=pl.BlockSpec((CELLS, GROUP, channels), lambda i, *_: (0, i, 0)),
            scratch_shapes=[
                pltpu.VMEM((GROUP * 8, lanes), f32),
                pltpu.VMEM((GROUP * 8, lanes), f32),
                pltpu.VMEM((GROUP * POOL * 8, 128), f32),
                pltpu.VMEM((GROUP * POOL * 8, 128), f32),
            ],
        ),
        out_shape=jax.ShapeDtypeStruct((CELLS, count, channels), bf16),
        compiler_params=pltpu.CompilerParams(vmem_limit_bytes=18 * MIB),
        cost_estimate=LIGHT,
        name="crops",
    )(base, col, maps, wr, wc, rep, til)


def first_kernel(parts, *refs):
    crops, weight, own, send = refs[:parts], refs[parts], refs[parts + 1], refs[parts + 2]
    step = pl.program_id(0)
    blocks, depth, cols = weight.shape
    channels = crops[0].shape[2]

    @pl.when(step == 0)
    def _():
        own[...] = jnp.zeros_like(own)
        send[...] = jnp.zeros_like(send)

    for out, refs_half in ((own, crops[: parts // 2]), (send, crops[parts // 2 :])):
        lhs = jnp.concatenate(
            [jnp.concatenate([ref[j] for ref in refs_half], axis=0) for j in range(depth // channels)], axis=1
        )
        for y in range(blocks):
            out[:, y * cols : (y + 1) * cols] += dot(lhs, weight[y])


def first_layer(crops, weight):
    parts = len(crops)
    blocks, feats, cols = weight.shape
    channels = crops[0].shape[2]
    rows = sum(c.shape[1] for c in crops) // 2
    return pl.pallas_call(
        functools.partial(first_kernel, parts),
        grid=(CELLS // KSTEP,),
        in_specs=[pl.BlockSpec((KSTEP,) + c.shape[1:], lambda i: (i, 0, 0)) for c in crops]
        + [pl.BlockSpec((blocks, KSTEP * channels, cols), lambda i: (0, i, 0))],
        out_specs=[pl.BlockSpec((rows, blocks * cols), lambda i: (0, 0))] * 2,
        out_shape=[jax.ShapeDtypeStruct((rows, blocks * cols), f32)] * 2,
        compiler_params=pltpu.CompilerParams(vmem_limit_bytes=60 * MIB),
        cost_estimate=LIGHT,
        name="first_layer",
    )(*crops, weight)


def first_grad_kernel(parts, cols, *refs):
    crops, own, got, out = refs[:parts], refs[parts], refs[parts + 1], refs[parts + 2]
    channels = crops[0].shape[2]
    grads = jnp.concatenate([own[...], got[...]], axis=0)
    for j in range(crops[0].shape[0]):
        lhs = jnp.concatenate([ref[j] for ref in crops], axis=0)
        res = dot(lhs, grads, ((0,), (0,))).astype(bf16)
        for y in range(out.shape[0]):
            out[y, j * channels : (j + 1) * channels, :] = res[:, y * cols : (y + 1) * cols]


def first_grad(crops, own, got, blocks):
    parts = len(crops)
    rows, units = own.shape
    cols = units // blocks
    channels = crops[0].shape[2]
    return pl.pallas_call(
        functools.partial(first_grad_kernel, parts, cols),
        grid=(CELLS // KSTEP,),
        in_specs=[pl.BlockSpec((KSTEP,) + c.shape[1:], lambda i: (i, 0, 0)) for c in crops]
        + [pl.BlockSpec((rows, units), lambda i: (0, 0))] * 2,
        out_specs=pl.BlockSpec((blocks, KSTEP * channels, cols), lambda i: (0, i, 0)),
        out_shape=jax.ShapeDtypeStruct((blocks, CELLS * channels, cols), bf16),
        compiler_params=pltpu.CompilerParams(vmem_limit_bytes=60 * MIB),
        cost_estimate=LIGHT,
        name="first_grad",
    )(*crops, own, got)


def block_span(feats, wide, channels):
    span = max(-(-((w * feats) % channels + feats) // channels) for w in range(wide))
    return span if all(w * feats // channels + span <= CELLS for w in range(wide)) else 0


def cell_copies(crops, start, span, cells, sems):
    found = []
    at = 0
    for n, ref in enumerate(crops):
        rows = ref.shape[1]
        found.append(pltpu.make_async_copy(ref.at[pl.ds(start, span)], cells.at[:, pl.ds(at, rows)], sems.at[n]))
        at += rows
    return found


def rows_of(kind, feats, most):
    return {"all": (0, feats), "most": (0, most), "last": (most, feats)}[kind]


def kind_span(kind, feats, most, wide, channels):
    begin, end = rows_of(kind, feats, most)
    return max(-(-((w * feats + begin) % channels + end - begin) // channels) for w in range(wide))


def block_kernel(items, feats, most, wide, parts, fresh, table, *refs):
    count = len(items)
    crops, rest = refs[:parts], refs[parts:]
    own, send, pad, cells, sems = rest[-5:]
    before, inputs = (None, rest[:-5]) if fresh else (rest[:2], rest[2:-5])
    step = pl.program_id(0)
    rows = own.shape[0]
    channels = cells.shape[3]
    cols = channels
    needs = [len(item[2]) * (item[3] != "last") + (item[3] != "most") for item in items]
    spans = [kind_span(item[3], feats, most, wide, channels) for item in items]

    def copies(i):
        slot = i % 2
        number, side, ys, kind = items[i]
        begin, end = rows_of(kind, feats, most)
        start = table[number] * feats + begin
        cell = jnp.minimum(start // channels, CELLS - spans[i])
        at = pl.multiple_of(start - cell * channels, 16)
        found = cell_copies(crops, cell, spans[i], cells.at[slot, pl.ds(0, spans[i])], sems.at[slot])
        group = inputs[sum(needs[:i]) : sum(needs[: i + 1])]
        for k, y in enumerate(ys):
            lanes = pl.ds(y * cols, cols)
            if kind != "last":
                source = group[k].at[pl.ds(0, most)]
                found.append(
                    pltpu.make_async_copy(source, pad.at[slot, pl.ds(at, most), lanes], sems.at[slot, parts + 2 * k])
                )
            if kind != "most":
                source = group[-1].at[y, side, pl.ds(0, feats - most)]
                to = pl.ds(pl.multiple_of(at + most - begin, 16), feats - most)
                found.append(pltpu.make_async_copy(source, pad.at[slot, to, lanes], sems.at[slot, parts + 1 + 2 * k]))
        return found

    def edges(i):
        begin, end = rows_of(items[i][3], feats, most)
        deep = spans[i] * channels
        low = (end - begin) // channels * channels
        lanes = pad.shape[2]
        if low:
            pad[i % 2, :channels, :] = jnp.zeros((channels, lanes), bf16)
        pad[i % 2, low:deep, :] = jnp.zeros((deep - low, lanes), bf16)

    @pl.when(step == 0)
    def _():
        edges(0)
        for copy in copies(0):
            copy.start()
        if fresh:
            own[...] = jnp.zeros_like(own)
            send[...] = jnp.zeros_like(send)
        else:
            own[...] = before[0][...]
            send[...] = before[1][...]

    for i in range(count):

        @pl.when(step == i)
        def _(i=i):
            if i + 1 < count:
                edges(i + 1)
                for copy in copies(i + 1):
                    copy.start()
            for copy in copies(i):
                copy.wait()

    slot = lax.rem(step, 2)
    forms = [(span, item[2]) for span, item in zip(spans, items)]
    for form in sorted(set(forms)):
        span, ys = form
        lanes = slice(ys[0] * cols, (ys[-1] + 1) * cols)

        @pl.when(functools.reduce(jnp.logical_or, [step == i for i in range(count) if forms[i] == form]))
        def _(span=span, lanes=lanes):
            lhs = jnp.concatenate([cells[slot, j] for j in range(span)], axis=1)
            got = dot(lhs, pad[slot, : span * channels, lanes])
            own[:, lanes] += got[:rows]
            send[:, lanes] += got[rows:]


def whole(shape):
    return pl.BlockSpec(shape, lambda i, place: (0,) * len(shape))


def first_blocks(table, crops, inputs, items, feats, most, wide, blocks, before):
    rows = sum(c.shape[1] for c in crops) // 2
    channels = crops[0].shape[2]
    units = blocks * channels
    lead = [] if before is None else list(before)
    away = pl.BlockSpec(memory_space=pl.ANY)
    parts = len(crops)
    span = kind_span("all", feats, most, wide, channels)
    return pl.pallas_call(
        functools.partial(block_kernel, items, feats, most, wide, parts, before is None),
        grid_spec=pltpu.PrefetchScalarGridSpec(
            num_scalar_prefetch=1,
            grid=(len(items),),
            in_specs=[away] * parts + [whole((rows, units))] * len(lead) + [away] * len(inputs),
            out_specs=[whole((rows, units))] * 2,
            scratch_shapes=[
                pltpu.VMEM((2, span * channels, units), bf16),
                pltpu.VMEM((2, span, 2 * rows, channels), bf16),
                pltpu.SemaphoreType.DMA((2, parts + 2 * blocks)),
            ],
        ),
        out_shape=[jax.ShapeDtypeStruct((rows, units), f32)] * 2,
        input_output_aliases={} if before is None else {1 + parts: 0, 2 + parts: 1},
        compiler_params=pltpu.CompilerParams(vmem_limit_bytes=WIDE * MIB),
        cost_estimate=LIGHT,
        name="first_blocks",
    )(table, *crops, *lead, *inputs)


def block_grad_kernel(span, numbers, feats, blocks, parts, table, *refs):
    crops, (own, got), rest = refs[:parts], refs[parts : parts + 2], refs[parts + 2 :]
    outs, (full, cells, in_sems, out_sems) = rest[:-4], rest[-4:]
    step = pl.program_id(0)
    count = len(outs) // (2 * blocks)
    channels = cells.shape[3]
    cols = full.shape[2] // blocks

    def loads(i):
        return cell_copies(crops, (table[numbers[i]] * feats) // channels, span, cells.at[i % 2], in_sems.at[i % 2])

    def stores(i):
        at = pl.multiple_of((table[numbers[i]] * feats) % channels, 16)
        found = []
        for y in range(blocks):
            main, late = outs[(i * blocks + y) * 2], outs[(i * blocks + y) * 2 + 1]
            most = main.shape[0]
            lanes = pl.ds(y * cols, cols)
            found.append(pltpu.make_async_copy(full.at[i % 2, pl.ds(at, most), lanes], main, out_sems.at[i % 2, 2 * y]))
            found.append(
                pltpu.make_async_copy(
                    full.at[i % 2, pl.ds(pl.multiple_of(at + most, 16), feats - most), lanes],
                    late,
                    out_sems.at[i % 2, 2 * y + 1],
                )
            )
        return found

    @pl.when(step == 0)
    def _():
        for copy in loads(0):
            copy.start()

    for i in range(count):

        @pl.when(step == i)
        def _(i=i):
            if i + 1 < count:
                for copy in loads(i + 1):
                    copy.start()
            for copy in loads(i):
                copy.wait()
            if i >= 2:
                for copy in stores(i - 2):
                    copy.wait()

    slot = lax.rem(step, 2)
    grads = jnp.concatenate([own[...], got[...]], axis=0)
    for j in range(span):
        full[slot, j * channels : (j + 1) * channels, :] = dot(cells[slot, j], grads, ((0,), (0,))).astype(bf16)

    for i in range(count):

        @pl.when(step == i)
        def _(i=i):
            for copy in stores(i):
                copy.start()
            if i == count - 1:
                for k in range(max(0, count - 2), count):
                    for copy in stores(k):
                        copy.wait()


def first_grad_blocks(table, numbers, crops, own, got, feats, late, blocks, span):
    rows, units = own.shape
    channels = crops[0].shape[2]
    cols = units // blocks
    count = len(numbers)
    parts = len(crops)
    outs = [(feats - late, cols), (late, cols)] * (count * blocks)
    away = pl.BlockSpec(memory_space=pl.ANY)
    return pl.pallas_call(
        functools.partial(block_grad_kernel, span, numbers, feats, blocks, parts),
        grid_spec=pltpu.PrefetchScalarGridSpec(
            num_scalar_prefetch=1,
            grid=(count,),
            in_specs=[away] * parts + [whole((rows, units))] * 2,
            out_specs=[away] * len(outs),
            scratch_shapes=[
                pltpu.VMEM((2, span * channels, units), bf16),
                pltpu.VMEM((2, span, 2 * rows, channels), bf16),
                pltpu.SemaphoreType.DMA((2, parts)),
                pltpu.SemaphoreType.DMA((2, 2 * blocks)),
            ],
        ),
        out_shape=[jax.ShapeDtypeStruct(v, bf16) for v in outs],
        compiler_params=pltpu.CompilerParams(vmem_limit_bytes=WIDE * MIB),
        cost_estimate=LIGHT,
        name="first_grad",
    )(table, *crops, own, got)


def small_place(half, begin, end):
    lane = 0 if end <= half else 128
    back = half if lane else 0
    return slice(begin - back, end - back), slice(lane, lane + 128)


def prepare_kernel(first, second, heads, crowd, mine, low, first_s, second_s, heads_s, crowd_s, wide_heads, low_s, in_sems, out_sems):
    feats = first.shape[0]
    share = second.shape[0]
    rows = heads.shape[0]
    half = mine.shape[0] - feats
    most = low.shape[0]
    cuts = [feats * k // 4 // 16 * 16 for k in range(4)] + [feats]
    loads = [
        pltpu.make_async_copy(first.at[pl.ds(a, b - a)], first_s.at[pl.ds(a, b - a)], in_sems.at[k])
        for k, (a, b) in enumerate(zip(cuts, cuts[1:]))
    ]
    others = [
        pltpu.make_async_copy(ref, to, in_sems.at[4 + k])
        for k, (ref, to) in enumerate(((second, second_s), (heads, heads_s), (crowd, crowd_s)))
    ]
    for copy in others + loads:
        copy.start()
    for copy in others:
        copy.wait()
    kept = jnp.sum(1 - crowd_s[...], axis=1, keepdims=True)
    wide_heads[...] = jnp.zeros_like(wide_heads)
    wide_heads[:, :HEAD] = heads_s[...]
    lane = lax.broadcasted_iota(jnp.int32, (rows, 128), 1)
    row = lax.broadcasted_iota(jnp.int32, (rows, 128), 0)
    marks = jnp.where(lane == 127, kept % 128, jnp.where(lane == 126, kept // 128, 0))
    wide_heads[:, HEADP - 128 :] += jnp.where(row == 0, marks, 0).astype(f32)
    for begin, end in ((0, min(share, half)), (half, share)):
        if begin < end:
            at, lanes = small_place(half, begin, end)
            low_s[feats + at.start : feats + at.stop, lanes] = second_s[begin:end, :].astype(bf16)
    for k in range(HEADP // 128):
        at, lanes = small_place(half, share + k * rows, share + (k + 1) * rows)
        low_s[feats + at.start : feats + at.stop, lanes] = wide_heads[:, k * 128 : (k + 1) * 128].astype(bf16)
    stores = []
    for k, (a, b) in enumerate(zip(cuts, cuts[1:])):
        loads[k].wait()
        low_s[a:b, :] = first_s[a:b, :].astype(bf16)
        end = mine.shape[0] if b == feats else b
        stores.append(pltpu.make_async_copy(low_s.at[pl.ds(a, end - a)], mine.at[pl.ds(a, end - a)], out_sems.at[k]))
        stores[-1].start()
    stores.append(pltpu.make_async_copy(low_s.at[pl.ds(0, most)], low, out_sems.at[4]))
    stores[-1].start()
    for copy in stores:
        copy.wait()


def prepare(first, second, heads, crowd, most):
    feats, cols = first.shape
    half = (second.shape[0] + heads.shape[0] * HEADP // 128) // 2
    away = pl.BlockSpec(memory_space=pl.ANY)
    crowd = crowd[None, :]
    return pl.pallas_call(
        prepare_kernel,
        in_specs=[away] * 4,
        out_specs=[away] * 2,
        out_shape=[jax.ShapeDtypeStruct((feats + half, cols), bf16), jax.ShapeDtypeStruct((most, cols), bf16)],
        scratch_shapes=[
            pltpu.VMEM(first.shape, f32),
            pltpu.VMEM(second.shape, f32),
            pltpu.VMEM(heads.shape, f32),
            pltpu.VMEM(crowd.shape, jnp.int32),
            pltpu.VMEM((heads.shape[0], HEADP), f32),
            pltpu.VMEM((feats + half, cols), bf16),
            pltpu.SemaphoreType.DMA((7,)),
            pltpu.SemaphoreType.DMA((5,)),
        ],
        cost_estimate=LIGHT,
        compiler_params=pltpu.CompilerParams(vmem_limit_bytes=WIDE * MIB),
        name="prepare",
    )(first, second, heads, crowd)


def pack_kernel(table, *refs):
    lates, sides, sums = refs[:8], refs[8:12], refs[12]
    stack_two, stack_three, near_out, near, far, gw2s, gwhs, late_sems, in_sems, small_sems = refs[13:]
    gw2, gw2_got, gwh, gwh_got = gw2s.at[0], gw2s.at[1], gwhs.at[0], gwhs.at[1]
    arrive = [
        pltpu.make_async_copy(ref, to, in_sems.at[n]) for n, (ref, to) in enumerate(zip(sides, (gw2, gw2_got, gwh, gwh_got)))
    ]
    for copy in arrive:
        copy.start()
    depth = near.shape[0] + far.shape[0]
    _, blocks, xs, tall, _ = near.shape
    half = tall - EXTRA
    share = gw2.shape[0] // blocks
    count = depth * xs
    rows = gwh.shape[0] // (count * blocks)
    long = lates[0].shape[0]
    stacks = (stack_two, stack_three)
    copies = []
    for d in range(2):
        for y in range(blocks):
            for x in range(xs):
                n = (d * blocks + y) * xs + x
                copies.append(pltpu.make_async_copy(lates[n], far.at[d, y, x, pl.ds(0, long)], late_sems.at[n]))
    for copy in copies:
        copy.start()
    rest = sums[...]
    rows_left = []
    for _ in range(TERMS):
        term = rest.astype(bf16).astype(f32)
        rest = rest - term
        rows_left += [term[:, k : k + 256] for k in range(0, term.shape[1], 256)]
    rows_left += [jnp.zeros_like(rows_left[0])] * (-len(rows_left) % (blocks * xs))
    each = len(rows_left) // (blocks * xs)
    for copy in arrive:
        copy.wait()
    for dz in (2, 3, 1, 0):
        out, at, skip = (far, dz - 2, long) if dz >= 2 else (near, dz, 0)
        for y in range(blocks):
            for x in range(xs):
                here = table[count + dz * xs + x]
                lanes = pl.ds(pl.multiple_of(here * 128, 128), 128)

                def small(begin, end, value):
                    rows_at, lanes_at = small_place(half, begin, end)
                    out[at, y, x, skip + rows_at.start : skip + rows_at.stop, lanes_at] = value.astype(bf16)

                turned = (blocks - y) % blocks
                for begin, end in ((0, min(share, half)), (half, share)):
                    if begin < end:
                        part = slice(turned * share + begin, turned * share + end)
                        small(begin, end, gw2[part, lanes].astype(f32) + gw2_got[part, lanes].astype(f32))
                ahead = lax.rem(table[2 * count] + y, blocks)
                block = pl.ds(pl.multiple_of((here * blocks + ahead) * rows, rows), rows)
                for k in range(HEADP // 128):
                    group = slice(k * 128, (k + 1) * 128)
                    value = gwh[block, group].astype(f32) + gwh_got[block, group].astype(f32)
                    small(share + k * rows, share + (k + 1) * rows, value)
                n = y * xs + x
                some = rows_left[n * each : (n + 1) * each] + [jnp.zeros_like(rows_left[0])] * (EXTRA - each)
                some = jnp.concatenate(some, axis=0).astype(bf16)
                out[at, y, x, skip + half :, :] = some if dz >= 2 else jnp.zeros_like(some)
        if dz >= 2:
            for copy in copies[at * blocks * xs : (at + 1) * blocks * xs]:
                copy.wait()
            pltpu.make_async_copy(far.at[at], stacks[at], small_sems.at[at]).start()
    last = pltpu.make_async_copy(near, near_out, small_sems.at[2])
    last.start()
    for at in range(2):
        pltpu.make_async_copy(far.at[at], stacks[at], small_sems.at[at]).wait()
    last.wait()


def pack(table, lates, gw2, gwh, sums, half, places):
    smem = pl.BlockSpec(memory_space=pltpu.SMEM)
    vmem = pl.BlockSpec(memory_space=pltpu.VMEM)
    away = pl.BlockSpec(memory_space=pl.ANY)
    long, cols = lates[0].shape
    tall = half + EXTRA
    stack = jax.ShapeDtypeStruct((*places, long + tall, cols), bf16)
    return pl.pallas_call(
        pack_kernel,
        in_specs=[smem] + [away] * (len(lates) + 4) + [vmem],
        out_specs=[away] * 3,
        out_shape=[stack, stack, jax.ShapeDtypeStruct((2, *places, tall, cols), bf16)],
        scratch_shapes=[
            pltpu.VMEM((2, *places, tall, cols), bf16),
            pltpu.VMEM((2, *places, long + tall, cols), bf16),
            pltpu.VMEM((2, *gw2[0].shape), bf16),
            pltpu.VMEM((2, *gwh[0].shape), bf16),
            pltpu.SemaphoreType.DMA((len(lates),)),
            pltpu.SemaphoreType.DMA((4,)),
            pltpu.SemaphoreType.DMA((3,)),
        ],
        cost_estimate=LIGHT,
        compiler_params=pltpu.CompilerParams(vmem_limit_bytes=WIDE * MIB),
        name="pack",
    )(table, *lates, *gw2, *gwh, sums)


def gelu(x):
    return 0.5 * x * (1.0 + jnp.tanh(GELU_A * (x + GELU_B * x * x * x)))


def gelu_slope(x):
    t = jnp.tanh(GELU_A * (x + GELU_B * x * x * x))
    return 0.5 * (1.0 + t) + 0.5 * x * (1.0 - t * t) * (GELU_A * (1.0 + 3.0 * GELU_B * x * x))


def kept_count(wh):
    ends = jnp.sum(wh[:, HEADP - 128 :].astype(f32), axis=0, keepdims=True)
    return 128.0 * ends[:, 126:127] + ends[:, 127:128]


def losses(out, flags, kept):
    rows, width = out.shape
    label = flags[:, 0:1].astype(jnp.int32)
    valid = 1.0 - flags[:, 1:2]
    fore = jnp.where(label > 0, valid, 0.0)
    scale = 1.0 / kept
    lane = lax.broadcasted_iota(jnp.int32, flags.shape, 1)
    onehot = jnp.where(lane == label, 1.0, 0.0)
    logits = out[:, : flags.shape[1]]
    masked = jnp.where(lane < CLS, logits, -jnp.inf)
    top = jnp.max(masked, axis=1, keepdims=True)
    shifted = jnp.exp(masked - top)
    total = jnp.sum(shifted, axis=1, keepdims=True)
    cross = jnp.log(total) + top - jnp.sum(onehot * logits, axis=1, keepdims=True)
    col = lax.broadcasted_iota(jnp.int32, out.shape, 1)
    base = CLS + 4 * (label - 1)
    row = jnp.where((col >= base) & (col < base + 4) & (col >= CLS), 1.0, 0.0)
    at = lax.broadcasted_iota(jnp.int32, (width, flags.shape[1]), 0) - CLS
    to = lax.broadcasted_iota(jnp.int32, (width, flags.shape[1]), 1) - 2
    bring = jnp.where((at >= 0) & (at < HEAD - CLS) & ((at & 3) == to), 1.0, 0.0)
    full = functools.partial(lax.dot_general, precision=lax.Precision.HIGHEST, preferred_element_type=f32)
    boxes = full(out * row, bring, (((1,), (0,)), ((), ())))
    error = jnp.where((lane >= 2) & (lane < 6), boxes - flags, 0.0)
    size = jnp.abs(error)
    smooth = jnp.sum(jnp.where(size < 1.0, 0.5 * error * error, size - 0.5 * jnp.where(size > 0.0, 1.0, 0.0)), axis=1, keepdims=True)
    back = full(jnp.clip(error, -1.0, 1.0) * (fore * scale), bring, (((1,), (1,)), ((), ())))
    grad = back * row
    first = (shifted / total - onehot) * (valid * scale) + grad[:, : flags.shape[1]]
    return valid * cross + fore * smooth, jnp.concatenate([first, grad[:, flags.shape[1] :]], axis=1)


def head_blocks_kernel(share, depth, table, *refs):
    stacks, (pre_own, pre_sib, biases, labels, crowd, targets) = refs[: 2 * depth], refs[2 * depth : 2 * depth + 6]
    g_outs, gw2_outs, gwh_outs = refs[2 * depth + 6 : 2 * depth + 8], refs[2 * depth + 8 : 2 * depth + 10], refs[
        2 * depth + 10 : 2 * depth + 12
    ]
    sums, kept_out, small, pres, w2, wh, pre1, h1, pre2, gpre2, gwh, g, gw2, gwhs, bias, in_sems, out_sems = refs[
        2 * depth + 12 :
    ]
    rows, units = pre_own.shape
    blocks, xs, half, _ = small.shape[1:]
    count = depth * xs
    each = HID // (count * blocks * CORES)
    copies = [
        pltpu.make_async_copy(ref.at[:, :, pl.ds(ref.shape[2] - half, half)], small.at[n], in_sems.at[n])
        for n, ref in enumerate(stacks)
    ]
    early = [pltpu.make_async_copy(ref, pres.at[n], in_sems.at[2 * depth + n]) for n, ref in enumerate((pre_own, pre_sib))]
    for copy in early + copies:
        copy.start()
    core = table[2 * count + 1]
    for copy in early:
        copy.wait()
    for side, pre in enumerate((pres.at[0], pres.at[1])):
        for k in range(blocks):
            unit = table[2 * count + 2 + side * blocks + k]
            lanes = slice(side * units + k * share, side * units + (k + 1) * share)
            first_bias = biases[:, pl.ds(pl.multiple_of(unit * share, share), share)]
            pre1[:, lanes] = pre[:, k * share : (k + 1) * share] + first_bias
        lanes = slice(side * units, (side + 1) * units)
        h1[:, lanes] = gelu(pre1[:, lanes]).astype(bf16)
    for copy in copies:
        copy.wait()
    for n in range(count):
        at = table[n]
        lanes = pl.ds(pl.multiple_of(at * 128, 128), 128)
        for y in range(blocks):
            turned = lax.rem(table[2 * count] + blocks - y, blocks)
            for side in range(CORES):

                def piece(begin, end):
                    rows_at, lanes_at = small_place(half, begin, end)
                    return small[side * depth + n // xs, y, n % xs, rows_at, lanes_at]

                for begin, end in ((0, min(share, half)), (half, share)):
                    if begin < end:
                        w2[side, y * share + begin : y * share + end, lanes] = piece(begin, end)
                owner = core if side == 0 else 1 - core
                to = pl.multiple_of(((at * blocks + turned) * CORES + owner) * each, each)
                for k in range(HEADP // 128):
                    wh[pl.ds(to, each), k * 128 : (k + 1) * 128] = piece(share + k * each, share + (k + 1) * each)
    bias[...] = jnp.zeros_like(bias)
    bias[:, :HEAD] = biases[:, 2 * HID :]
    pre2[...] = jnp.zeros_like(pre2) + biases[:, HID : 2 * HID]
    for side in range(CORES):
        for k in range(0, units, share):
            part = dot(h1[:, side * units + k : side * units + k + share], w2[side, k : k + share, :])
            pre2[...] += part.astype(bf16).astype(f32)
    h2 = gelu(pre2[...]).astype(bf16)
    out = dot(h2, wh[...]) + bias[...]
    flags = jnp.concatenate([labels[...], crowd[...]], axis=0).astype(f32)
    flags = jnp.concatenate([flags, targets[...].astype(f32), jnp.zeros((122, rows), f32)], axis=0)
    flags = jnp.transpose(flags)
    kept = kept_count(wh)
    kept_out[...] = kept
    row_loss, grad = losses(out, flags, kept)
    g_out = grad.astype(bf16)
    g_h2 = dot(g_out, wh[...], ((1,), (1,)))
    g2 = (g_h2 * gelu_slope(pre2[...])).astype(bf16)
    gpre2[...] = g2
    sums[:, HID : 2 * HID] = jnp.sum(g2.astype(f32), axis=0, keepdims=True)
    sent = []
    for side in (1, 0):
        lanes = slice(side * units, (side + 1) * units)
        g_h1 = dot(gpre2[...], w2[side], ((1,), (1,)))
        g[side] = (g_h1 * gelu_slope(pre1[:, lanes])).astype(bf16)
        sent.append(pltpu.make_async_copy(g.at[side], g_outs[side], out_sems.at[side]))
        sent[-1].start()
    for side in (1, 0):
        lanes = slice(side * units, (side + 1) * units)
        gw2[side] = dot(h1[:, lanes], gpre2[...], ((0,), (0,))).astype(bf16)
        sent.append(pltpu.make_async_copy(gw2.at[side], gw2_outs[side], out_sems.at[CORES + side]))
        sent[-1].start()
    gwh[...] = dot(h2, g_out, ((0,), (0,)))
    for n in range(count * blocks):
        for side in (1, 0):
            owner = core if side == 0 else 1 - core
            row = pl.multiple_of((n * CORES + owner) * each, each)
            gwhs[side, n * each : (n + 1) * each, :] = gwh[pl.ds(row, each), :].astype(bf16)
    for side in (1, 0):
        sent.append(pltpu.make_async_copy(gwhs.at[side], gwh_outs[side], out_sems.at[2 * CORES + side]))
        sent[-1].start()
    for side in range(CORES):
        columns = jnp.sum(g[side].astype(f32), axis=0, keepdims=True)
        for k in range(blocks):
            unit = table[2 * count + 2 + side * blocks + k]
            sums[:, pl.ds(pl.multiple_of(unit * share, share), share)] = columns[:, k * share : (k + 1) * share]
    head_sums = jnp.sum(g_out.astype(f32), axis=0, keepdims=True)
    lane = lax.broadcasted_iota(jnp.int32, head_sums.shape, 1)
    loss = jnp.sum(row_loss, axis=0, keepdims=True)
    sums[:, 2 * HID : 2 * HID + HEADP] = jnp.where(lane == HEAD, loss, head_sums)
    for copy in sent:
        copy.wait()


def heads_blocks(share, half, table, own, sib, pre_own, pre_sib, biases, labels, crowd, targets):
    rows, units = pre_own.shape
    depth = len(own)
    blocks, xs, _, cols = own[0].shape
    smem = pl.BlockSpec(memory_space=pltpu.SMEM)
    vmem = pl.BlockSpec(memory_space=pltpu.VMEM)
    away = pl.BlockSpec(memory_space=pl.ANY)
    shape = jax.ShapeDtypeStruct
    return pl.pallas_call(
        functools.partial(head_blocks_kernel, share, depth),
        in_specs=[smem] + [away] * (2 * depth + 2) + [vmem] * 4,
        out_specs=[away] * 6 + [vmem] * 2,
        out_shape=[shape((rows, units), bf16)] * 2
        + [shape((units, HID), bf16)] * 2
        + [shape((HID // CORES, HEADP), bf16)] * 2
        + [shape((1, 2 * HID + HEADP), f32), shape((1, 1), f32)],
        scratch_shapes=[
            pltpu.VMEM((2 * depth, blocks, xs, half, cols), bf16),
            pltpu.VMEM((CORES, rows, units), f32),
            pltpu.VMEM((CORES, units, HID), bf16),
            pltpu.VMEM((HID, HEADP), bf16),
            pltpu.VMEM((rows, HID), f32),
            pltpu.VMEM((rows, HID), bf16),
            pltpu.VMEM((rows, HID), f32),
            pltpu.VMEM((rows, HID), bf16),
            pltpu.VMEM((HID, HEADP), f32),
            pltpu.VMEM((CORES, rows, units), bf16),
            pltpu.VMEM((CORES, units, HID), bf16),
            pltpu.VMEM((CORES, HID // CORES, HEADP), bf16),
            pltpu.VMEM((1, HEADP), f32),
            pltpu.SemaphoreType.DMA((2 * depth + 2,)),
            pltpu.SemaphoreType.DMA((3 * CORES,)),
        ],
        compiler_params=pltpu.CompilerParams(vmem_limit_bytes=WIDE * MIB),
        cost_estimate=LIGHT,
        name="heads",
    )(table, *own, *sib, pre_own, pre_sib, biases, labels, crowd, targets)


def head_kernel(
    share,
    wide,
    at_ref,
    pre_own,
    pre_sib,
    w2_own,
    w2_sib,
    wh,
    b1,
    b2,
    bh,
    tags,
    g_own,
    g_sib,
    gw2_own,
    gw2_sib,
    gwh_own,
    gwh_sib,
    sums,
    count,
    h1,
    pre2,
    gpre2,
    gwh,
):
    rows, units = pre_own.shape
    sides = ((pre_own, w2_own, g_own, gw2_own, 0), (pre_sib, w2_sib, g_sib, gw2_sib, units))
    pre2[...] = jnp.zeros_like(pre2) + b2[...]
    for pre, w2, _, _, at in sides:
        h1[:, at : at + units] = gelu(pre[...] + b1[:, at : at + units]).astype(bf16)
        for k in range(0, units, share):
            part = dot(h1[:, at + k : at + k + share], w2[k : k + share, :])
            pre2[...] += part.astype(bf16).astype(f32)
    h2 = gelu(pre2[...]).astype(bf16)
    out = dot(h2, wh[...]) + bh[...]
    kept = kept_count(wh)
    count[...] = kept
    row_loss, grad = losses(out, tags[...], kept)
    g_out = grad.astype(bf16)
    head_sums = jnp.sum(g_out.astype(f32), axis=0, keepdims=True)
    lane = lax.broadcasted_iota(jnp.int32, head_sums.shape, 1)
    loss = jnp.sum(row_loss, axis=0, keepdims=True)
    sums[:, 2 * HID : 2 * HID + HEADP] = jnp.where(lane == HEAD, loss, head_sums)
    gwh[...] = dot(h2, g_out, ((0,), (0,)))
    each = HID // (HID // share * wide)
    for side in range(CORES):

        @pl.when(at_ref[HID // share] == side)
        def _(side=side):
            for n in range(HID // each // CORES):
                for c, part in ((side, gwh_own), (1 - side, gwh_sib)):
                    row = (n * CORES + c) * each
                    part[n * each : (n + 1) * each, :] = gwh[row : row + each, :].astype(bf16)

    g_h2 = dot(g_out, wh[...], ((1,), (1,)))
    g2 = (g_h2 * gelu_slope(pre2[...])).astype(bf16)
    sums[:, HID : 2 * HID] = jnp.sum(g2.astype(f32), axis=0, keepdims=True)
    gpre2[...] = g2
    for n, (pre, w2, g1, gw2, at) in enumerate(sides):
        g_h1 = dot(gpre2[...], w2[...], ((1,), (1,)))
        g = (g_h1 * gelu_slope(pre[...] + b1[:, at : at + units])).astype(bf16)
        g1[...] = g
        columns = jnp.sum(g.astype(f32), axis=0, keepdims=True)
        for k in range(units // share):
            to = pl.multiple_of(at_ref[n * (units // share) + k] * share, share)
            sums[:, pl.ds(to, share)] = columns[:, k * share : (k + 1) * share]
        gw2[...] = dot(h1[:, at : at + units], gpre2[...], ((0,), (0,))).astype(gw2.dtype)


def heads_step(share, wide, at, pre_own, pre_sib, w2_own, w2_sib, wh, b1, b2, bh, tags):
    rows, units = pre_own.shape
    vmem = pl.BlockSpec(memory_space=pltpu.VMEM)
    shape = jax.ShapeDtypeStruct
    return pl.pallas_call(
        functools.partial(head_kernel, share, wide),
        in_specs=[pl.BlockSpec(memory_space=pltpu.SMEM)] + [vmem] * 9,
        out_specs=[vmem] * 8,
        out_shape=[
            shape((rows, units), bf16),
            shape((rows, units), bf16),
            shape((units, HID), bf16),
            shape((units, HID), bf16),
            shape((HID // CORES, HEADP), bf16),
            shape((HID // CORES, HEADP), bf16),
            shape((1, 2 * HID + HEADP), f32),
            shape((1, 1), f32),
        ],
        scratch_shapes=[
            pltpu.VMEM((rows, HID), bf16),
            pltpu.VMEM((rows, HID), f32),
            pltpu.VMEM((rows, HID), bf16),
            pltpu.VMEM((HID, HEADP), f32),
        ],
        compiler_params=pltpu.CompilerParams(vmem_limit_bytes=WIDE * MIB),
        cost_estimate=LIGHT,
        name="heads",
    )(at, pre_own, pre_sib, w2_own, w2_sib, wh, b1, b2, bh, tags)


class Grid:
    def __init__(self):
        self.wide = lax.axis_size("wide")
        self.tp = lax.axis_size("tp")
        self.y = self.tp // CORES
        self.x = self.y if self.wide % self.y == 0 else 1
        self.z = self.wide // self.x
        self.size = {"z": self.z, "x": self.x, "y": self.y, "c": CORES}
        wide, tp = lax.axis_index("wide"), lax.axis_index("tp")
        self.at = {"z": wide // self.x, "x": wide % self.x, "y": tp // CORES, "c": tp % CORES}

    def move(self, value, axis, by):
        pairs = []
        for z in range(self.z):
            for x in range(self.x):
                for y in range(self.y):
                    for c in range(CORES):
                        to = {"z": z, "x": x, "y": y, "c": c}
                        for a in axis:
                            to[a] = (to[a] + by) % self.size[a]
                        pairs.append((self.index(z, x, y, c), self.index(to["z"], to["x"], to["y"], to["c"])))
        return lax.ppermute(value, AXES, pairs)

    def flip(self, value, axis, bit):
        unit = {"c": 1, "y": CORES, "x": CORES * self.y, "z": CORES * self.y * self.x}
        step = bit * sum(unit[a] for a in axis)
        return lax.ppermute(value, AXES, [(i, i ^ step) for i in range(self.wide * self.tp)])

    def index(self, z, x, y, c):
        return ((z * self.x + x) * self.y + y) * CORES + c

    def swap(self, value):
        return self.move(value, "c", 1)


def spread_stacked(grid, value, order):
    stack = value[None, None, None]
    for axis in order:
        place = "zxy".index(axis)
        stack = jnp.concatenate([stack] + [grid.move(stack, axis, by) for by in range(1, grid.size[axis])], axis=place)
    for place, axis in enumerate("zxy"):
        if grid.size[axis] > 1:
            back = (grid.at[axis] - jnp.arange(grid.size[axis])) % grid.size[axis]
            stack = jnp.take(stack, back, axis=place, mode="clip")
    return stack


def collect_stacked(grid, stack, order):
    left = "zxy"
    total = stack
    for axis in order:
        place = left.index(axis)
        total = total.astype(bf16)

        def block(by):
            at = (grid.at[axis] + by) % grid.size[axis]
            return lax.dynamic_index_in_dim(total, at, place, keepdims=False)

        mine = block(0).astype(f32)
        for by in range(1, grid.size[axis]):
            mine = mine + grid.move(block(by), axis, by).astype(f32)
        total = mine
        left = left.replace(axis, "")
    return total


def all_sum(value):
    count = lax.axis_size("wide") * lax.axis_size("tp")
    if count & (count - 1):
        return lax.psum(value, AXES)
    bit = 1
    while bit < count:
        value = value + lax.ppermute(value, AXES, [(i, i ^ bit) for i in range(count)])
        bit *= 2
    return value


def after(value, *others):
    return lax.optimization_barrier((value, *others))[0]


class Links:
    def __init__(self, grid, in_step):
        self.grid = grid
        self.in_step = in_step
        self.last = {}
        self.slots = [{}, {}]

    def next(self):
        self.slots.append({})

    def send(self, value, axis, by=1):
        before = [self.slots[-2]["x"]] if self.in_step and axis == "z" and "x" in self.slots[-2] else []
        if axis in self.last:
            before.append(self.last[axis])
        sent = self.grid.move(after(value, *before) if before else value, axis, by)
        self.last[axis] = self.slots[-1][axis] = sent
        return sent


def adam_update(weight, grad, first, second, rate):
    first_new = decay_one * first + (1.0 - decay_one) * grad
    second_new = decay_two * second + (1.0 - decay_two) * grad * grad
    first_hat = first_new / (1.0 - decay_one**STEP)
    second_hat = second_new / (1.0 - decay_two**STEP)
    weight_new = weight - rate * (first_hat / (jnp.sqrt(second_hat) + epsilon) + weight_decay * weight)
    return (weight_new, first_new, second_new)


def by_blocks(grid, feats, cols, share, second_cols, head_rows, channels, rows):
    return (
        (grid.z, grid.x, grid.y) == (4, 2, 2)
        and feats % 16 == 0
        and feats > max(LATE_OUT, LATE_BACK)
        and cols == channels == 256
        and second_cols == 128
        and (share, head_rows) == (256, 32)
        and rows % (CHUNKS * GROUP) == 0
        and block_span(feats, grid.wide, channels) > 0
    )


def place_table(grid):
    found = []
    for sign in (-1, 1):
        for dz in range(grid.z):
            for dx in range(grid.x):
                z, x = (grid.at["z"] + sign * dz) % grid.z, (grid.at["x"] + sign * dx) % grid.x
                found.append(z * grid.x + x)
    y, core = grid.at["y"], grid.at["c"]
    found += [y, core]
    found += [CORES * ((y + k) % grid.y) + c for c in (core, 1 - core) for k in range(grid.y)]
    return jnp.stack(found).astype(jnp.int32)


def low_sum(first, *others):
    total = first.astype(f32)
    for value in others:
        total = total + value.astype(f32)
    return total.astype(bf16)


def terms(value):
    found = []
    for _ in range(TERMS):
        found.append(lax.optimization_barrier(value.astype(bf16)))
        value = value - found[-1].astype(f32)
    return jnp.concatenate(found, axis=0)


def from_terms(rows):
    count = rows.shape[0] // TERMS
    total = rows[:count].astype(f32)
    for k in range(1, TERMS):
        total = total + rows[k * count : (k + 1) * count].astype(f32)
    return total


def blocks_step(grid, make_crops, w_first, w_second, w_heads, biases, labels, crowd, targets):
    feats, cols = w_first.shape
    share, _ = w_second.shape
    head_rows = w_heads.shape[0]
    table = place_table(grid)
    count = grid.z * grid.x

    links = Links(grid, True)
    most = feats - LATE_OUT
    mine, first_low = prepare(w_first, w_second, w_heads, crowd, most)
    half = mine.shape[0] - feats
    m = {(0, 0, 0): mine}
    stacks = {}

    m[0, 1, 0] = grid.move(mine, "x", 1)
    m[0, 0, 1] = grid.move(mine, "y", 1)
    m[1, 0, 0] = grid.move(first_low, "z", 1)
    own_crops = [make_crops(i) for i in range(CHUNKS)]
    made = own_crops[:EARLY] + [m[key] for key in ((0, 1, 0), (0, 0, 1), (1, 0, 0))]
    m[3, 0, 0] = links.send(after(first_low, m[1, 0, 0]), "z", 3)
    m[1, 1, 0] = links.send(after(m[1, 0, 0], *made), "x")
    m[0, 1, 1] = links.send(after(m[0, 1, 0], *made), "y")
    stacks[0] = jnp.stack([jnp.stack([m[0, x, y][most:] for x in range(grid.x)]) for y in range(grid.y)])
    links.next()
    m[2, 0, 0] = links.send(m[1, 0, 0], "z", 1)
    m[3, 1, 0] = links.send(m[3, 0, 0], "x")
    m[1, 0, 1] = links.send(m[1, 0, 0], "y")
    links.next()
    stacks[1] = links.send(stacks[0], "z", 1)
    m[2, 1, 0] = links.send(m[2, 0, 0], "x")
    m[3, 0, 1] = links.send(m[3, 0, 0], "y")
    links.next()
    stacks[3] = links.send(stacks[0], "z", 3)
    m[1, 1, 1] = links.send(m[1, 0, 1], "x")
    m[2, 0, 1] = links.send(m[2, 0, 0], "y")
    links.next()
    stacks[2] = links.send(stacks[1], "z", 1)
    m[3, 1, 1] = links.send(m[3, 0, 1], "x")
    m[2, 1, 1] = links.send(m[2, 1, 0], "y")
    sib_crops = []
    for chunk in own_crops:
        sib_crops.append(grid.swap(after(chunk, *made)))
    crops = own_crops + sib_crops

    span = block_span(feats, grid.wide, cols)
    both = (0, 1)

    def products(work, before):
        inputs = []
        for dz, dx, ys, kind in work:
            inputs += [m[dz, dx, y] for y in ys if kind != "last"] + [stacks[dz]] * (kind != "most")
        items = tuple((dz * grid.x + dx, dx, ys, kind) for dz, dx, ys, kind in work)
        return first_blocks(table, crops, inputs, items, feats, most, grid.wide, grid.y, before)

    work = [(dz, dx, both, "all") for dz, dx in ((0, 0), (0, 1), (1, 0), (3, 0), (1, 1))]
    first_pre = products(work + [(3, 1, (0,), "all"), (2, 0, both, "most"), (2, 1, (0,), "most")], None)
    work = [(2, 0, both, "last"), (2, 1, both, "last"), (2, 1, (1,), "most"), (3, 1, (1,), "all")]
    pre = products(work, first_pre)
    sib_stacks = {2: grid.swap(after(stacks[2], first_pre[0]))}
    sib_stacks[0] = grid.swap(stacks[0])
    sib_stacks[1] = grid.swap(after(stacks[1], sib_stacks[0]))
    sib_stacks[3] = grid.swap(after(stacks[3], sib_stacks[1], first_pre[0]))
    g_own, g_send, gw2, gw2_send, gwh, gwh_send, sums, roi_count = heads_blocks(
        share,
        half,
        table,
        [stacks[z] for z in range(4)],
        [sib_stacks[z] for z in range(4)],
        pre[0],
        grid.swap(pre[1]),
        biases[None, :],
        labels[None, :],
        crowd[None, :],
        targets.T,
    )

    g_got = grid.swap(g_send)
    m = {}
    parts = {}

    def gradients(keys, wait=()):
        numbers = tuple(count + dz * grid.x + dx for dz, dx in keys)
        outs = first_grad_blocks(after(table, *wait), numbers, crops, g_own, g_got, feats, LATE_BACK, grid.y, span)
        for i, (dz, dx) in enumerate(keys):
            for y in range(grid.y):
                m[dz, dx, y], parts[dz, dx, y] = outs[(i * grid.y + y) * 2 : (i * grid.y + y) * 2 + 2]

    gradients([(2, 1), (2, 0), (3, 1), (3, 0)])
    lates = [parts[dz, dx, y] for dz in (2, 3) for y in range(grid.y) for dx in range(grid.x)]
    packed = pack(
        table,
        lates,
        (gw2, grid.swap(after(gw2_send, g_got))),
        (gwh, grid.swap(after(gwh_send, g_got))),
        sums,
        half,
        (grid.y, grid.x),
    )

    def stack_of(dz):
        if dz >= 2:
            return packed[dz - 2]
        first = jnp.stack([jnp.stack([parts[dz, dx, y] for dx in range(grid.x)]) for y in range(grid.y)])
        return jnp.concatenate([first, packed[2][dz]], axis=2)

    links = Links(grid, False)
    far = stack_of(2)
    gradients([(1, 1), (1, 0), (0, 1), (0, 0)], [far])
    begun = (far, m[3, 1, 1])
    z0 = links.send(after(far, *begun[1:]), "z", 1)
    y0 = links.send(after(m[2, 1, 1], *begun), "y")
    x0 = links.send(after(m[3, 1, 1], *begun[:1]), "x")
    z1 = links.send(stack_of(3), "z", 3)
    y1 = links.send(m[2, 0, 1], "y")
    x1 = links.send(m[3, 1, 0], "x")
    z2 = links.send(low_sum(stack_of(1), z0), "z", 1)
    x2 = links.send(low_sum(m[2, 1, 0], y0), "x")
    y2 = links.send(low_sum(m[3, 0, 1], x0), "y")
    z3 = links.send(low_sum(m[2, 0, 0], x2, y1), "z", 1)
    x3 = links.send(m[1, 1, 1], "x")
    y3 = links.send(m[0, 1, 1], "y")
    z4 = links.send(low_sum(m[3, 0, 0], x1, y2), "z", 3)
    x4 = links.send(m[1, 1, 0], "x")
    y4 = links.send(low_sum(m[1, 0, 1], x3), "y")

    def extra_rows(stack):
        rows = stack[:, :, -EXTRA : 8 - EXTRA].reshape(-1, cols)
        return from_terms(rows[: TERMS * (sums.shape[1] // cols)])

    odd = grid.at["z"] % 2 == 1
    below, above, opposite = extra_rows(z0), extra_rows(z1), extra_rows(z2)
    total = sums.reshape(-1, cols)
    total = (total + jnp.where(odd, below, above)) + (opposite + jnp.where(odd, above, below))
    extra = TERMS * total.shape[0]
    late = low_sum(stack_of(0), z1, z2)
    x5 = links.send(jnp.concatenate([late[:, 1].reshape(-1, cols), terms(total)], axis=0), "x")
    x6 = links.send(low_sum(m[0, 1, 0], y3), "x")
    z5 = links.send(low_sum(m[1, 0, 0], x4, y4, z3), "z", 1)
    y5 = links.send(m[0, 0, 1], "y")
    total = total + from_terms(x5[-extra:])
    late = low_sum(late[:, 0], x5[:-extra].reshape(late[:, 0].shape))
    y6 = links.send(jnp.concatenate([late[1], terms(total)], axis=0), "y")
    total = total + from_terms(y6[-extra:])
    total = total + grid.swap(total)
    sums = total.reshape(1, -1)
    main = m[0, 0, 0].astype(f32)
    for value in (x6, y5, z4, z5):
        main = main + value.astype(f32)
    late = late[0].astype(f32) + y6[:-extra].astype(f32)

    first_total = jnp.concatenate([main, late[:LATE_BACK]], axis=0)
    late = late[LATE_BACK : LATE_BACK + half]
    total = jnp.concatenate([late[:, :128], late[:, 128:]], axis=0)
    heads_total = jnp.concatenate(
        [total[share + k * head_rows : share + (k + 1) * head_rows] for k in range(HEADP // 128)], axis=1
    )[:, :HEAD]
    return roi_count.reshape(()), sums, first_total, total[:share], heads_total


def stacked_step(grid, make_crops, w_first, w_second, w_heads, biases, labels, crowd, targets):
    tags = jnp.concatenate([labels[:, None].astype(f32), crowd[:, None].astype(f32), targets.astype(f32)], axis=1)
    tags = jnp.pad(tags, ((0, 0), (0, 122)))
    feats, cols = w_first.shape
    share, second_cols = w_second.shape
    head_rows = w_heads.shape[0]
    units = HID // CORES
    core = grid.at["c"]
    kept = jnp.sum(1 - crowd)
    head_block = jnp.pad(w_heads, ((0, 0), (0, HEADP - HEAD)))
    spot = (lax.broadcasted_iota(jnp.int32, head_block.shape, 0) == 0) * 1
    lane = lax.broadcasted_iota(jnp.int32, head_block.shape, 1)
    head_block = head_block + (
        spot * (jnp.where(lane == HEADP - 1, kept % 128, 0) + jnp.where(lane == HEADP - 2, kept // 128, 0))
    ).astype(f32)
    small = jnp.concatenate(
        [w_second.astype(bf16).reshape(-1, cols), head_block.astype(bf16).reshape(-1, cols)], axis=0
    )
    second_rows = share * second_cols // cols
    small_all = spread_stacked(grid, small, "zxy").reshape(grid.wide, grid.y, *small.shape)
    weight = spread_stacked(grid, w_first.astype(bf16), "zxy")
    weight = weight.transpose(2, 0, 1, 3, 4).reshape(grid.y, grid.wide * feats, cols)
    crops = [make_crops(i) for i in range(CHUNKS)]
    crops = crops + [grid.swap(c) for c in crops]
    second_own = (
        small_all[:, :, :second_rows]
        .reshape(grid.wide, grid.y, share, second_cols)
        .transpose(1, 2, 0, 3)
        .reshape(units, HID)
    )
    heads_own = small_all[:, :, second_rows:].reshape(grid.wide, grid.y, head_rows, HEADP)
    heads_sib = grid.swap(heads_own)
    head_matrix = jnp.where(
        core == 0, jnp.stack([heads_own, heads_sib], axis=2), jnp.stack([heads_sib, heads_own], axis=2)
    ).reshape(HID, HEADP)
    bias = biases[:HID].reshape(grid.y, CORES, share)
    bias = jnp.where(core == 0, bias, bias[:, ::-1]).transpose(1, 0, 2).reshape(1, -1)
    pre_own, pre_send = first_layer(crops, weight)
    unit_at = [2 * y + c for c in (core, 1 - core) for y in range(grid.y)]
    g_own, g_send, gw2_own, gw2_send, gwh, gwh_send, sums, roi_count = heads_step(
        share,
        grid.wide,
        jnp.stack([jnp.asarray(v) for v in unit_at + [core]]).astype(jnp.int32),
        pre_own,
        grid.swap(pre_send),
        second_own,
        grid.swap(second_own),
        head_matrix,
        bias,
        biases[HID : 2 * HID].reshape(1, -1),
        jnp.pad(biases[2 * HID :], (0, HEADP - HEAD)).reshape(1, -1),
        tags,
    )
    grad = first_grad(crops, g_own, grid.swap(g_send), grid.y)
    grad = grad.reshape(grid.y, grid.wide, feats, cols).transpose(1, 0, 2, 3)
    first_total = collect_stacked(grid, grad.reshape(grid.z, grid.x, grid.y, feats, cols), "yxz")
    gw2 = gw2_own.astype(f32) + grid.swap(gw2_send).astype(f32)
    gwh = gwh.astype(f32) + grid.swap(gwh_send).astype(f32)
    gw2 = gw2.astype(bf16).reshape(grid.y, share, grid.wide, second_cols).transpose(2, 0, 1, 3)
    small_grad = jnp.concatenate(
        [
            gw2.reshape(grid.wide, grid.y, second_rows, cols),
            gwh.astype(bf16).reshape(grid.wide, grid.y, -1, cols),
        ],
        axis=2,
    ).reshape(grid.z, grid.x, grid.y, -1, cols)
    small_total = collect_stacked(grid, small_grad, "yxz")
    second_total = small_total[:second_rows].reshape(share, second_cols)
    heads_total = small_total[second_rows:].reshape(head_rows, HEADP)[:, :HEAD]
    sums = all_sum(sums)
    return roi_count.reshape(()), sums, first_total, second_total, heads_total


def shards(
    maps,
    roi_image,
    roi_level,
    roi_corner,
    roi_weights,
    crowd,
    labels,
    box_targets,
    w_first,
    m_first,
    v_first,
    w_second,
    m_second,
    v_second,
    w_heads,
    m_heads,
    v_heads,
    biases,
    bias_m,
    bias_v,
):
    grid = Grid()
    rows = crowd.shape[0]

    images, levels, height, width, channels = maps.shape
    base = ((roi_image * levels + roi_level) * height + roi_corner[:, 0]).astype(jnp.int32)
    col = roi_corner[:, 1].astype(jnp.int32)
    flat_maps = maps.reshape(images * levels * height, width, channels)
    padded = jnp.pad(roi_weights, ((0, 0), (0, 0), (0, 1), (0, 0)))
    row_w = padded[:, 0].reshape(rows * 8, WIN)
    col_w = padded[:, 1].reshape(rows * 8, WIN)
    step = rows // CHUNKS
    def make_crops(i, *wait):
        return window_crops(flat_maps, after(base, *wait) if wait else base, col, row_w, col_w, i * step, step)

    shapes = (*w_first.shape, *w_second.shape, w_heads.shape[0], channels, rows)
    run = blocks_step if by_blocks(grid, *shapes) else stacked_step
    roi_count, sums, first_total, second_total, heads_total = run(
        grid, make_crops, w_first, w_second, w_heads, biases, labels, crowd, box_targets
    )
    loss_total = sums[0, 2 * HID + HEAD]
    bias_grad = sums[0, : 2 * HID + HEAD]

    first_out = adam_update(w_first, first_total, m_first, v_first, rate_first)
    second_out = adam_update(w_second, second_total, m_second, v_second, rate_second)
    heads_out = adam_update(w_heads, heads_total, m_heads, v_heads, rate_heads)
    bias_out = adam_update(biases, bias_grad, bias_m, bias_v, rate_biases)
    return (loss_total, roi_count, *first_out, *second_out, *heads_out, *bias_out)


def solution(mesh):
    rows = P(("wide", "tp"))
    both = P("wide", "tp")
    turned = P("tp", "wide")
    return jax.shard_map(
        shards,
        mesh=mesh,
        in_specs=(rows,) * 8 + (both,) * 3 + (turned,) * 3 + (rows,) * 3 + (P(),) * 3,
        out_specs=(P(), P()) + (both,) * 3 + (turned,) * 3 + (rows,) * 3 + (P(),) * 3,
        check_vma=False,
    )
```

```python
import functools

import jax
import jax.numpy as jnp
import numpy as np
from jax import lax
from jax.experimental import pallas as pl
from jax.experimental.pallas import tpu as pltpu
from jax.sharding import PartitionSpec as P

HID = 1024
CLS = 81
POOL = 7
CELLS = POOL * POOL
WIN = 16
STEP = 10
HEAD = 401
HEADP = 512
CORES = 2
CHUNKS = 8
EARLY = 4
GROUP = 32
KSTEP = 7
LATE_OUT = 192
LATE_BACK = 208
TERMS = 3
EXTRA = 16
WIDE = 60
MIB = 2**20
LIGHT = pl.CostEstimate(flops=0, bytes_accessed=1024, transcendentals=0)

AXES = ("wide", "tp")
rate_first = 0.02
rate_second = 0.06
rate_heads = 0.06
rate_biases = 0.3
decay_one = 0.9
decay_two = 0.999
epsilon = 1e-08
weight_decay = 0.1
GELU_A = 0.7978845608028654
GELU_B = 0.044715

f32 = jnp.float32
bf16 = jnp.bfloat16


def dot(a, b, contract=((1,), (0,))):
    return lax.dot_general(a, b, (contract, ((), ())), preferred_element_type=f32)


def crop_kernel(first, base_ref, col_ref, maps_ref, wr_ref, wc_ref, rep_ref, tile_ref, *refs):
    out_ref, rows_s, cols_s, left, right = refs
    step = pl.program_id(0)
    lanes = rows_s.shape[1]
    halves = (left, right)
    rows_s[...] = dot(wr_ref[...], rep_ref[...])
    cols_s[...] = dot(wc_ref[...], tile_ref[...])

    def one(i, carry):
        r = first + step * GROUP + i
        at = pl.multiple_of(i * 8, 8)
        rows = rows_s[pl.ds(at, 8), :]
        x0 = col_ref[r]
        cols = jnp.concatenate(
            [pltpu.roll(cols_s[pl.ds(at, 8), k : k + 128], x0, 1) for k in range(0, lanes, 128)], axis=1
        )
        both = jnp.concatenate([rows[a : a + 1, :] * cols for a in range(POOL)], axis=0)
        high = both.astype(bf16)
        low = (both - high.astype(f32)).astype(bf16)
        window = maps_ref[pl.ds(base_ref[r], WIN), :, :].reshape(lanes, maps_ref.shape[2])
        got = dot(jnp.concatenate([high, low], axis=0), window)
        got = got[: POOL * 8] + got[POOL * 8 :]
        for h, half in enumerate(halves):
            half[pl.ds(pl.multiple_of(i * POOL * 8, 8), POOL * 8), :] = got[:, h * 128 : (h + 1) * 128]
        return carry

    lax.fori_loop(0, GROUP, one, 0, unroll=8)
    for a in range(POOL):
        for b in range(POOL):
            for h, half in enumerate(halves):
                out_ref[a * POOL + b, :, h * 128 : (h + 1) * 128] = half[
                    pl.ds(a * 8 + b, GROUP, stride=POOL * 8), :
                ].astype(bf16)


def window_crops(maps, base, col, wr, wc, first, count):
    rows, width, channels = maps.shape
    lanes = WIN * width
    lane = np.arange(lanes)[None]
    unit = np.arange(WIN)[:, None]
    rep = jnp.asarray(lane // width == unit, bf16)
    til = jnp.asarray(lane % width == unit, bf16)
    return pl.pallas_call(
        functools.partial(crop_kernel, first),
        grid_spec=pltpu.PrefetchScalarGridSpec(
            num_scalar_prefetch=2,
            grid=(count // GROUP,),
            in_specs=[
                pl.BlockSpec(maps.shape, lambda i, *_: (0, 0, 0)),
                pl.BlockSpec((GROUP * 8, WIN), lambda i, *_: (first // GROUP + i, 0)),
                pl.BlockSpec((GROUP * 8, WIN), lambda i, *_: (first // GROUP + i, 0)),
                pl.BlockSpec(rep.shape, lambda i, *_: (0, 0)),
                pl.BlockSpec(til.shape, lambda i, *_: (0, 0)),
            ],
            out_specs=pl.BlockSpec((CELLS, GROUP, channels), lambda i, *_: (0, i, 0)),
            scratch_shapes=[
                pltpu.VMEM((GROUP * 8, lanes), f32),
                pltpu.VMEM((GROUP * 8, lanes), f32),
                pltpu.VMEM((GROUP * POOL * 8, 128), f32),
                pltpu.VMEM((GROUP * POOL * 8, 128), f32),
            ],
        ),
        out_shape=jax.ShapeDtypeStruct((CELLS, count, channels), bf16),
        compiler_params=pltpu.CompilerParams(vmem_limit_bytes=18 * MIB),
        cost_estimate=LIGHT,
        name="crops",
    )(base, col, maps, wr, wc, rep, til)


def first_kernel(parts, *refs):
    crops, weight, own, send = refs[:parts], refs[parts], refs[parts + 1], refs[parts + 2]
    step = pl.program_id(0)
    blocks, depth, cols = weight.shape
    channels = crops[0].shape[2]

    @pl.when(step == 0)
    def _():
        own[...] = jnp.zeros_like(own)
        send[...] = jnp.zeros_like(send)

    for out, refs_half in ((own, crops[: parts // 2]), (send, crops[parts // 2 :])):
        lhs = jnp.concatenate(
            [jnp.concatenate([ref[j] for ref in refs_half], axis=0) for j in range(depth // channels)], axis=1
        )
        for y in range(blocks):
            out[:, y * cols : (y + 1) * cols] += dot(lhs, weight[y])


def first_layer(crops, weight):
    parts = len(crops)
    blocks, feats, cols = weight.shape
    channels = crops[0].shape[2]
    rows = sum(c.shape[1] for c in crops) // 2
    return pl.pallas_call(
        functools.partial(first_kernel, parts),
        grid=(CELLS // KSTEP,),
        in_specs=[pl.BlockSpec((KSTEP,) + c.shape[1:], lambda i: (i, 0, 0)) for c in crops]
        + [pl.BlockSpec((blocks, KSTEP * channels, cols), lambda i: (0, i, 0))],
        out_specs=[pl.BlockSpec((rows, blocks * cols), lambda i: (0, 0))] * 2,
        out_shape=[jax.ShapeDtypeStruct((rows, blocks * cols), f32)] * 2,
        compiler_params=pltpu.CompilerParams(vmem_limit_bytes=60 * MIB),
        cost_estimate=LIGHT,
        name="first_layer",
    )(*crops, weight)


def first_grad_kernel(parts, cols, *refs):
    crops, own, got, out = refs[:parts], refs[parts], refs[parts + 1], refs[parts + 2]
    channels = crops[0].shape[2]
    grads = jnp.concatenate([own[...], got[...]], axis=0)
    for j in range(crops[0].shape[0]):
        lhs = jnp.concatenate([ref[j] for ref in crops], axis=0)
        res = dot(lhs, grads, ((0,), (0,))).astype(bf16)
        for y in range(out.shape[0]):
            out[y, j * channels : (j + 1) * channels, :] = res[:, y * cols : (y + 1) * cols]


def first_grad(crops, own, got, blocks):
    parts = len(crops)
    rows, units = own.shape
    cols = units // blocks
    channels = crops[0].shape[2]
    return pl.pallas_call(
        functools.partial(first_grad_kernel, parts, cols),
        grid=(CELLS // KSTEP,),
        in_specs=[pl.BlockSpec((KSTEP,) + c.shape[1:], lambda i: (i, 0, 0)) for c in crops]
        + [pl.BlockSpec((rows, units), lambda i: (0, 0))] * 2,
        out_specs=pl.BlockSpec((blocks, KSTEP * channels, cols), lambda i: (0, i, 0)),
        out_shape=jax.ShapeDtypeStruct((blocks, CELLS * channels, cols), bf16),
        compiler_params=pltpu.CompilerParams(vmem_limit_bytes=60 * MIB),
        cost_estimate=LIGHT,
        name="first_grad",
    )(*crops, own, got)


def block_span(feats, wide, channels):
    span = max(-(-((w * feats) % channels + feats) // channels) for w in range(wide))
    return span if all(w * feats // channels + span <= CELLS for w in range(wide)) else 0


def cell_copies(crops, start, span, cells, sems):
    found = []
    at = 0
    for n, ref in enumerate(crops):
        rows = ref.shape[1]
        found.append(pltpu.make_async_copy(ref.at[pl.ds(start, span)], cells.at[:, pl.ds(at, rows)], sems.at[n]))
        at += rows
    return found


def rows_of(kind, feats, most):
    return {"all": (0, feats), "most": (0, most), "last": (most, feats)}[kind]


def kind_span(kind, feats, most, wide, channels):
    begin, end = rows_of(kind, feats, most)
    return max(-(-((w * feats + begin) % channels + end - begin) // channels) for w in range(wide))


def block_kernel(items, feats, most, wide, parts, fresh, table, *refs):
    count = len(items)
    crops, rest = refs[:parts], refs[parts:]
    own, send, pad, cells, sems = rest[-5:]
    before, inputs = (None, rest[:-5]) if fresh else (rest[:2], rest[2:-5])
    step = pl.program_id(0)
    rows = own.shape[0]
    channels = cells.shape[3]
    cols = channels
    needs = [len(item[2]) * (item[3] != "last") + (item[3] != "most") for item in items]
    spans = [kind_span(item[3], feats, most, wide, channels) for item in items]

    def copies(i):
        slot = i % 2
        number, side, ys, kind = items[i]
        begin, end = rows_of(kind, feats, most)
        start = table[number] * feats + begin
        cell = jnp.minimum(start // channels, CELLS - spans[i])
        at = pl.multiple_of(start - cell * channels, 16)
        found = cell_copies(crops, cell, spans[i], cells.at[slot, pl.ds(0, spans[i])], sems.at[slot])
        group = inputs[sum(needs[:i]) : sum(needs[: i + 1])]
        for k, y in enumerate(ys):
            lanes = pl.ds(y * cols, cols)
            if kind != "last":
                source = group[k].at[pl.ds(0, most)]
                found.append(
                    pltpu.make_async_copy(source, pad.at[slot, pl.ds(at, most), lanes], sems.at[slot, parts + 2 * k])
                )
            if kind != "most":
                source = group[-1].at[y, side, pl.ds(0, feats - most)]
                to = pl.ds(pl.multiple_of(at + most - begin, 16), feats - most)
                found.append(pltpu.make_async_copy(source, pad.at[slot, to, lanes], sems.at[slot, parts + 1 + 2 * k]))
        return found

    def edges(i):
        begin, end = rows_of(items[i][3], feats, most)
        deep = spans[i] * channels
        low = (end - begin) // channels * channels
        lanes = pad.shape[2]
        if low:
            pad[i % 2, :channels, :] = jnp.zeros((channels, lanes), bf16)
        pad[i % 2, low:deep, :] = jnp.zeros((deep - low, lanes), bf16)

    @pl.when(step == 0)
    def _():
        edges(0)
        for copy in copies(0):
            copy.start()
        if fresh:
            own[...] = jnp.zeros_like(own)
            send[...] = jnp.zeros_like(send)
        else:
            own[...] = before[0][...]
            send[...] = before[1][...]

    for i in range(count):

        @pl.when(step == i)
        def _(i=i):
            if i + 1 < count:
                edges(i + 1)
                for copy in copies(i + 1):
                    copy.start()
            for copy in copies(i):
                copy.wait()

    slot = lax.rem(step, 2)
    forms = [(span, item[2]) for span, item in zip(spans, items)]
    for form in sorted(set(forms)):
        span, ys = form
        lanes = slice(ys[0] * cols, (ys[-1] + 1) * cols)

        @pl.when(functools.reduce(jnp.logical_or, [step == i for i in range(count) if forms[i] == form]))
        def _(span=span, lanes=lanes):
            lhs = jnp.concatenate([cells[slot, j] for j in range(span)], axis=1)
            got = dot(lhs, pad[slot, : span * channels, lanes])
            own[:, lanes] += got[:rows]
            send[:, lanes] += got[rows:]


def whole(shape):
    return pl.BlockSpec(shape, lambda i, place: (0,) * len(shape))


def first_blocks(table, crops, inputs, items, feats, most, wide, blocks, before):
    rows = sum(c.shape[1] for c in crops) // 2
    channels = crops[0].shape[2]
    units = blocks * channels
    lead = [] if before is None else list(before)
    away = pl.BlockSpec(memory_space=pl.ANY)
    parts = len(crops)
    span = kind_span("all", feats, most, wide, channels)
    return pl.pallas_call(
        functools.partial(block_kernel, items, feats, most, wide, parts, before is None),
        grid_spec=pltpu.PrefetchScalarGridSpec(
            num_scalar_prefetch=1,
            grid=(len(items),),
            in_specs=[away] * parts + [whole((rows, units))] * len(lead) + [away] * len(inputs),
            out_specs=[whole((rows, units))] * 2,
            scratch_shapes=[
                pltpu.VMEM((2, span * channels, units), bf16),
                pltpu.VMEM((2, span, 2 * rows, channels), bf16),
                pltpu.SemaphoreType.DMA((2, parts + 2 * blocks)),
            ],
        ),
        out_shape=[jax.ShapeDtypeStruct((rows, units), f32)] * 2,
        input_output_aliases={} if before is None else {1 + parts: 0, 2 + parts: 1},
        compiler_params=pltpu.CompilerParams(vmem_limit_bytes=WIDE * MIB),
        cost_estimate=LIGHT,
        name="first_blocks",
    )(table, *crops, *lead, *inputs)


def block_grad_kernel(span, numbers, feats, blocks, parts, table, *refs):
    crops, (own, got), rest = refs[:parts], refs[parts : parts + 2], refs[parts + 2 :]
    outs, (full, cells, in_sems, out_sems) = rest[:-4], rest[-4:]
    step = pl.program_id(0)
    count = len(outs) // (2 * blocks)
    channels = cells.shape[3]
    cols = full.shape[2] // blocks

    def loads(i):
        return cell_copies(crops, (table[numbers[i]] * feats) // channels, span, cells.at[i % 2], in_sems.at[i % 2])

    def stores(i):
        at = pl.multiple_of((table[numbers[i]] * feats) % channels, 16)
        found = []
        for y in range(blocks):
            main, late = outs[(i * blocks + y) * 2], outs[(i * blocks + y) * 2 + 1]
            most = main.shape[0]
            lanes = pl.ds(y * cols, cols)
            found.append(pltpu.make_async_copy(full.at[i % 2, pl.ds(at, most), lanes], main, out_sems.at[i % 2, 2 * y]))
            found.append(
                pltpu.make_async_copy(
                    full.at[i % 2, pl.ds(pl.multiple_of(at + most, 16), feats - most), lanes],
                    late,
                    out_sems.at[i % 2, 2 * y + 1],
                )
            )
        return found

    @pl.when(step == 0)
    def _():
        for copy in loads(0):
            copy.start()

    for i in range(count):

        @pl.when(step == i)
        def _(i=i):
            if i + 1 < count:
                for copy in loads(i + 1):
                    copy.start()
            for copy in loads(i):
                copy.wait()
            if i >= 2:
                for copy in stores(i - 2):
                    copy.wait()

    slot = lax.rem(step, 2)
    grads = jnp.concatenate([own[...], got[...]], axis=0)
    for j in range(span):
        full[slot, j * channels : (j + 1) * channels, :] = dot(cells[slot, j], grads, ((0,), (0,))).astype(bf16)

    for i in range(count):

        @pl.when(step == i)
        def _(i=i):
            for copy in stores(i):
                copy.start()
            if i == count - 1:
                for k in range(max(0, count - 2), count):
                    for copy in stores(k):
                        copy.wait()


def first_grad_blocks(table, numbers, crops, own, got, feats, late, blocks, span):
    rows, units = own.shape
    channels = crops[0].shape[2]
    cols = units // blocks
    count = len(numbers)
    parts = len(crops)
    outs = [(feats - late, cols), (late, cols)] * (count * blocks)
    away = pl.BlockSpec(memory_space=pl.ANY)
    return pl.pallas_call(
        functools.partial(block_grad_kernel, span, numbers, feats, blocks, parts),
        grid_spec=pltpu.PrefetchScalarGridSpec(
            num_scalar_prefetch=1,
            grid=(count,),
            in_specs=[away] * parts + [whole((rows, units))] * 2,
            out_specs=[away] * len(outs),
            scratch_shapes=[
                pltpu.VMEM((2, span * channels, units), bf16),
                pltpu.VMEM((2, span, 2 * rows, channels), bf16),
                pltpu.SemaphoreType.DMA((2, parts)),
                pltpu.SemaphoreType.DMA((2, 2 * blocks)),
            ],
        ),
        out_shape=[jax.ShapeDtypeStruct(v, bf16) for v in outs],
        compiler_params=pltpu.CompilerParams(vmem_limit_bytes=WIDE * MIB),
        cost_estimate=LIGHT,
        name="first_grad",
    )(table, *crops, own, got)


def small_place(half, begin, end):
    lane = 0 if end <= half else 128
    back = half if lane else 0
    return slice(begin - back, end - back), slice(lane, lane + 128)


def prepare_kernel(first, second, heads, crowd, mine, low, first_s, second_s, heads_s, crowd_s, wide_heads, low_s, in_sems, out_sems):
    feats = first.shape[0]
    share = second.shape[0]
    rows = heads.shape[0]
    half = mine.shape[0] - feats
    most = low.shape[0]
    cuts = [feats * k // 4 // 16 * 16 for k in range(4)] + [feats]
    loads = [
        pltpu.make_async_copy(first.at[pl.ds(a, b - a)], first_s.at[pl.ds(a, b - a)], in_sems.at[k])
        for k, (a, b) in enumerate(zip(cuts, cuts[1:]))
    ]
    others = [
        pltpu.make_async_copy(ref, to, in_sems.at[4 + k])
        for k, (ref, to) in enumerate(((second, second_s), (heads, heads_s), (crowd, crowd_s)))
    ]
    for copy in others + loads:
        copy.start()
    for copy in others:
        copy.wait()
    kept = jnp.sum(1 - crowd_s[...], axis=1, keepdims=True)
    wide_heads[...] = jnp.zeros_like(wide_heads)
    wide_heads[:, :HEAD] = heads_s[...]
    lane = lax.broadcasted_iota(jnp.int32, (rows, 128), 1)
    row = lax.broadcasted_iota(jnp.int32, (rows, 128), 0)
    marks = jnp.where(lane == 127, kept % 128, jnp.where(lane == 126, kept // 128, 0))
    wide_heads[:, HEADP - 128 :] += jnp.where(row == 0, marks, 0).astype(f32)
    for begin, end in ((0, min(share, half)), (half, share)):
        if begin < end:
            at, lanes = small_place(half, begin, end)
            low_s[feats + at.start : feats + at.stop, lanes] = second_s[begin:end, :].astype(bf16)
    for k in range(HEADP // 128):
        at, lanes = small_place(half, share + k * rows, share + (k + 1) * rows)
        low_s[feats + at.start : feats + at.stop, lanes] = wide_heads[:, k * 128 : (k + 1) * 128].astype(bf16)
    stores = []
    for k, (a, b) in enumerate(zip(cuts, cuts[1:])):
        loads[k].wait()
        low_s[a:b, :] = first_s[a:b, :].astype(bf16)
        end = mine.shape[0] if b == feats else b
        stores.append(pltpu.make_async_copy(low_s.at[pl.ds(a, end - a)], mine.at[pl.ds(a, end - a)], out_sems.at[k]))
        stores[-1].start()
    stores.append(pltpu.make_async_copy(low_s.at[pl.ds(0, most)], low, out_sems.at[4]))
    stores[-1].start()
    for copy in stores:
        copy.wait()


def prepare(first, second, heads, crowd, most):
    feats, cols = first.shape
    half = (second.shape[0] + heads.shape[0] * HEADP // 128) // 2
    away = pl.BlockSpec(memory_space=pl.ANY)
    crowd = crowd[None, :]
    return pl.pallas_call(
        prepare_kernel,
        in_specs=[away] * 4,
        out_specs=[away] * 2,
        out_shape=[jax.ShapeDtypeStruct((feats + half, cols), bf16), jax.ShapeDtypeStruct((most, cols), bf16)],
        scratch_shapes=[
            pltpu.VMEM(first.shape, f32),
            pltpu.VMEM(second.shape, f32),
            pltpu.VMEM(heads.shape, f32),
            pltpu.VMEM(crowd.shape, jnp.int32),
            pltpu.VMEM((heads.shape[0], HEADP), f32),
            pltpu.VMEM((feats + half, cols), bf16),
            pltpu.SemaphoreType.DMA((7,)),
            pltpu.SemaphoreType.DMA((5,)),
        ],
        cost_estimate=LIGHT,
        compiler_params=pltpu.CompilerParams(vmem_limit_bytes=WIDE * MIB),
        name="prepare",
    )(first, second, heads, crowd)


def pack_kernel(table, *refs):
    lates, sides, sums = refs[:8], refs[8:12], refs[12]
    stack_two, stack_three, near_out, near, far, gw2s, gwhs, late_sems, in_sems, small_sems = refs[13:]
    gw2, gw2_got, gwh, gwh_got = gw2s.at[0], gw2s.at[1], gwhs.at[0], gwhs.at[1]
    arrive = [
        pltpu.make_async_copy(ref, to, in_sems.at[n]) for n, (ref, to) in enumerate(zip(sides, (gw2, gw2_got, gwh, gwh_got)))
    ]
    for copy in arrive:
        copy.start()
    depth = near.shape[0] + far.shape[0]
    _, blocks, xs, tall, _ = near.shape
    half = tall - EXTRA
    share = gw2.shape[0] // blocks
    count = depth * xs
    rows = gwh.shape[0] // (count * blocks)
    long = lates[0].shape[0]
    stacks = (stack_two, stack_three)
    copies = []
    for d in range(2):
        for y in range(blocks):
            for x in range(xs):
                n = (d * blocks + y) * xs + x
                copies.append(pltpu.make_async_copy(lates[n], far.at[d, y, x, pl.ds(0, long)], late_sems.at[n]))
    for copy in copies:
        copy.start()
    rest = sums[...]
    rows_left = []
    for _ in range(TERMS):
        term = rest.astype(bf16).astype(f32)
        rest = rest - term
        rows_left += [term[:, k : k + 256] for k in range(0, term.shape[1], 256)]
    rows_left += [jnp.zeros_like(rows_left[0])] * (-len(rows_left) % (blocks * xs))
    each = len(rows_left) // (blocks * xs)
    for copy in arrive:
        copy.wait()
    for dz in (2, 3, 1, 0):
        out, at, skip = (far, dz - 2, long) if dz >= 2 else (near, dz, 0)
        for y in range(blocks):
            for x in range(xs):
                here = table[count + dz * xs + x]
                lanes = pl.ds(pl.multiple_of(here * 128, 128), 128)

                def small(begin, end, value):
                    rows_at, lanes_at = small_place(half, begin, end)
                    out[at, y, x, skip + rows_at.start : skip + rows_at.stop, lanes_at] = value.astype(bf16)

                turned = (blocks - y) % blocks
                for begin, end in ((0, min(share, half)), (half, share)):
                    if begin < end:
                        part = slice(turned * share + begin, turned * share + end)
                        small(begin, end, gw2[part, lanes].astype(f32) + gw2_got[part, lanes].astype(f32))
                ahead = lax.rem(table[2 * count] + y, blocks)
                block = pl.ds(pl.multiple_of((here * blocks + ahead) * rows, rows), rows)
                for k in range(HEADP // 128):
                    group = slice(k * 128, (k + 1) * 128)
                    value = gwh[block, group].astype(f32) + gwh_got[block, group].astype(f32)
                    small(share + k * rows, share + (k + 1) * rows, value)
                n = y * xs + x
                some = rows_left[n * each : (n + 1) * each] + [jnp.zeros_like(rows_left[0])] * (EXTRA - each)
                some = jnp.concatenate(some, axis=0).astype(bf16)
                out[at, y, x, skip + half :, :] = some if dz >= 2 else jnp.zeros_like(some)
        if dz >= 2:
            for copy in copies[at * blocks * xs : (at + 1) * blocks * xs]:
                copy.wait()
            pltpu.make_async_copy(far.at[at], stacks[at], small_sems.at[at]).start()
    last = pltpu.make_async_copy(near, near_out, small_sems.at[2])
    last.start()
    for at in range(2):
        pltpu.make_async_copy(far.at[at], stacks[at], small_sems.at[at]).wait()
    last.wait()


def pack(table, lates, gw2, gwh, sums, half, places):
    smem = pl.BlockSpec(memory_space=pltpu.SMEM)
    vmem = pl.BlockSpec(memory_space=pltpu.VMEM)
    away = pl.BlockSpec(memory_space=pl.ANY)
    long, cols = lates[0].shape
    tall = half + EXTRA
    stack = jax.ShapeDtypeStruct((*places, long + tall, cols), bf16)
    return pl.pallas_call(
        pack_kernel,
        in_specs=[smem] + [away] * (len(lates) + 4) + [vmem],
        out_specs=[away] * 3,
        out_shape=[stack, stack, jax.ShapeDtypeStruct((2, *places, tall, cols), bf16)],
        scratch_shapes=[
            pltpu.VMEM((2, *places, tall, cols), bf16),
            pltpu.VMEM((2, *places, long + tall, cols), bf16),
            pltpu.VMEM((2, *gw2[0].shape), bf16),
            pltpu.VMEM((2, *gwh[0].shape), bf16),
            pltpu.SemaphoreType.DMA((len(lates),)),
            pltpu.SemaphoreType.DMA((4,)),
            pltpu.SemaphoreType.DMA((3,)),
        ],
        cost_estimate=LIGHT,
        compiler_params=pltpu.CompilerParams(vmem_limit_bytes=WIDE * MIB),
        name="pack",
    )(table, *lates, *gw2, *gwh, sums)


def gelu(x):
    return 0.5 * x * (1.0 + jnp.tanh(GELU_A * (x + GELU_B * x * x * x)))


def gelu_slope(x):
    t = jnp.tanh(GELU_A * (x + GELU_B * x * x * x))
    return 0.5 * (1.0 + t) + 0.5 * x * (1.0 - t * t) * (GELU_A * (1.0 + 3.0 * GELU_B * x * x))


def kept_count(wh):
    ends = jnp.sum(wh[:, HEADP - 128 :].astype(f32), axis=0, keepdims=True)
    return 128.0 * ends[:, 126:127] + ends[:, 127:128]


def losses(out, flags, kept):
    rows, width = out.shape
    label = flags[:, 0:1].astype(jnp.int32)
    valid = 1.0 - flags[:, 1:2]
    fore = jnp.where(label > 0, valid, 0.0)
    scale = 1.0 / kept
    lane = lax.broadcasted_iota(jnp.int32, flags.shape, 1)
    onehot = jnp.where(lane == label, 1.0, 0.0)
    logits = out[:, : flags.shape[1]]
    masked = jnp.where(lane < CLS, logits, -jnp.inf)
    top = jnp.max(masked, axis=1, keepdims=True)
    shifted = jnp.exp(masked - top)
    total = jnp.sum(shifted, axis=1, keepdims=True)
    cross = jnp.log(total) + top - jnp.sum(onehot * logits, axis=1, keepdims=True)
    col = lax.broadcasted_iota(jnp.int32, out.shape, 1)
    base = CLS + 4 * (label - 1)
    row = jnp.where((col >= base) & (col < base + 4) & (col >= CLS), 1.0, 0.0)
    at = lax.broadcasted_iota(jnp.int32, (width, flags.shape[1]), 0) - CLS
    to = lax.broadcasted_iota(jnp.int32, (width, flags.shape[1]), 1) - 2
    bring = jnp.where((at >= 0) & (at < HEAD - CLS) & ((at & 3) == to), 1.0, 0.0)
    full = functools.partial(lax.dot_general, precision=lax.Precision.HIGHEST, preferred_element_type=f32)
    boxes = full(out * row, bring, (((1,), (0,)), ((), ())))
    error = jnp.where((lane >= 2) & (lane < 6), boxes - flags, 0.0)
    size = jnp.abs(error)
    smooth = jnp.sum(jnp.where(size < 1.0, 0.5 * error * error, size - 0.5 * jnp.where(size > 0.0, 1.0, 0.0)), axis=1, keepdims=True)
    back = full(jnp.clip(error, -1.0, 1.0) * (fore * scale), bring, (((1,), (1,)), ((), ())))
    grad = back * row
    first = (shifted / total - onehot) * (valid * scale) + grad[:, : flags.shape[1]]
    return valid * cross + fore * smooth, jnp.concatenate([first, grad[:, flags.shape[1] :]], axis=1)


def head_blocks_kernel(share, depth, table, *refs):
    stacks, (pre_own, pre_sib, biases, labels, crowd, targets) = refs[: 2 * depth], refs[2 * depth : 2 * depth + 6]
    g_outs, gw2_outs, gwh_outs = refs[2 * depth + 6 : 2 * depth + 8], refs[2 * depth + 8 : 2 * depth + 10], refs[
        2 * depth + 10 : 2 * depth + 12
    ]
    sums, kept_out, small, pres, w2, wh, pre1, h1, pre2, gpre2, gwh, g, gw2, gwhs, bias, in_sems, out_sems = refs[
        2 * depth + 12 :
    ]
    rows, units = pre_own.shape
    blocks, xs, half, _ = small.shape[1:]
    count = depth * xs
    each = HID // (count * blocks * CORES)
    copies = [
        pltpu.make_async_copy(ref.at[:, :, pl.ds(ref.shape[2] - half, half)], small.at[n], in_sems.at[n])
        for n, ref in enumerate(stacks)
    ]
    early = [pltpu.make_async_copy(ref, pres.at[n], in_sems.at[2 * depth + n]) for n, ref in enumerate((pre_own, pre_sib))]
    for copy in early + copies:
        copy.start()
    core = table[2 * count + 1]
    for copy in early:
        copy.wait()
    for side, pre in enumerate((pres.at[0], pres.at[1])):
        for k in range(blocks):
            unit = table[2 * count + 2 + side * blocks + k]
            lanes = slice(side * units + k * share, side * units + (k + 1) * share)
            first_bias = biases[:, pl.ds(pl.multiple_of(unit * share, share), share)]
            pre1[:, lanes] = pre[:, k * share : (k + 1) * share] + first_bias
        lanes = slice(side * units, (side + 1) * units)
        h1[:, lanes] = gelu(pre1[:, lanes]).astype(bf16)
    for copy in copies:
        copy.wait()
    for n in range(count):
        at = table[n]
        lanes = pl.ds(pl.multiple_of(at * 128, 128), 128)
        for y in range(blocks):
            turned = lax.rem(table[2 * count] + blocks - y, blocks)
            for side in range(CORES):

                def piece(begin, end):
                    rows_at, lanes_at = small_place(half, begin, end)
                    return small[side * depth + n // xs, y, n % xs, rows_at, lanes_at]

                for begin, end in ((0, min(share, half)), (half, share)):
                    if begin < end:
                        w2[side, y * share + begin : y * share + end, lanes] = piece(begin, end)
                owner = core if side == 0 else 1 - core
                to = pl.multiple_of(((at * blocks + turned) * CORES + owner) * each, each)
                for k in range(HEADP // 128):
                    wh[pl.ds(to, each), k * 128 : (k + 1) * 128] = piece(share + k * each, share + (k + 1) * each)
    bias[...] = jnp.zeros_like(bias)
    bias[:, :HEAD] = biases[:, 2 * HID :]
    pre2[...] = jnp.zeros_like(pre2) + biases[:, HID : 2 * HID]
    for side in range(CORES):
        for k in range(0, units, share):
            part = dot(h1[:, side * units + k : side * units + k + share], w2[side, k : k + share, :])
            pre2[...] += part.astype(bf16).astype(f32)
    h2 = gelu(pre2[...]).astype(bf16)
    out = dot(h2, wh[...]) + bias[...]
    flags = jnp.concatenate([labels[...], crowd[...]], axis=0).astype(f32)
    flags = jnp.concatenate([flags, targets[...].astype(f32), jnp.zeros((122, rows), f32)], axis=0)
    flags = jnp.transpose(flags)
    kept = kept_count(wh)
    kept_out[...] = kept
    row_loss, grad = losses(out, flags, kept)
    g_out = grad.astype(bf16)
    g_h2 = dot(g_out, wh[...], ((1,), (1,)))
    g2 = (g_h2 * gelu_slope(pre2[...])).astype(bf16)
    gpre2[...] = g2
    sums[:, HID : 2 * HID] = jnp.sum(g2.astype(f32), axis=0, keepdims=True)
    sent = []
    for side in (1, 0):
        lanes = slice(side * units, (side + 1) * units)
        g_h1 = dot(gpre2[...], w2[side], ((1,), (1,)))
        g[side] = (g_h1 * gelu_slope(pre1[:, lanes])).astype(bf16)
        sent.append(pltpu.make_async_copy(g.at[side], g_outs[side], out_sems.at[side]))
        sent[-1].start()
    for side in (1, 0):
        lanes = slice(side * units, (side + 1) * units)
        gw2[side] = dot(h1[:, lanes], gpre2[...], ((0,), (0,))).astype(bf16)
        sent.append(pltpu.make_async_copy(gw2.at[side], gw2_outs[side], out_sems.at[CORES + side]))
        sent[-1].start()
    gwh[...] = dot(h2, g_out, ((0,), (0,)))
    for n in range(count * blocks):
        for side in (1, 0):
            owner = core if side == 0 else 1 - core
            row = pl.multiple_of((n * CORES + owner) * each, each)
            gwhs[side, n * each : (n + 1) * each, :] = gwh[pl.ds(row, each), :].astype(bf16)
    for side in (1, 0):
        sent.append(pltpu.make_async_copy(gwhs.at[side], gwh_outs[side], out_sems.at[2 * CORES + side]))
        sent[-1].start()
    for side in range(CORES):
        columns = jnp.sum(g[side].astype(f32), axis=0, keepdims=True)
        for k in range(blocks):
            unit = table[2 * count + 2 + side * blocks + k]
            sums[:, pl.ds(pl.multiple_of(unit * share, share), share)] = columns[:, k * share : (k + 1) * share]
    head_sums = jnp.sum(g_out.astype(f32), axis=0, keepdims=True)
    lane = lax.broadcasted_iota(jnp.int32, head_sums.shape, 1)
    loss = jnp.sum(row_loss, axis=0, keepdims=True)
    sums[:, 2 * HID : 2 * HID + HEADP] = jnp.where(lane == HEAD, loss, head_sums)
    for copy in sent:
        copy.wait()


def heads_blocks(share, half, table, own, sib, pre_own, pre_sib, biases, labels, crowd, targets):
    rows, units = pre_own.shape
    depth = len(own)
    blocks, xs, _, cols = own[0].shape
    smem = pl.BlockSpec(memory_space=pltpu.SMEM)
    vmem = pl.BlockSpec(memory_space=pltpu.VMEM)
    away = pl.BlockSpec(memory_space=pl.ANY)
    shape = jax.ShapeDtypeStruct
    return pl.pallas_call(
        functools.partial(head_blocks_kernel, share, depth),
        in_specs=[smem] + [away] * (2 * depth + 2) + [vmem] * 4,
        out_specs=[away] * 6 + [vmem] * 2,
        out_shape=[shape((rows, units), bf16)] * 2
        + [shape((units, HID), bf16)] * 2
        + [shape((HID // CORES, HEADP), bf16)] * 2
        + [shape((1, 2 * HID + HEADP), f32), shape((1, 1), f32)],
        scratch_shapes=[
            pltpu.VMEM((2 * depth, blocks, xs, half, cols), bf16),
            pltpu.VMEM((CORES, rows, units), f32),
            pltpu.VMEM((CORES, units, HID), bf16),
            pltpu.VMEM((HID, HEADP), bf16),
            pltpu.VMEM((rows, HID), f32),
            pltpu.VMEM((rows, HID), bf16),
            pltpu.VMEM((rows, HID), f32),
            pltpu.VMEM((rows, HID), bf16),
            pltpu.VMEM((HID, HEADP), f32),
            pltpu.VMEM((CORES, rows, units), bf16),
            pltpu.VMEM((CORES, units, HID), bf16),
            pltpu.VMEM((CORES, HID // CORES, HEADP), bf16),
            pltpu.VMEM((1, HEADP), f32),
            pltpu.SemaphoreType.DMA((2 * depth + 2,)),
            pltpu.SemaphoreType.DMA((3 * CORES,)),
        ],
        compiler_params=pltpu.CompilerParams(vmem_limit_bytes=WIDE * MIB),
        cost_estimate=LIGHT,
        name="heads",
    )(table, *own, *sib, pre_own, pre_sib, biases, labels, crowd, targets)


def head_kernel(
    share,
    wide,
    at_ref,
    pre_own,
    pre_sib,
    w2_own,
    w2_sib,
    wh,
    b1,
    b2,
    bh,
    tags,
    g_own,
    g_sib,
    gw2_own,
    gw2_sib,
    gwh_own,
    gwh_sib,
    sums,
    count,
    h1,
    pre2,
    gpre2,
    gwh,
):
    rows, units = pre_own.shape
    sides = ((pre_own, w2_own, g_own, gw2_own, 0), (pre_sib, w2_sib, g_sib, gw2_sib, units))
    pre2[...] = jnp.zeros_like(pre2) + b2[...]
    for pre, w2, _, _, at in sides:
        h1[:, at : at + units] = gelu(pre[...] + b1[:, at : at + units]).astype(bf16)
        for k in range(0, units, share):
            part = dot(h1[:, at + k : at + k + share], w2[k : k + share, :])
            pre2[...] += part.astype(bf16).astype(f32)
    h2 = gelu(pre2[...]).astype(bf16)
    out = dot(h2, wh[...]) + bh[...]
    kept = kept_count(wh)
    count[...] = kept
    row_loss, grad = losses(out, tags[...], kept)
    g_out = grad.astype(bf16)
    head_sums = jnp.sum(g_out.astype(f32), axis=0, keepdims=True)
    lane = lax.broadcasted_iota(jnp.int32, head_sums.shape, 1)
    loss = jnp.sum(row_loss, axis=0, keepdims=True)
    sums[:, 2 * HID : 2 * HID + HEADP] = jnp.where(lane == HEAD, loss, head_sums)
    gwh[...] = dot(h2, g_out, ((0,), (0,)))
    each = HID // (HID // share * wide)
    for side in range(CORES):

        @pl.when(at_ref[HID // share] == side)
        def _(side=side):
            for n in range(HID // each // CORES):
                for c, part in ((side, gwh_own), (1 - side, gwh_sib)):
                    row = (n * CORES + c) * each
                    part[n * each : (n + 1) * each, :] = gwh[row : row + each, :].astype(bf16)

    g_h2 = dot(g_out, wh[...], ((1,), (1,)))
    g2 = (g_h2 * gelu_slope(pre2[...])).astype(bf16)
    sums[:, HID : 2 * HID] = jnp.sum(g2.astype(f32), axis=0, keepdims=True)
    gpre2[...] = g2
    for n, (pre, w2, g1, gw2, at) in enumerate(sides):
        g_h1 = dot(gpre2[...], w2[...], ((1,), (1,)))
        g = (g_h1 * gelu_slope(pre[...] + b1[:, at : at + units])).astype(bf16)
        g1[...] = g
        columns = jnp.sum(g.astype(f32), axis=0, keepdims=True)
        for k in range(units // share):
            to = pl.multiple_of(at_ref[n * (units // share) + k] * share, share)
            sums[:, pl.ds(to, share)] = columns[:, k * share : (k + 1) * share]
        gw2[...] = dot(h1[:, at : at + units], gpre2[...], ((0,), (0,))).astype(gw2.dtype)


def heads_step(share, wide, at, pre_own, pre_sib, w2_own, w2_sib, wh, b1, b2, bh, tags):
    rows, units = pre_own.shape
    vmem = pl.BlockSpec(memory_space=pltpu.VMEM)
    shape = jax.ShapeDtypeStruct
    return pl.pallas_call(
        functools.partial(head_kernel, share, wide),
        in_specs=[pl.BlockSpec(memory_space=pltpu.SMEM)] + [vmem] * 9,
        out_specs=[vmem] * 8,
        out_shape=[
            shape((rows, units), bf16),
            shape((rows, units), bf16),
            shape((units, HID), bf16),
            shape((units, HID), bf16),
            shape((HID // CORES, HEADP), bf16),
            shape((HID // CORES, HEADP), bf16),
            shape((1, 2 * HID + HEADP), f32),
            shape((1, 1), f32),
        ],
        scratch_shapes=[
            pltpu.VMEM((rows, HID), bf16),
            pltpu.VMEM((rows, HID), f32),
            pltpu.VMEM((rows, HID), bf16),
            pltpu.VMEM((HID, HEADP), f32),
        ],
        compiler_params=pltpu.CompilerParams(vmem_limit_bytes=WIDE * MIB),
        cost_estimate=LIGHT,
        name="heads",
    )(at, pre_own, pre_sib, w2_own, w2_sib, wh, b1, b2, bh, tags)


class Grid:
    def __init__(self):
        self.wide = lax.axis_size("wide")
        self.tp = lax.axis_size("tp")
        self.y = self.tp // CORES
        self.x = self.y if self.wide % self.y == 0 else 1
        self.z = self.wide // self.x
        self.size = {"z": self.z, "x": self.x, "y": self.y, "c": CORES}
        wide, tp = lax.axis_index("wide"), lax.axis_index("tp")
        self.at = {"z": wide // self.x, "x": wide % self.x, "y": tp // CORES, "c": tp % CORES}

    def move(self, value, axis, by):
        pairs = []
        for z in range(self.z):
            for x in range(self.x):
                for y in range(self.y):
                    for c in range(CORES):
                        to = {"z": z, "x": x, "y": y, "c": c}
                        for a in axis:
                            to[a] = (to[a] + by) % self.size[a]
                        pairs.append((self.index(z, x, y, c), self.index(to["z"], to["x"], to["y"], to["c"])))
        return lax.ppermute(value, AXES, pairs)

    def flip(self, value, axis, bit):
        unit = {"c": 1, "y": CORES, "x": CORES * self.y, "z": CORES * self.y * self.x}
        step = bit * sum(unit[a] for a in axis)
        return lax.ppermute(value, AXES, [(i, i ^ step) for i in range(self.wide * self.tp)])

    def index(self, z, x, y, c):
        return ((z * self.x + x) * self.y + y) * CORES + c

    def swap(self, value):
        return self.move(value, "c", 1)


def spread_stacked(grid, value, order):
    stack = value[None, None, None]
    for axis in order:
        place = "zxy".index(axis)
        stack = jnp.concatenate([stack] + [grid.move(stack, axis, by) for by in range(1, grid.size[axis])], axis=place)
    for place, axis in enumerate("zxy"):
        if grid.size[axis] > 1:
            back = (grid.at[axis] - jnp.arange(grid.size[axis])) % grid.size[axis]
            stack = jnp.take(stack, back, axis=place, mode="clip")
    return stack


def collect_stacked(grid, stack, order):
    left = "zxy"
    total = stack
    for axis in order:
        place = left.index(axis)
        total = total.astype(bf16)

        def block(by):
            at = (grid.at[axis] + by) % grid.size[axis]
            return lax.dynamic_index_in_dim(total, at, place, keepdims=False)

        mine = block(0).astype(f32)
        for by in range(1, grid.size[axis]):
            mine = mine + grid.move(block(by), axis, by).astype(f32)
        total = mine
        left = left.replace(axis, "")
    return total


def all_sum(value):
    count = lax.axis_size("wide") * lax.axis_size("tp")
    if count & (count - 1):
        return lax.psum(value, AXES)
    bit = 1
    while bit < count:
        value = value + lax.ppermute(value, AXES, [(i, i ^ bit) for i in range(count)])
        bit *= 2
    return value


def after(value, *others):
    return lax.optimization_barrier((value, *others))[0]


class Links:
    def __init__(self, grid, in_step):
        self.grid = grid
        self.in_step = in_step
        self.last = {}
        self.slots = [{}, {}]

    def next(self):
        self.slots.append({})

    def send(self, value, axis, by=1):
        before = [self.slots[-2]["x"]] if self.in_step and axis == "z" and "x" in self.slots[-2] else []
        if axis in self.last:
            before.append(self.last[axis])
        sent = self.grid.move(after(value, *before) if before else value, axis, by)
        self.last[axis] = self.slots[-1][axis] = sent
        return sent


def adam_update(weight, grad, first, second, rate):
    first_new = decay_one * first + (1.0 - decay_one) * grad
    second_new = decay_two * second + (1.0 - decay_two) * grad * grad
    first_hat = first_new / (1.0 - decay_one**STEP)
    second_hat = second_new / (1.0 - decay_two**STEP)
    weight_new = weight - rate * (first_hat / (jnp.sqrt(second_hat) + epsilon) + weight_decay * weight)
    return (weight_new, first_new, second_new)


def by_blocks(grid, feats, cols, share, second_cols, head_rows, channels, rows):
    return (
        (grid.z, grid.x, grid.y) == (4, 2, 2)
        and feats % 16 == 0
        and feats > max(LATE_OUT, LATE_BACK)
        and cols == channels == 256
        and second_cols == 128
        and (share, head_rows) == (256, 32)
        and rows % (CHUNKS * GROUP) == 0
        and block_span(feats, grid.wide, channels) > 0
    )


def place_table(grid):
    found = []
    for sign in (-1, 1):
        for dz in range(grid.z):
            for dx in range(grid.x):
                z, x = (grid.at["z"] + sign * dz) % grid.z, (grid.at["x"] + sign * dx) % grid.x
                found.append(z * grid.x + x)
    y, core = grid.at["y"], grid.at["c"]
    found += [y, core]
    found += [CORES * ((y + k) % grid.y) + c for c in (core, 1 - core) for k in range(grid.y)]
    return jnp.stack(found).astype(jnp.int32)


def low_sum(first, *others):
    total = first.astype(f32)
    for value in others:
        total = total + value.astype(f32)
    return total.astype(bf16)


def terms(value):
    found = []
    for _ in range(TERMS):
        found.append(lax.optimization_barrier(value.astype(bf16)))
        value = value - found[-1].astype(f32)
    return jnp.concatenate(found, axis=0)


def from_terms(rows):
    count = rows.shape[0] // TERMS
    total = rows[:count].astype(f32)
    for k in range(1, TERMS):
        total = total + rows[k * count : (k + 1) * count].astype(f32)
    return total


def blocks_step(grid, make_crops, w_first, w_second, w_heads, biases, labels, crowd, targets):
    feats, cols = w_first.shape
    share, _ = w_second.shape
    head_rows = w_heads.shape[0]
    table = place_table(grid)
    count = grid.z * grid.x

    links = Links(grid, True)
    most = feats - LATE_OUT
    mine, first_low = prepare(w_first, w_second, w_heads, crowd, most)
    half = mine.shape[0] - feats
    m = {(0, 0, 0): mine}
    stacks = {}

    m[0, 1, 0] = grid.move(mine, "x", 1)
    m[0, 0, 1] = grid.move(mine, "y", 1)
    m[1, 0, 0] = grid.move(first_low, "z", 1)
    own_crops = [make_crops(i) for i in range(CHUNKS)]
    made = own_crops[:EARLY] + [m[key] for key in ((0, 1, 0), (0, 0, 1), (1, 0, 0))]
    m[3, 0, 0] = links.send(after(first_low, m[1, 0, 0]), "z", 3)
    m[1, 1, 0] = links.send(after(m[1, 0, 0], *made), "x")
    m[0, 1, 1] = links.send(after(m[0, 1, 0], m[0, 0, 1]), "y")
    stacks[0] = jnp.stack([jnp.stack([m[0, x, y][most:] for x in range(grid.x)]) for y in range(grid.y)])
    links.next()
    m[2, 0, 0] = links.send(m[1, 0, 0], "z", 1)
    m[3, 1, 0] = links.send(m[3, 0, 0], "x")
    m[1, 0, 1] = links.send(m[1, 0, 0], "y")
    links.next()
    stacks[1] = links.send(stacks[0], "z", 1)
    m[2, 1, 0] = links.send(m[2, 0, 0], "x")
    m[3, 0, 1] = links.send(m[3, 0, 0], "y")
    links.next()
    stacks[3] = links.send(stacks[0], "z", 3)
    m[1, 1, 1] = links.send(m[1, 0, 1], "x")
    m[2, 0, 1] = links.send(m[2, 0, 0], "y")
    links.next()
    stacks[2] = links.send(stacks[1], "z", 1)
    m[3, 1, 1] = links.send(m[3, 0, 1], "x")
    m[2, 1, 1] = links.send(m[2, 1, 0], "y")
    sib_crops = []
    for chunk in own_crops:
        sib_crops.append(grid.swap(after(chunk, *made)))
    crops = own_crops + sib_crops

    span = block_span(feats, grid.wide, cols)
    both = (0, 1)

    def products(work, before):
        inputs = []
        for dz, dx, ys, kind in work:
            inputs += [m[dz, dx, y] for y in ys if kind != "last"] + [stacks[dz]] * (kind != "most")
        items = tuple((dz * grid.x + dx, dx, ys, kind) for dz, dx, ys, kind in work)
        return first_blocks(table, crops, inputs, items, feats, most, grid.wide, grid.y, before)

    work = [(dz, dx, both, "all") for dz, dx in ((0, 0), (0, 1), (1, 0), (3, 0), (1, 1))]
    first_pre = products(work + [(3, 1, (0,), "all"), (2, 0, both, "most"), (2, 1, (0,), "most")], None)
    work = [(2, 0, both, "last"), (2, 1, both, "last"), (2, 1, (1,), "most"), (3, 1, (1,), "all")]
    pre = products(work, first_pre)
    sib_stacks = {2: grid.swap(after(stacks[2], first_pre[0]))}
    sib_stacks[0] = grid.swap(stacks[0])
    sib_stacks[1] = grid.swap(after(stacks[1], sib_stacks[0]))
    sib_stacks[3] = grid.swap(after(stacks[3], sib_stacks[1], first_pre[0]))
    g_own, g_send, gw2, gw2_send, gwh, gwh_send, sums, roi_count = heads_blocks(
        share,
        half,
        table,
        [stacks[z] for z in range(4)],
        [sib_stacks[z] for z in range(4)],
        pre[0],
        grid.swap(pre[1]),
        biases[None, :],
        labels[None, :],
        crowd[None, :],
        targets.T,
    )

    g_got = grid.swap(g_send)
    m = {}
    parts = {}

    def gradients(keys, wait=()):
        numbers = tuple(count + dz * grid.x + dx for dz, dx in keys)
        outs = first_grad_blocks(after(table, *wait), numbers, crops, g_own, g_got, feats, LATE_BACK, grid.y, span)
        for i, (dz, dx) in enumerate(keys):
            for y in range(grid.y):
                m[dz, dx, y], parts[dz, dx, y] = outs[(i * grid.y + y) * 2 : (i * grid.y + y) * 2 + 2]

    gradients([(2, 1), (2, 0), (3, 1), (3, 0)])
    lates = [parts[dz, dx, y] for dz in (2, 3) for y in range(grid.y) for dx in range(grid.x)]
    packed = pack(
        table,
        lates,
        (gw2, grid.swap(after(gw2_send, g_got))),
        (gwh, grid.swap(after(gwh_send, g_got))),
        sums,
        half,
        (grid.y, grid.x),
    )

    def stack_of(dz):
        if dz >= 2:
            return packed[dz - 2]
        first = jnp.stack([jnp.stack([parts[dz, dx, y] for dx in range(grid.x)]) for y in range(grid.y)])
        return jnp.concatenate([first, packed[2][dz]], axis=2)

    links = Links(grid, False)
    far = stack_of(2)
    gradients([(1, 1), (1, 0), (0, 1), (0, 0)], [far])
    begun = (far, m[3, 1, 1])
    z0 = links.send(after(far, *begun[1:]), "z", 1)
    y0 = links.send(after(m[2, 1, 1], *begun), "y")
    x0 = links.send(after(m[3, 1, 1], *begun[:1]), "x")
    z1 = links.send(stack_of(3), "z", 3)
    y1 = links.send(m[2, 0, 1], "y")
    x1 = links.send(m[3, 1, 0], "x")
    z2 = links.send(low_sum(stack_of(1), z0), "z", 1)
    x2 = links.send(low_sum(m[2, 1, 0], y0), "x")
    y2 = links.send(low_sum(m[3, 0, 1], x0), "y")
    z3 = links.send(low_sum(m[2, 0, 0], x2, y1), "z", 1)
    x3 = links.send(m[1, 1, 1], "x")
    y3 = links.send(m[0, 1, 1], "y")
    z4 = links.send(low_sum(m[3, 0, 0], x1, y2), "z", 3)
    x4 = links.send(m[1, 1, 0], "x")
    y4 = links.send(low_sum(m[1, 0, 1], x3), "y")

    def extra_rows(stack):
        rows = stack[:, :, -EXTRA : 8 - EXTRA].reshape(-1, cols)
        return from_terms(rows[: TERMS * (sums.shape[1] // cols)])

    odd = grid.at["z"] % 2 == 1
    below, above, opposite = extra_rows(z0), extra_rows(z1), extra_rows(z2)
    total = sums.reshape(-1, cols)
    total = (total + jnp.where(odd, below, above)) + (opposite + jnp.where(odd, above, below))
    extra = TERMS * total.shape[0]
    late = low_sum(stack_of(0), z1, z2)
    x5 = links.send(jnp.concatenate([late[:, 1].reshape(-1, cols), terms(total)], axis=0), "x")
    x6 = links.send(low_sum(m[0, 1, 0], y3), "x")
    z5 = links.send(low_sum(m[1, 0, 0], x4, y4, z3), "z", 1)
    y5 = links.send(m[0, 0, 1], "y")
    total = total + from_terms(x5[-extra:])
    late = low_sum(late[:, 0], x5[:-extra].reshape(late[:, 0].shape))
    y6 = links.send(jnp.concatenate([late[1], terms(total)], axis=0), "y")
    total = total + from_terms(y6[-extra:])
    total = total + grid.swap(total)
    sums = total.reshape(1, -1)
    main = m[0, 0, 0].astype(f32)
    for value in (x6, y5, z4, z5):
        main = main + value.astype(f32)
    late = late[0].astype(f32) + y6[:-extra].astype(f32)

    first_total = jnp.concatenate([main, late[:LATE_BACK]], axis=0)
    late = late[LATE_BACK : LATE_BACK + half]
    total = jnp.concatenate([late[:, :128], late[:, 128:]], axis=0)
    heads_total = jnp.concatenate(
        [total[share + k * head_rows : share + (k + 1) * head_rows] for k in range(HEADP // 128)], axis=1
    )[:, :HEAD]
    return roi_count.reshape(()), sums, first_total, total[:share], heads_total


def stacked_step(grid, make_crops, w_first, w_second, w_heads, biases, labels, crowd, targets):
    tags = jnp.concatenate([labels[:, None].astype(f32), crowd[:, None].astype(f32), targets.astype(f32)], axis=1)
    tags = jnp.pad(tags, ((0, 0), (0, 122)))
    feats, cols = w_first.shape
    share, second_cols = w_second.shape
    head_rows = w_heads.shape[0]
    units = HID // CORES
    core = grid.at["c"]
    kept = jnp.sum(1 - crowd)
    head_block = jnp.pad(w_heads, ((0, 0), (0, HEADP - HEAD)))
    spot = (lax.broadcasted_iota(jnp.int32, head_block.shape, 0) == 0) * 1
    lane = lax.broadcasted_iota(jnp.int32, head_block.shape, 1)
    head_block = head_block + (
        spot * (jnp.where(lane == HEADP - 1, kept % 128, 0) + jnp.where(lane == HEADP - 2, kept // 128, 0))
    ).astype(f32)
    small = jnp.concatenate(
        [w_second.astype(bf16).reshape(-1, cols), head_block.astype(bf16).reshape(-1, cols)], axis=0
    )
    second_rows = share * second_cols // cols
    small_all = spread_stacked(grid, small, "zxy").reshape(grid.wide, grid.y, *small.shape)
    weight = spread_stacked(grid, w_first.astype(bf16), "zxy")
    weight = weight.transpose(2, 0, 1, 3, 4).reshape(grid.y, grid.wide * feats, cols)
    crops = [make_crops(i) for i in range(CHUNKS)]
    crops = crops + [grid.swap(c) for c in crops]
    second_own = (
        small_all[:, :, :second_rows]
        .reshape(grid.wide, grid.y, share, second_cols)
        .transpose(1, 2, 0, 3)
        .reshape(units, HID)
    )
    heads_own = small_all[:, :, second_rows:].reshape(grid.wide, grid.y, head_rows, HEADP)
    heads_sib = grid.swap(heads_own)
    head_matrix = jnp.where(
        core == 0, jnp.stack([heads_own, heads_sib], axis=2), jnp.stack([heads_sib, heads_own], axis=2)
    ).reshape(HID, HEADP)
    bias = biases[:HID].reshape(grid.y, CORES, share)
    bias = jnp.where(core == 0, bias, bias[:, ::-1]).transpose(1, 0, 2).reshape(1, -1)
    pre_own, pre_send = first_layer(crops, weight)
    unit_at = [2 * y + c for c in (core, 1 - core) for y in range(grid.y)]
    g_own, g_send, gw2_own, gw2_send, gwh, gwh_send, sums, roi_count = heads_step(
        share,
        grid.wide,
        jnp.stack([jnp.asarray(v) for v in unit_at + [core]]).astype(jnp.int32),
        pre_own,
        grid.swap(pre_send),
        second_own,
        grid.swap(second_own),
        head_matrix,
        bias,
        biases[HID : 2 * HID].reshape(1, -1),
        jnp.pad(biases[2 * HID :], (0, HEADP - HEAD)).reshape(1, -1),
        tags,
    )
    grad = first_grad(crops, g_own, grid.swap(g_send), grid.y)
    grad = grad.reshape(grid.y, grid.wide, feats, cols).transpose(1, 0, 2, 3)
    first_total = collect_stacked(grid, grad.reshape(grid.z, grid.x, grid.y, feats, cols), "yxz")
    gw2 = gw2_own.astype(f32) + grid.swap(gw2_send).astype(f32)
    gwh = gwh.astype(f32) + grid.swap(gwh_send).astype(f32)
    gw2 = gw2.astype(bf16).reshape(grid.y, share, grid.wide, second_cols).transpose(2, 0, 1, 3)
    small_grad = jnp.concatenate(
        [
            gw2.reshape(grid.wide, grid.y, second_rows, cols),
            gwh.astype(bf16).reshape(grid.wide, grid.y, -1, cols),
        ],
        axis=2,
    ).reshape(grid.z, grid.x, grid.y, -1, cols)
    small_total = collect_stacked(grid, small_grad, "yxz")
    second_total = small_total[:second_rows].reshape(share, second_cols)
    heads_total = small_total[second_rows:].reshape(head_rows, HEADP)[:, :HEAD]
    sums = all_sum(sums)
    return roi_count.reshape(()), sums, first_total, second_total, heads_total


def shards(
    maps,
    roi_image,
    roi_level,
    roi_corner,
    roi_weights,
    crowd,
    labels,
    box_targets,
    w_first,
    m_first,
    v_first,
    w_second,
    m_second,
    v_second,
    w_heads,
    m_heads,
    v_heads,
    biases,
    bias_m,
    bias_v,
):
    grid = Grid()
    rows = crowd.shape[0]

    images, levels, height, width, channels = maps.shape
    base = ((roi_image * levels + roi_level) * height + roi_corner[:, 0]).astype(jnp.int32)
    col = roi_corner[:, 1].astype(jnp.int32)
    flat_maps = maps.reshape(images * levels * height, width, channels)
    padded = jnp.pad(roi_weights, ((0, 0), (0, 0), (0, 1), (0, 0)))
    row_w = padded[:, 0].reshape(rows * 8, WIN)
    col_w = padded[:, 1].reshape(rows * 8, WIN)
    step = rows // CHUNKS
    def make_crops(i, *wait):
        return window_crops(flat_maps, after(base, *wait) if wait else base, col, row_w, col_w, i * step, step)

    shapes = (*w_first.shape, *w_second.shape, w_heads.shape[0], channels, rows)
    run = blocks_step if by_blocks(grid, *shapes) else stacked_step
    roi_count, sums, first_total, second_total, heads_total = run(
        grid, make_crops, w_first, w_second, w_heads, biases, labels, crowd, box_targets
    )
    loss_total = sums[0, 2 * HID + HEAD]
    bias_grad = sums[0, : 2 * HID + HEAD]

    first_out = adam_update(w_first, first_total, m_first, v_first, rate_first)
    second_out = adam_update(w_second, second_total, m_second, v_second, rate_second)
    heads_out = adam_update(w_heads, heads_total, m_heads, v_heads, rate_heads)
    bias_out = adam_update(biases, bias_grad, bias_m, bias_v, rate_biases)
    return (loss_total, roi_count, *first_out, *second_out, *heads_out, *bias_out)


def solution(mesh):
    rows = P(("wide", "tp"))
    both = P("wide", "tp")
    turned = P("tp", "wide")
    return jax.shard_map(
        shards,
        mesh=mesh,
        in_specs=(rows,) * 8 + (both,) * 3 + (turned,) * 3 + (rows,) * 3 + (P(),) * 3,
        out_specs=(P(), P()) + (both,) * 3 + (turned,) * 3 + (rows,) * 3 + (P(),) * 3,
        check_vma=False,
    )
```
